32 devices in a mesh: sub: 4 (over z), crow: 4 (over x, core), ccol: 2 (over y).
Axes of the slice: x: 2, y: 2, z: 4, core: 2. Of those that a mesh axis runs over, the one named last changes fastest.
Arguments:
- rhs: float32 [24, 48, 3, 10, 256], P('sub', ('crow', 'ccol')), may hold values from -6 to 6
- start: float32 [24, 48, 3, 10, 256], P('sub', ('crow', 'ccol')), may hold values from -1.75 to 1.75
- stiffness: float32 [24, 48, 3, 10], P('sub', ('crow', 'ccol')), may hold values from 0.1 to 1
- sub_inverse: bfloat16 [32, 1920, 1920], P(('sub', 'crow', 'ccol')), may hold values from -0.0625 to 0.0625
- basis: bfloat16 [32, 1920, 128], P(('sub', 'crow', 'ccol')), may hold values from -0.0625 to 0.0625
- coarse_inverse: bfloat16 [4, 512, 2048], P(None, ('crow', 'ccol'), 'sub'), may hold values from -0.1875 to 0.1875
- offsets: int32 [4, 8], P('sub'), may hold values from 0 to 464, as said below
Outputs:
- solution: float32 [24, 48, 3, 10, 256], P('sub', ('crow', 'ccol'))
The draws below stay inside these ranges and needn't reach their ends.
Inputs may be any that keep to these rules, and one draw needn't show every extreme that they name: In every row g, offsets[g, 0] = 0 and the offsets rise; each count (next offset minus this one, 512 after the last) lies between 48 and 128, and every group has a subdomain with exactly 128.
All inputs are finite; a program needn't handle non-finite values.
Results may differ from the reference program's by a relative error of at most 0.0037.
Values may be sent and summed in bfloat16 or wider, within the bound.
No kernel may reach another device: no remote copies, remote signals or barrier semaphores. Data moves between devices by JAX's collectives and lax.ppermute only.
A program may use at most 64 MiB of HBM per device.

```python
import math
import jax
import jax.numpy as jnp
from jax import lax

CS = 6
CQ = 6
CZ = 10
NRHS = 256
ITERS = 2
KMIN = 48
KMEAN = 64
KMAX = 128
GROUP = 8
NLOC = 1920
KGROUP = 512
NCOARSE = 2048
NSUBD = 32
NX = 24
NQ = 48
N_SUB = 4


def draw_offsets(key, part):
    key_big = jax.random.fold_in(key, 11)
    key_cuts = jax.random.fold_in(key, 12)
    spare = GROUP * (KMEAN - KMIN) - (KMAX - KMIN)
    big_member = jax.random.randint(key_big, (N_SUB, 1), 0, GROUP)
    cut_points = jnp.sort(jax.random.randint(key_cuts, (N_SUB, GROUP - 2), 0, spare + 1), axis=1)
    bounds = jnp.concatenate([jnp.zeros((N_SUB, 1), jnp.int32), cut_points.astype(jnp.int32), jnp.full((N_SUB, 1), spare, jnp.int32)], axis=1)
    shares = bounds[:, 1:] - bounds[:, :-1]
    shares_low = jnp.concatenate([shares, jnp.zeros((N_SUB, 1), jnp.int32)], axis=1)
    shares_high = jnp.concatenate([jnp.zeros((N_SUB, 1), jnp.int32), shares], axis=1)
    position = jnp.arange(GROUP, dtype=jnp.int32)[None, :]
    extra = jnp.where(position < big_member, shares_low, jnp.where(position == big_member, KMAX - KMIN, shares_high))
    counts = KMIN + extra
    return (jnp.cumsum(counts, axis=1) - counts).astype(jnp.int32)


def spiked(entries, stream_key, source, target, shards_of, factor):
    owner, partner = [(jnp.arange(entries.shape[dim]) // (entries.shape[dim] // shards_of)).reshape([-1 if axis == dim else 1 for axis in range(entries.ndim)]) for dim in (source, target)]
    chosen = jax.random.permutation(stream_key, shards_of)[partner]
    strong = (owner == chosen) | (owner == (partner + shards_of // 2) % shards_of)
    return jnp.where(strong, factor * entries, entries)


def level_of(rng, shape, split, least, top_value):
    loudness = 1.0
    for dim, blocks in split:
        draws = jax.random.uniform(jax.random.fold_in(jax.random.fold_in(rng, 6), dim), (blocks,), jnp.float32, least / len(split), top_value / len(split))
        loudness = loudness * jnp.repeat(jnp.exp(draws), shape[dim] // blocks).reshape((-1,) + (1,) * (len(shape) - 1 - dim))
    return loudness


def centred(stream_key, extent, deviation, bound, cuts=(), held_as=jnp.bfloat16):
    level = level_of(stream_key, extent, cuts, -0.22, 0.18) if cuts else 1.0
    result = jax.random.normal(stream_key, extent, jnp.float32) * deviation * level
    return jnp.minimum(jnp.maximum(result, -bound), bound).astype(held_as)


def heavy_noise(rng, shape, scale, bound, cuts, heavy, kind=jnp.bfloat16):
    values = scale * jax.random.normal(rng, shape, jnp.float32)
    if cuts:
        values = values * level_of(rng, shape, cuts, -0.22, 0.18)
    return jnp.clip(spiked(values, jax.random.fold_in(rng, 3), *heavy), -bound, bound).astype(kind)


def setup_inputs(seed: int = 0) -> dict:
    seeds = jax.random.split(jax.random.key(seed), 8)
    return {
        "rhs": centred(seeds[0], (NX, NQ, 3, CZ, NRHS), 1.0, 6.0, ((0, 4), (1, 8)), jnp.float32),
        "start": centred(seeds[1], (NX, NQ, 3, CZ, NRHS), 0.3, 1.75, ((0, 4), (1, 8)), jnp.float32),
        "stiffness": jnp.clip(jnp.exp(math.log(1.0) - 2.3025851 * jax.random.uniform(seeds[2], (NX, NQ, 3, CZ), jnp.float32) ** level_of(seeds[2], (NX, NQ, 3, CZ), ((0, 4), (1, 8)), -0.2, 0.2)), 0.1, 1.0),
        "sub_inverse": centred(seeds[3], (NSUBD, NLOC, NLOC), (4 * NLOC) ** -0.5, 0.0625, ((0, 32),)),
        "basis": centred(seeds[4], (NSUBD, NLOC, KMAX), (4 * NLOC) ** -0.5, 0.0625, ((0, 32),)),
        "coarse_inverse": heavy_noise(seeds[5], (N_SUB, KGROUP, NCOARSE), NCOARSE ** -0.5, 0.1875, ((1, 8), (2, 4)), (2, 0, 4, 2.0)),
        "offsets": draw_offsets(jax.random.fold_in(seeds[7], 71), 0),
    }


def apply_stiffness(field, stiffness):
    padded = jnp.pad(field, ((1, 1), (1, 1), (0, 0), (1, 1), (0, 0)))
    beside = padded[2:, 1:-1, :, 1:-1] + padded[:-2, 1:-1, :, 1:-1]
    beside = beside + padded[1:-1, 2:, :, 1:-1] + padded[1:-1, :-2, :, 1:-1]
    beside = beside + padded[1:-1, 1:-1, :, 2:] + padded[1:-1, 1:-1, :, :-2]
    return (6.0 + stiffness)[..., None] * field - beside


def window(padded_res, domain):
    group_id = (domain // GROUP).astype(jnp.int32)
    member_id = (domain % GROUP).astype(jnp.int32)
    zero = jnp.zeros((), jnp.int32)
    corner_s = (group_id * CS).astype(jnp.int32)
    corner_q = (member_id * CQ).astype(jnp.int32)
    piece = lax.dynamic_slice(padded_res, (corner_s, corner_q, zero, zero, zero), (CS + 2, CQ + 2, 3, CZ, NRHS))
    return piece.reshape(NLOC, NRHS)


def selector_for(offsets, counts, domain):
    group_id = domain // GROUP
    member_id = domain % GROUP
    first_slot = offsets[group_id, member_id]
    col_count = counts[group_id, member_id]
    slot_ids = jnp.arange(KGROUP, dtype=jnp.int32)[:, None]
    col_ids = jnp.arange(KMAX, dtype=jnp.int32)[None, :]
    selector = ((slot_ids == first_slot + col_ids) & (col_ids < col_count)).astype(jnp.bfloat16)
    return selector, col_count


def reference(rhs, start, stiffness, sub_inverse, basis, coarse_inverse, offsets):
    counts = jnp.concatenate([offsets[:, 1:], jnp.full((N_SUB, 1), KGROUP, jnp.int32)], axis=1) - offsets
    domains = jnp.arange(N_SUB * GROUP, dtype=jnp.int32)
    solution = start
    for sweep in range(ITERS):
        residual = rhs - apply_stiffness(solution, stiffness)
        padded_res = jnp.pad(residual, ((1, 1), (1, 1), (0, 0), (0, 0), (0, 0))).astype(jnp.bfloat16)

        def restrict(domain):
            local_res = window(padded_res, domain)
            selector, col_count = selector_for(offsets, counts, domain)
            own_basis = lax.dynamic_index_in_dim(basis, domain, 0, keepdims=False)
            projected = jnp.dot(own_basis.T, local_res, preferred_element_type=jnp.float32)
            keep = jnp.arange(KMAX, dtype=jnp.int32)[:, None] < col_count
            restricted = jnp.where(keep, projected, jnp.zeros_like(projected)).astype(jnp.bfloat16)
            return jnp.dot(selector, restricted, preferred_element_type=jnp.float32)

        placed = lax.map(restrict, domains)
        coefficients = placed.reshape(N_SUB, GROUP, KGROUP, NRHS).sum(axis=1).astype(jnp.bfloat16)
        flat_coeffs = coefficients.reshape(N_SUB * KGROUP, NRHS)

        def coarse_rows(group_rows):
            return jnp.dot(group_rows, flat_coeffs, preferred_element_type=jnp.float32)

        row_values = lax.map(coarse_rows, coarse_inverse).astype(jnp.bfloat16)
        coarse_values = row_values.reshape(N_SUB, GROUP, KMEAN, NRHS).transpose(0, 2, 1, 3).reshape(N_SUB, KGROUP, NRHS)

        def correct(domain):
            local_res = window(padded_res, domain)
            selector, col_count = selector_for(offsets, counts, domain)
            own_basis = lax.dynamic_index_in_dim(basis, domain, 0, keepdims=False)
            own_inverse = lax.dynamic_index_in_dim(sub_inverse, domain, 0, keepdims=False)
            own_values = lax.dynamic_index_in_dim(coarse_values, domain // GROUP, 0, keepdims=False)
            selected = jnp.dot(selector.T, own_values, preferred_element_type=jnp.float32).astype(jnp.bfloat16)
            fine_part = jnp.dot(own_inverse, local_res, preferred_element_type=jnp.float32)
            coarse_part = jnp.dot(own_basis, selected, preferred_element_type=jnp.float32)
            total = (fine_part + coarse_part).reshape(CS + 2, CQ + 2, 3, CZ, NRHS)
            return total[1:-1, 1:-1]

        pieces = lax.map(correct, domains)
        correction = pieces.reshape(N_SUB, GROUP, CS, CQ, 3, CZ, NRHS).transpose(0, 2, 1, 3, 4, 5, 6)
        correction = correction.reshape(N_SUB * CS, GROUP * CQ, 3, CZ, NRHS)
        solution = solution + correction
    return solution
```

```python
import jax
import jax.numpy as jnp
from jax import lax
from jax.sharding import PartitionSpec as P

ITERS = 2
GROUP_AXES = ("crow", "ccol")
ALL_AXES = ("sub", "crow", "ccol")


def swap(to_low, to_high, axis):
    count = lax.axis_size(axis)
    even = [(i, i + 1) for i in range(0, count - 1, 2)]
    odd = [(i, i + 1) for i in range(1, count - 1, 2)]
    is_even = lax.axis_index(axis) % 2 == 0
    first = lax.ppermute(
        jnp.where(is_even, to_high, to_low), axis, even + [(b, a) for a, b in even]
    )
    second = lax.ppermute(
        jnp.where(is_even, to_low, to_high), axis, odd + [(b, a) for a, b in odd]
    )
    return jnp.where(is_even, second, first), jnp.where(is_even, first, second)


def inside(solution, rhs, diagonal):
    padded = jnp.pad(solution, ((1, 1), (1, 1), (0, 0), (1, 1), (0, 0)))
    beside = padded[2:, 1:-1, :, 1:-1] + padded[:-2, 1:-1, :, 1:-1]
    beside = beside + padded[1:-1, 2:, :, 1:-1] + padded[1:-1, :-2, :, 1:-1]
    beside = beside + padded[1:-1, 1:-1, :, 2:] + padded[1:-1, 1:-1, :, :-2]
    return rhs - diagonal * solution + beside


def residual_window(solution, rhs, diagonal):
    bf16, f32 = jnp.bfloat16, jnp.float32
    row, rows = lax.axis_index("sub"), lax.axis_size("sub")
    col, cols = lax.axis_index(GROUP_AXES), lax.axis_size(GROUP_AXES)
    base = inside(solution, rhs, diagonal)
    own = solution.astype(bf16)
    low, high = swap(
        jnp.stack([base[:, 0].astype(bf16), own[:, 0]]),
        jnp.stack([base[:, -1].astype(bf16), own[:, -1]]),
        GROUP_AXES,
    )
    low, high = low.astype(f32), high.astype(f32)
    edge_low = jnp.where(col > 0, low[0] + solution[:, 0], 0.0)
    edge_high = jnp.where(col < cols - 1, high[0] + solution[:, -1], 0.0)
    wide = jnp.concatenate(
        [
            edge_low[:, None],
            base[:, :1] + low[1][:, None],
            base[:, 1:-1],
            base[:, -1:] + high[1][:, None],
            edge_high[:, None],
        ],
        axis=1,
    )
    wide_solution = jnp.concatenate([low[1][:, None], solution, high[1][:, None]], axis=1)
    above, below = swap(
        jnp.stack([wide[0], wide_solution[0]]).astype(bf16),
        jnp.stack([wide[-1], wide_solution[-1]]).astype(bf16),
        "sub",
    )
    above, below = above.astype(f32), below.astype(f32)
    first = jnp.where(row > 0, above[0] + wide_solution[0], 0.0)
    last = jnp.where(row < rows - 1, below[0] + wide_solution[-1], 0.0)
    window = jnp.concatenate(
        [
            first[None],
            wide[:1] + above[1][None],
            wide[1:-1],
            wide[-1:] + below[1][None],
            last[None],
        ],
        axis=0,
    )
    return window.astype(bf16).reshape(-1, solution.shape[-1])


def slots_of(offsets, kgroup, groups, depth):
    ends = jnp.concatenate(
        [offsets[..., 1:], jnp.full(offsets.shape[:-1] + (1,), kgroup, jnp.int32)], axis=-1
    )
    member = jnp.arange(groups, dtype=jnp.int32)[:, None]
    turn = jnp.arange(depth, dtype=jnp.int32)[None, :]
    first = offsets[..., None, None]
    slots = first + (member - first) % groups + turn * groups
    return slots, slots < ends[..., None, None]


def shards(rhs, start, stiffness, sub_inverse, basis, coarse_inverse, offsets):
    bf16, f32 = jnp.bfloat16, jnp.float32
    cells_s, cells_q, comps, layers, columns = rhs.shape
    n_sub, share_rows, kgroup = coarse_inverse.shape
    max_cols = basis.shape[2]
    groups = offsets.shape[1]
    depth = -(-max_cols // groups)
    padded_cols = groups * depth
    member = lax.axis_index(GROUP_AXES)
    sub_index = lax.axis_index("sub")

    every = lax.all_to_all(
        jnp.broadcast_to(offsets, (n_sub, groups)), "sub", 0, 0, tiled=True
    )
    slots, valid = slots_of(every, kgroup, groups, depth)
    own_slots = lax.dynamic_index_in_dim(slots, sub_index, 0, keepdims=False)
    own_valid = lax.dynamic_index_in_dim(valid, sub_index, 0, keepdims=False)
    member_slots = lax.dynamic_index_in_dim(own_slots, member, 0, keepdims=False).reshape(-1)
    member_valid = lax.dynamic_index_in_dim(own_valid, member, 0, keepdims=False).reshape(-1)
    member_start = lax.dynamic_index_in_dim(offsets[0], member, 0, keepdims=False)
    picked = jnp.where(member_valid, member_slots - member_start, -1)
    order = (jnp.arange(max_cols, dtype=jnp.int32)[:, None] == picked[None, :]).astype(bf16)
    local_basis = jnp.dot(basis[0], order, preferred_element_type=f32).astype(bf16)
    mine = lax.dynamic_index_in_dim(slots, member, 2, keepdims=False).reshape(n_sub, -1)
    mine_valid = lax.dynamic_index_in_dim(valid, member, 2, keepdims=False).reshape(n_sub, -1)
    rows = jnp.where(mine_valid, mine // groups, -1)
    row_pick = (rows[:, :, None] == jnp.arange(share_rows, dtype=jnp.int32)).astype(bf16)
    col_pick = (
        jnp.arange(kgroup, dtype=jnp.int32)[:, None]
        == jnp.where(own_valid, own_slots, -1).reshape(1, -1)
    ).astype(bf16)
    spread = jnp.einsum("gri,gik->grk", row_pick, coarse_inverse, preferred_element_type=f32)
    spread = jnp.dot(
        spread.astype(bf16).reshape(-1, kgroup), col_pick, preferred_element_type=f32
    ).astype(bf16)

    diagonal = (6.0 + stiffness)[..., None]
    local_inverse = sub_inverse[0]
    solution = start
    for sweep in range(ITERS):
        local_res = residual_window(solution, rhs, diagonal)
        restricted = lax.dot_general(
            local_basis, local_res, (((0,), (0,)), ((), ())), preferred_element_type=f32
        ).astype(bf16)
        gathered = lax.all_to_all(
            jnp.broadcast_to(restricted[None], (groups,) + restricted.shape),
            GROUP_AXES, 0, 0, tiled=True,
        )
        terms = jnp.dot(
            spread, gathered.reshape(-1, columns), preferred_element_type=f32
        ).astype(bf16)
        arrived = lax.all_to_all(
            terms.reshape(n_sub * groups, depth, columns), ALL_AXES, 0, 0, tiled=True
        )
        chosen = jnp.sum(
            arrived.reshape(n_sub, padded_cols, columns).astype(f32), axis=0
        ).astype(bf16)
        fine_part = jnp.dot(local_inverse, local_res, preferred_element_type=f32)
        coarse_part = jnp.dot(local_basis, chosen, preferred_element_type=f32)
        correction = (fine_part + coarse_part).reshape(
            cells_s + 2, cells_q + 2, comps, layers, columns
        )
        solution = solution + correction[1:-1, 1:-1]
    return solution


def solution(mesh):
    return jax.shard_map(
        shards,
        mesh=mesh,
        in_specs=(
            P("sub", ("crow", "ccol"), None, None, None),
            P("sub", ("crow", "ccol"), None, None, None),
            P("sub", ("crow", "ccol"), None, None),
            P(("sub", "crow", "ccol"), None, None),
            P(("sub", "crow", "ccol"), None, None),
            P(None, ("crow", "ccol"), "sub"),
            P("sub", None),
        ),
        out_specs=P("sub", ("crow", "ccol"), None, None, None),
        check_vma=False,
    )
```

```python
import functools

import jax
import jax.numpy as jnp
import numpy as np
from jax import lax
from jax.experimental import pallas as pl
from jax.experimental.pallas import tpu as pltpu
from jax.sharding import PartitionSpec as P

ITERS = 2
GROUP_AXES = ("crow", "ccol")
ALL_AXES = ("sub", "crow", "ccol")
bf16, f32 = jnp.bfloat16, jnp.float32
VMEM = pl.BlockSpec(memory_space=pltpu.VMEM)


def call(body, ins, outs, scratch=(), limit=24, flops=0):
    size = sum(x.size * x.dtype.itemsize for x in (*ins, *outs))
    return pl.pallas_call(
        body,
        out_shape=tuple(outs),
        in_specs=[VMEM] * len(ins),
        out_specs=tuple([VMEM] * len(outs)),
        scratch_shapes=list(scratch),
        compiler_params=pltpu.CompilerParams(vmem_limit_bytes=limit << 20),
        cost_estimate=pl.CostEstimate(flops=flops, bytes_accessed=size, transcendentals=0),
    )(*ins)


def swap(first, second, axis):
    count = lax.axis_size(axis)
    even = [(i, i + 1) for i in range(0, count - 1, 2)]
    odd = [(i, i + 1) for i in range(1, count - 1, 2)]
    return (
        lax.ppermute(first, axis, even + [(b, a) for a, b in even]),
        lax.ppermute(second, axis, odd + [(b, a) for a, b in odd]),
    )


def write_base(layers, rhs, diag, sol, base, shape):
    cells_s, cells_q, _, pad, columns = shape
    at = lax.broadcasted_iota(jnp.int32, (pad, columns), 0)
    comps = shape[2]
    used = comps * layers
    has_up, has_down = at < used, at < used
    for c in range(comps):
        has_up = has_up & (at != c * layers)
        has_down = has_down & (at != c * layers + layers - 1)
    for s in range(cells_s):
        for q in range(cells_q):
            i = s * cells_q + q
            x = sol[i]
            d = diag[i]
            d = jnp.concatenate([d] * (columns // d.shape[1]), axis=1)
            total = rhs[i] - d * x
            total = total + jnp.where(has_up, pltpu.roll(x, 1, 0), 0.0)
            total = total + jnp.where(has_down, pltpu.roll(x, pad - 1, 0), 0.0)
            if q > 0:
                total = total + sol[i - 1]
            if q < cells_q - 1:
                total = total + sol[i + 1]
            if s > 0:
                total = total + sol[i - cells_q]
            if s < cells_s - 1:
                total = total + sol[i + cells_q]
            base[i] = total


def write_column_messages(sol, base, first, second, shape):
    cells_s, cells_q = shape[:2]
    even = lax.axis_index(GROUP_AXES) % 2 == 0
    for out, q in (
        (first, jnp.where(even, cells_q - 1, 0)),
        (second, jnp.where(even, 0, cells_q - 1)),
    ):
        for s in range(cells_s):
            out[0, s] = base[s * cells_q + q].astype(bf16)
            out[1, s] = sol[s * cells_q + q].astype(bf16)


def open_kernel(shape, layers, start, rhs_in, diag, sol, rhs, base, first, second):
    cells_s, cells_q, comps, pad, columns = shape
    for source, target in ((start, sol), (rhs_in, rhs)):
        for s in range(cells_s):
            for q in range(cells_q):
                i = s * cells_q + q
                for c in range(comps):
                    target[i, c * layers : (c + 1) * layers, :] = source[s, q, c]
                target[i, comps * layers :, :] = jnp.zeros((pad - comps * layers, columns), f32)
    write_base(layers, rhs, diag, sol, base, shape)
    write_column_messages(sol, base, first, second, shape)


def column_sides(first, second):
    even = lax.axis_index(GROUP_AXES) % 2 == 0

    def low(kind, s):
        return jnp.where(even, second[kind, s].astype(f32), first[kind, s].astype(f32))

    def high(kind, s):
        return jnp.where(even, first[kind, s].astype(f32), second[kind, s].astype(f32))

    return low, high


def edge_cells(low, high, sol, s, cells_q):
    col, cols = lax.axis_index(GROUP_AXES), lax.axis_size(GROUP_AXES)
    left = jnp.where(col > 0, low(0, s) + sol[s * cells_q], 0.0)
    right = jnp.where(col < cols - 1, high(0, s) + sol[s * cells_q + cells_q - 1], 0.0)
    return left, right


def row_kernel(shape, sol, base, first_in, second_in, first, second):
    cells_s, cells_q = shape[:2]
    low, high = column_sides(first_in, second_in)
    even = lax.axis_index("sub") % 2 == 0
    for out, s in (
        (first, jnp.where(even, cells_s - 1, 0)),
        (second, jnp.where(even, 0, cells_s - 1)),
    ):
        left, right = edge_cells(low, high, sol, s, cells_q)
        out[0, 0] = left.astype(bf16)
        out[0, cells_q + 1] = right.astype(bf16)
        low_s, high_s = low(1, s), high(1, s)
        out[1, 0] = low_s.astype(bf16)
        out[1, cells_q + 1] = high_s.astype(bf16)
        for q in range(cells_q):
            value = base[s * cells_q + q]
            if q == 0:
                value = value + low_s
            if q == cells_q - 1:
                value = value + high_s
            out[0, q + 1] = value.astype(bf16)
            out[1, q + 1] = sol[s * cells_q + q].astype(bf16)


def window_kernel(
    shape, sol, base, first_q, second_q, first_s, second_s, basis_t, pack, message, packed, local
):
    cells_s, cells_q, _, pad, columns = shape
    wide = cells_q + 2
    low, high = column_sides(first_q, second_q)
    row, rows = lax.axis_index("sub"), lax.axis_size("sub")
    even = row % 2 == 0

    def above(kind, w):
        return jnp.where(even, second_s[kind, w].astype(f32), first_s[kind, w].astype(f32))

    def below(kind, w):
        return jnp.where(even, first_s[kind, w].astype(f32), second_s[kind, w].astype(f32))

    for s in range(cells_s):
        left, right = edge_cells(low, high, sol, s, cells_q)
        values = [left] + [base[s * cells_q + q] for q in range(cells_q)] + [right]
        values[1] = values[1] + low(1, s)
        values[cells_q] = values[cells_q] + high(1, s)
        for w in range(wide):
            value = values[w]
            if s == 0:
                value = value + above(1, w)
            if s == cells_s - 1:
                value = value + below(1, w)
            local[(s + 1) * wide + w] = value.astype(bf16)
    for s, side, place, there in (
        (0, above, 0, row > 0),
        (cells_s - 1, below, (cells_s + 1) * wide, row < rows - 1),
    ):
        near = [low(1, s)] + [sol[s * cells_q + q] for q in range(cells_q)] + [high(1, s)]
        for w in range(wide):
            local[place + w] = jnp.where(there, side(0, w) + near[w], 0.0).astype(bf16)
    flat = local[...].reshape(-1, columns)
    restricted = jnp.dot(basis_t[...], flat, preferred_element_type=f32).astype(bf16)
    for j in range(message.shape[0]):
        message[j] = restricted
    span, chunk = pack.shape
    for s in range(cells_s + 2):
        packed[s * span : (s + 1) * span, :] = jnp.dot(
            pack[...], flat[s * chunk : (s + 1) * chunk], preferred_element_type=f32
        ).astype(bf16)


def matmul_kernel(left, right, out):
    out[...] = jnp.dot(left[...], right[...], preferred_element_type=f32).astype(out.dtype)


def corrected(shape, arrived, fine, own_basis, sol, new):
    cells_s, cells_q, _, pad, columns = shape
    chosen = arrived[0].astype(f32)
    for h in range(1, arrived.shape[0]):
        chosen = chosen + arrived[h].astype(f32)
    chosen = chosen.astype(bf16)
    span = cells_q * pad
    for s in range(cells_s):
        part = slice(s * span, (s + 1) * span)
        change = fine[part, :] + jnp.dot(own_basis[part, :], chosen, preferred_element_type=f32)
        for q in range(cells_q):
            i = s * cells_q + q
            new[i] = sol[i] + change[q * pad : (q + 1) * pad]


def step_kernel(
    shape, layers, arrived, fine, own_basis, sol, rhs, diag, new, base, first, second
):
    corrected(shape, arrived, fine, own_basis, sol, new)
    write_base(layers, rhs, diag, new, base, shape)
    write_column_messages(new, base, first, second, shape)


def close_kernel(shape, layers, arrived, fine, own_basis, sol, out, new):
    cells_s, cells_q, comps, _, _ = shape
    corrected(shape, arrived, fine, own_basis, sol, new)
    for s in range(cells_s):
        for q in range(cells_q):
            for c in range(comps):
                out[s, q, c] = new[s * cells_q + q, c * layers : (c + 1) * layers, :]


def basis_kernel(basis, order, pack, pick, basis_t, own_basis):
    span, chunk = pack.shape
    rows = basis.shape[0] // span
    for s in range(rows):
        ordered = jnp.dot(
            basis[s * span : (s + 1) * span, :], order[...], preferred_element_type=f32
        ).astype(bf16)
        basis_t[:, s * chunk : (s + 1) * chunk] = lax.dot_general(
            ordered, pack[...], (((0,), (0,)), ((), ())), preferred_element_type=f32
        ).astype(bf16)
        if 0 < s < rows - 1:
            size = pick.shape[0]
            own_basis[(s - 1) * size : s * size, :] = jnp.dot(
                pick[...], ordered, preferred_element_type=f32
            ).astype(bf16)


def own_rows(sub_inverse, pick, rows):
    size, span = pick.shape
    width = sub_inverse.shape[2]
    return pl.pallas_call(
        lambda inverse, chosen, out: matmul_kernel(chosen, inverse.at[0], out),
        grid=(rows,),
        out_shape=jax.ShapeDtypeStruct((rows * size, width), bf16),
        in_specs=[
            pl.BlockSpec((1, span, width), lambda s: (0, s + 1, 0)),
            pl.BlockSpec((size, span), lambda s: (0, 0)),
        ],
        out_specs=pl.BlockSpec((size, width), lambda s: (s, 0)),
        compiler_params=pltpu.CompilerParams(vmem_limit_bytes=24 << 20),
        cost_estimate=pl.CostEstimate(
            flops=2 * rows * size * span * width,
            bytes_accessed=2 * rows * (size + span) * width,
            transcendentals=0,
        ),
    )(sub_inverse, pick)


def slots_of(offsets, kgroup, groups, depth):
    ends = jnp.concatenate(
        [offsets[..., 1:], jnp.full(offsets.shape[:-1] + (1,), kgroup, jnp.int32)], axis=-1
    )
    member = jnp.arange(groups, dtype=jnp.int32)[:, None]
    turn = jnp.arange(depth, dtype=jnp.int32)[None, :]
    first = offsets[..., None, None]
    slots = first + (member - first) % groups + turn * groups
    return slots, slots < ends[..., None, None]


def selections(basis, coarse_inverse, offsets):
    n_sub, share_rows, kgroup = coarse_inverse.shape
    max_cols = basis.shape[2]
    groups = offsets.shape[1]
    depth = -(-max_cols // groups)
    member = lax.axis_index(GROUP_AXES)
    sub_index = lax.axis_index("sub")
    every = lax.all_to_all(jnp.broadcast_to(offsets, (n_sub, groups)), "sub", 0, 0, tiled=True)
    slots, valid = slots_of(every, kgroup, groups, depth)
    own_slots, own_valid = slots_of(offsets[0], kgroup, groups, depth)
    member_slots = lax.dynamic_index_in_dim(own_slots, member, 0, keepdims=False).reshape(-1)
    member_valid = lax.dynamic_index_in_dim(own_valid, member, 0, keepdims=False).reshape(-1)
    member_start = lax.dynamic_index_in_dim(offsets[0], member, 0, keepdims=False)
    picked = jnp.where(member_valid, member_slots - member_start, -1)
    order = (jnp.arange(max_cols, dtype=jnp.int32)[:, None] == picked[None, :]).astype(bf16)
    mine = lax.dynamic_index_in_dim(slots, member, 2, keepdims=False).reshape(n_sub, -1)
    mine_valid = lax.dynamic_index_in_dim(valid, member, 2, keepdims=False).reshape(n_sub, -1)
    rows = jnp.where(mine_valid, mine // groups, -1)
    row_pick = (rows[:, :, None] == jnp.arange(share_rows, dtype=jnp.int32)).astype(bf16)
    col_pick = (
        jnp.arange(kgroup, dtype=jnp.int32)[:, None]
        == jnp.where(own_valid, own_slots, -1).reshape(1, -1)
    ).astype(bf16)
    spread = jnp.einsum("gri,gik->grk", row_pick, coarse_inverse, preferred_element_type=f32)
    spread = jnp.dot(
        spread.astype(bf16).reshape(-1, kgroup), col_pick, preferred_element_type=f32
    ).astype(bf16)
    return order, spread


def shards(rhs, start, stiffness, sub_inverse, basis, coarse_inverse, offsets):
    cells_s, cells_q, comps, layers, columns = rhs.shape
    n_sub = coarse_inverse.shape[0]
    groups = offsets.shape[1]
    depth = -(-basis.shape[2] // groups)
    coarse = groups * depth
    cells = cells_s * cells_q
    per_cell = comps * layers
    pad = -(-per_cell // 16) * 16
    wide = cells_q + 2
    shape = (cells_s, cells_q, comps, pad, columns)

    field = jax.ShapeDtypeStruct((cells, pad, columns), f32)
    column_message = jax.ShapeDtypeStruct((2, cells_s, pad, columns), bf16)
    row_message = jax.ShapeDtypeStruct((2, wide, pad, columns), bf16)

    pack_map = np.zeros((wide * per_cell, wide * pad), np.float32)
    for w in range(wide):
        for t in range(per_cell):
            pack_map[w * per_cell + t, w * pad + t] = 1.0
    pack = jnp.asarray(pack_map, bf16)
    pick = jnp.asarray(pack_map.T[pad : (wide - 1) * pad], bf16)

    diagonal = (6.0 + stiffness).reshape(cells, per_cell)
    diagonal = jnp.pad(diagonal, ((0, 0), (0, pad - per_cell)))
    diagonal = jnp.broadcast_to(diagonal[:, :, None], (cells, pad, 128))
    solution, rhs_cells, base, first, second = call(
        functools.partial(open_kernel, shape, layers),
        (start, rhs, diagonal),
        (field, field, field, column_message, column_message),
    )
    order, spread = selections(basis, coarse_inverse, offsets)
    basis_t, own_basis = call(
        basis_kernel,
        (basis[0], order, pack, pick),
        (
            jax.ShapeDtypeStruct((coarse, (cells_s + 2) * wide * pad), bf16),
            jax.ShapeDtypeStruct((cells * pad, coarse), bf16),
        ),
    )
    inverse_rows = own_rows(sub_inverse, pick, cells_s)

    for sweep in range(ITERS):
        first_q, second_q = swap(first, second, GROUP_AXES)
        first, second = call(
            functools.partial(row_kernel, shape),
            (solution, base, first_q, second_q),
            (row_message, row_message),
        )
        first_s, second_s = swap(first, second, "sub")
        message, packed = call(
            functools.partial(window_kernel, shape),
            (solution, base, first_q, second_q, first_s, second_s, basis_t, pack),
            (
                jax.ShapeDtypeStruct((groups, coarse, columns), bf16),
                jax.ShapeDtypeStruct((sub_inverse.shape[1], columns), bf16),
            ),
            scratch=(pltpu.VMEM(((cells_s + 2) * wide, pad, columns), bf16),),
        )
        gathered = lax.all_to_all(message, GROUP_AXES, 0, 0, tiled=True)
        (terms,) = call(
            matmul_kernel,
            (spread, gathered.reshape(-1, columns)),
            (jax.ShapeDtypeStruct((spread.shape[0], columns), bf16),),
            flops=2 * spread.size * columns,
        )
        arrived = lax.all_to_all(
            terms.reshape(n_sub * groups, depth, columns), ALL_AXES, 0, 0, tiled=True
        ).reshape(n_sub, coarse, columns)
        (fine,) = call(
            matmul_kernel,
            (inverse_rows, packed),
            (jax.ShapeDtypeStruct((cells * pad, columns), f32),),
            flops=2 * inverse_rows.size * columns,
        )
        if sweep < ITERS - 1:
            solution, base, first, second = call(
                functools.partial(step_kernel, shape, layers),
                (arrived, fine, own_basis, solution, rhs_cells, diagonal),
                (field, field, column_message, column_message),
            )
        else:
            (solution,) = call(
                functools.partial(close_kernel, shape, layers),
                (arrived, fine, own_basis, solution),
                (jax.ShapeDtypeStruct(rhs.shape, f32),),
                scratch=(pltpu.VMEM(field.shape, f32),),
            )
    return solution


def solution(mesh):
    return jax.shard_map(
        shards,
        mesh=mesh,
        in_specs=(
            P("sub", ("crow", "ccol"), None, None, None),
            P("sub", ("crow", "ccol"), None, None, None),
            P("sub", ("crow", "ccol"), None, None),
            P(("sub", "crow", "ccol"), None, None),
            P(("sub", "crow", "ccol"), None, None),
            P(None, ("crow", "ccol"), "sub"),
            P("sub", None),
        ),
        out_specs=P("sub", ("crow", "ccol"), None, None, None),
        check_vma=False,
    )
```

```python
import functools
import math

import jax
import jax.numpy as jnp
from jax import lax
from jax.experimental import pallas as pl
from jax.experimental.pallas import tpu as pltpu
from jax.sharding import PartitionSpec as P

ITERS = 2
GROUP_AXES = ("crow", "ccol")
ALL_AXES = ("sub", "crow", "ccol")
bf16, f32 = jnp.bfloat16, jnp.float32
VMEM = pl.BlockSpec(memory_space=pltpu.VMEM)
HBM = pl.BlockSpec(memory_space=pltpu.HBM)


def sized(x):
    return math.prod(x.shape) * jnp.dtype(x.dtype).itemsize


def call(body, ins, outs, scratch=(), flops=0, held=()):
    size = sum(sized(x) for x in (*ins, *outs))
    room = size + sum(sized(x) for x in scratch if getattr(x, "dtype", None) in (bf16, f32))
    return pl.pallas_call(
        body,
        out_shape=tuple(outs),
        in_specs=[HBM if i in held else VMEM for i in range(len(ins))],
        out_specs=tuple(
            HBM if getattr(x, "memory_space", None) == pltpu.HBM else VMEM for x in outs
        ),
        scratch_shapes=list(scratch),
        compiler_params=pltpu.CompilerParams(vmem_limit_bytes=room + (4 << 20)),
        cost_estimate=pl.CostEstimate(flops=flops, bytes_accessed=size, transcendentals=0),
    )(
        *[
            pltpu.with_memory_space_constraint(x, pltpu.HBM) if i in held else x
            for i, x in enumerate(ins)
        ]
    )


def begun(source, target, sem):
    copy = pltpu.make_async_copy(source, target, sem)
    copy.start()
    return copy


def packing(cells, per_cell, pad):
    row = lax.broadcasted_iota(jnp.int32, (cells * per_cell, cells * pad), 0)
    column = lax.broadcasted_iota(jnp.int32, (cells * per_cell, cells * pad), 1)
    for w in range(1, cells):
        column = column - jnp.where(row >= w * per_cell, pad - per_cell, 0)
    return jnp.where(row == column, 1.0, 0.0).astype(bf16)


def swap(first, second, axis):
    count = lax.axis_size(axis)
    even = [(i, i + 1) for i in range(0, count - 1, 2)]
    odd = [(i, i + 1) for i in range(1, count - 1, 2)]
    return (
        lax.ppermute(first, axis, even + [(b, a) for a, b in even]),
        lax.ppermute(second, axis, odd + [(b, a) for a, b in odd]),
    )


def diagonal_of(stiffness, s, q, comps, layers, pad, columns):
    at = lax.broadcasted_iota(jnp.int32, (pad, layers), 0)
    layer = lax.broadcasted_iota(jnp.int32, (pad, layers), 1)
    column = jnp.zeros((pad, layers), f32)
    for c in range(comps):
        column = jnp.where(at == layer + c * layers, stiffness[s, q, c : c + 1, :], column)
    column = 6.0 + jnp.sum(column, axis=1, keepdims=True)
    return jnp.broadcast_to(column, (pad, columns))


def write_base(layers, begin, stiffness, field, base, shape):
    cells_s, cells_q, comps, pad, columns = shape
    at = lax.broadcasted_iota(jnp.int32, (pad, columns), 0)
    has_up, has_down = at < comps * layers, at < comps * layers
    for c in range(comps):
        has_up = has_up & (at != c * layers)
        has_down = has_down & (at != c * layers + layers - 1)
    for s in range(cells_s):
        for q in range(cells_q):
            i = s * cells_q + q
            x = field[i]
            diagonal = diagonal_of(stiffness, s, q, comps, layers, pad, columns)
            total = begin[i] - diagonal * x
            total = total + jnp.where(has_up, pltpu.roll(x, 1, 0), 0.0)
            total = total + jnp.where(has_down, pltpu.roll(x, pad - 1, 0), 0.0)
            if q > 0:
                total = total + field[i - 1]
            if q < cells_q - 1:
                total = total + field[i + 1]
            if s > 0:
                total = total + field[i - cells_q]
            if s < cells_s - 1:
                total = total + field[i + cells_q]
            base[i] = total


def write_column_messages(sol, base, first, second, shape):
    cells_s, cells_q = shape[:2]
    even = lax.axis_index(GROUP_AXES) % 2 == 0
    for out, q in (
        (first, jnp.where(even, cells_q - 1, 0)),
        (second, jnp.where(even, 0, cells_q - 1)),
    ):
        for s in range(cells_s):
            out[0, s] = base[s * cells_q + q].astype(bf16)
            out[1, s] = sol[s * cells_q + q].astype(bf16)


def open_kernel(
    shape, layers, start, rhs, stiffness, offsets, sol, base, first, second, sent, begin
):
    cells_s, cells_q, comps, pad, columns = shape
    sent[...] = jnp.broadcast_to(offsets[...], sent.shape)
    for s in range(cells_s):
        for q in range(cells_q):
            i = s * cells_q + q
            for source, target in ((start, sol), (rhs, begin)):
                for c in range(comps):
                    target[i, c * layers : (c + 1) * layers, :] = source[s, q, c]
                target[i, comps * layers :, :] = jnp.zeros((pad - comps * layers, columns), f32)
    write_base(layers, begin, stiffness, sol, base, shape)
    write_column_messages(sol, base, first, second, shape)


def column_sides(first, second):
    even = lax.axis_index(GROUP_AXES) % 2 == 0

    def low(kind, s):
        return jnp.where(even, second[kind, s].astype(f32), first[kind, s].astype(f32))

    def high(kind, s):
        return jnp.where(even, first[kind, s].astype(f32), second[kind, s].astype(f32))

    return low, high


def edge_cells(low, high, sol, s, cells_q):
    col, cols = lax.axis_index(GROUP_AXES), lax.axis_size(GROUP_AXES)
    left = jnp.where(col > 0, low(0, s) + sol[s * cells_q], 0.0)
    right = jnp.where(col < cols - 1, high(0, s) + sol[s * cells_q + cells_q - 1], 0.0)
    return left, right


def row_kernel(shape, sol, base, first_in, second_in, first, second):
    cells_s, cells_q = shape[:2]
    low, high = column_sides(first_in, second_in)
    even = lax.axis_index("sub") % 2 == 0
    for out, s in (
        (first, jnp.where(even, cells_s - 1, 0)),
        (second, jnp.where(even, 0, cells_s - 1)),
    ):
        left, right = edge_cells(low, high, sol, s, cells_q)
        out[0, 0] = left.astype(bf16)
        out[0, cells_q + 1] = right.astype(bf16)
        low_s, high_s = low(1, s), high(1, s)
        out[1, 0] = low_s.astype(bf16)
        out[1, cells_q + 1] = high_s.astype(bf16)
        for q in range(cells_q):
            value = base[s * cells_q + q]
            if q == 0:
                value = value + low_s
            if q == cells_q - 1:
                value = value + high_s
            out[0, q + 1] = value.astype(bf16)
            out[1, q + 1] = sol[s * cells_q + q].astype(bf16)


def window_kernel(
    shape,
    sol,
    base,
    first_q,
    second_q,
    first_s,
    second_s,
    basis_t,
    message,
    local_kept,
    local,
    restricted,
    sems,
):
    cells_s, cells_q, _, pad, columns = shape
    wide = cells_q + 2
    low, high = column_sides(first_q, second_q)
    row, rows = lax.axis_index("sub"), lax.axis_size("sub")
    even = row % 2 == 0

    def above(kind, w):
        return jnp.where(even, second_s[kind, w].astype(f32), first_s[kind, w].astype(f32))

    def below(kind, w):
        return jnp.where(even, first_s[kind, w].astype(f32), second_s[kind, w].astype(f32))

    for s in range(cells_s):
        left, right = edge_cells(low, high, sol, s, cells_q)
        values = [left] + [base[s * cells_q + q] for q in range(cells_q)] + [right]
        values[1] = values[1] + low(1, s)
        values[cells_q] = values[cells_q] + high(1, s)
        for w in range(wide):
            value = values[w]
            if s == 0:
                value = value + above(1, w)
            if s == cells_s - 1:
                value = value + below(1, w)
            local[(s + 1) * wide + w] = value.astype(bf16)
    for s, side, place, there in (
        (0, above, 0, row > 0),
        (cells_s - 1, below, (cells_s + 1) * wide, row < rows - 1),
    ):
        near = [low(1, s)] + [sol[s * cells_q + q] for q in range(cells_q)] + [high(1, s)]
        for w in range(wide):
            local[place + w] = jnp.where(there, side(0, w) + near[w], 0.0).astype(bf16)
    copies = [begun(local, local_kept, sems.at[0])]
    restricted[...] = jnp.dot(
        basis_t[...], local[...].reshape(-1, columns), preferred_element_type=f32
    ).astype(bf16)
    for j in range(message.shape[0]):
        copies.append(begun(restricted, message.at[j], sems.at[j + 1]))
    for copy in copies:
        copy.wait()


def terms_kernel(spread, gathered, out, kept, sem):
    kept[...] = jnp.dot(spread[...], gathered[...], preferred_element_type=f32).astype(bf16)
    begun(kept, out, sem).wait()


def fine_kernel(shape, layers, steps, last, local_kept, inverse_kept, sol_kept, *refs):
    cells_s, cells_q, comps, pad, columns = shape
    if last:
        out, local, inverse, packed, sol, fine, sems = refs
        fields = ((sol_kept, sol),)
    else:
        base_kept, stiffness, out, base_out, local, inverse, packed, sol, fine, base, sems = refs
        fields = ((sol_kept, sol), (base_kept, base))
    per_cell = comps * layers
    wide = cells_q + 2
    span, chunk = wide * per_cell, wide * pad
    size = cells_s // steps
    loaded = begun(local_kept, local, sems.at[0])
    arriving = [
        begun(
            inverse_kept.at[0, pl.ds((k * size + 1) * span, size * span)],
            inverse.at[pl.ds(k * size * span, size * span)],
            sems.at[k + 1],
        )
        for k in range(steps)
    ]
    others = [begun(a, b, sems.at[steps + 1 + k]) for k, (a, b) in enumerate(fields)]
    pack = packing(wide, per_cell, pad)
    loaded.wait()
    for s in range(packed.shape[0] // span):
        part = local[s * wide : (s + 1) * wide].reshape(chunk, columns)
        packed[s * span : (s + 1) * span, :] = jnp.dot(
            pack, part, preferred_element_type=f32
        ).astype(bf16)
    for k in range(steps):
        arriving[k].wait()
        rows = jnp.dot(
            inverse[k * size * span : (k + 1) * size * span, :],
            packed[...],
            preferred_element_type=f32,
        )
        for s in range(size):
            for q in range(cells_q):
                i = (k * size + s) * cells_q + q
                first = s * span + (q + 1) * per_cell
                fine[i, :per_cell, :] = rows[first : first + per_cell]
                fine[i, per_cell:, :] = jnp.zeros((pad - per_cell, columns), f32)
    for copy in others:
        copy.wait()
    for i in range(fine.shape[0]):
        sol[i] = sol[i] + fine[i]
    copies = [begun(sol, out, sems.at[steps + 3])]
    if not last:
        write_base(layers, base, stiffness, fine, base, shape)
        copies.append(begun(base, base_out, sems.at[steps + 4]))
    for copy in copies:
        copy.wait()


def fine_product(shape, layers, local, sub_inverse, sol, base, stiffness, last):
    cells_s, cells_q, comps, pad, columns = shape
    width = sub_inverse.shape[2]
    rows = cells_s * (cells_q + 2) * comps * layers
    steps = 3 if cells_s % 3 == 0 else 1
    kept = pltpu.HBM((cells_s * cells_q, pad, columns), f32)
    field = pltpu.VMEM(kept.shape, f32)
    return call(
        functools.partial(fine_kernel, shape, layers, steps, last),
        (local, sub_inverse, sol) if last else (local, sub_inverse, sol, base, stiffness),
        (kept,) if last else (kept, kept),
        scratch=(
            pltpu.VMEM(local.shape, bf16),
            pltpu.VMEM((rows, width), bf16),
            pltpu.VMEM((width, columns), bf16),
        )
        + ((field, field) if last else (field, field, field))
        + (pltpu.SemaphoreType.DMA((steps + 5,)),),
        flops=2 * rows * width * columns,
        held=(0, 1, 2) if last else (0, 1, 2, 3),
    )


def coarse_part(shape, arrived, basis_p, coarse):
    cells_s, cells_q, _, pad, _ = shape
    chosen = arrived[0].astype(f32)
    for h in range(1, arrived.shape[0]):
        chosen = chosen + arrived[h].astype(f32)
    chosen = chosen.astype(bf16)
    chunk = (cells_q + 2) * pad
    for s in range(cells_s):
        first = (s + 1) * chunk + pad
        rows = jnp.dot(
            basis_p[first : first + cells_q * pad, :], chosen, preferred_element_type=f32
        )
        coarse[s * cells_q : (s + 1) * cells_q] = rows.reshape(cells_q, pad, -1)


def step_kernel(
    shape,
    layers,
    arrived,
    basis_kept,
    sol_kept,
    base_kept,
    stiffness,
    new,
    base,
    first,
    second,
    basis_p,
    coarse,
    begin,
    sems,
):
    sources, targets = (basis_kept, sol_kept, base_kept), (basis_p, new, begin)
    copies = [begun(a, b, sems.at[k]) for k, (a, b) in enumerate(zip(sources, targets))]
    copies[0].wait()
    coarse_part(shape, arrived, basis_p, coarse)
    copies[1].wait()
    for i in range(new.shape[0]):
        new[i] = new[i] + coarse[i]
    copies[2].wait()
    write_base(layers, begin, stiffness, coarse, base, shape)
    write_column_messages(new, base, first, second, shape)


def close_kernel(shape, layers, arrived, basis_kept, sol_kept, out, basis_p, coarse, sol, sems):
    cells_s, cells_q, comps, _, _ = shape
    sources, targets = (basis_kept, sol_kept), (basis_p, sol)
    copies = [begun(a, b, sems.at[k]) for k, (a, b) in enumerate(zip(sources, targets))]
    copies[0].wait()
    coarse_part(shape, arrived, basis_p, coarse)
    copies[1].wait()
    for s in range(cells_s):
        for q in range(cells_q):
            i = s * cells_q + q
            for c in range(comps):
                part = slice(c * layers, (c + 1) * layers)
                out[s, q, c] = sol[i, part, :] + coarse[i, part, :]


def places(offsets, g, j, groups, depth, kgroup, shape):
    first = offsets[g, j]
    end = kgroup if j == groups - 1 else offsets[g, j + 1]
    at = lax.broadcasted_iota(jnp.int32, shape, 1)
    turn = at
    member = jnp.zeros(shape, jnp.int32)
    for m in range(1, groups):
        member = member + jnp.where(at >= m * depth, 1, 0)
        turn = turn - jnp.where(at >= m * depth, depth, 0)
    shifted = member - lax.rem(first, groups)
    shifted = jnp.where(shifted < 0, shifted + groups, shifted)
    place = shifted + turn * groups
    return first, place, place < end - first


def basis_kernel(dims, offsets, basis, basis_t, basis_p):
    wide, per_cell, pad, groups, depth, kgroup = dims
    span, chunk = wide * per_cell, wide * pad
    pack = packing(wide, per_cell, pad)
    member = lax.axis_index(GROUP_AXES)
    shape = (basis.shape[2], groups * depth)
    row = lax.broadcasted_iota(jnp.int32, shape, 0)
    order = jnp.zeros(shape, f32)
    for j in range(groups):
        _, place, valid = places(offsets, 0, j, groups, depth, kgroup, shape)
        order = order + jnp.where((row == place) & valid & (member == j), 1.0, 0.0)
    order = order.astype(bf16)
    for s in range(basis.shape[1] // span):
        ordered = jnp.dot(
            basis[0, s * span : (s + 1) * span, :], order, preferred_element_type=f32
        ).astype(bf16)
        part = slice(s * chunk, (s + 1) * chunk)
        basis_t[:, part] = lax.dot_general(
            ordered, pack, (((0,), (0,)), ((), ())), preferred_element_type=f32
        ).astype(bf16)
        basis_p[part, :] = lax.dot_general(
            pack, ordered, (((0,), (0,)), ((), ())), preferred_element_type=f32
        ).astype(bf16)


def spread_kernel(dims, every, inverse, out, columns):
    groups, depth, kgroup = dims
    g = pl.program_id(0)
    member = lax.axis_index(GROUP_AXES)

    @pl.when(g == 0)
    def _():
        own = lax.axis_index("sub")
        shape = (kgroup, groups * depth)
        slot = lax.broadcasted_iota(jnp.int32, shape, 0)
        for j in range(groups):
            first, place, valid = places(every, own, j, groups, depth, kgroup, shape)
            columns[:, j * groups * depth : (j + 1) * groups * depth] = jnp.where(
                (slot == place + first) & valid, 1.0, 0.0
            ).astype(bf16)

    rows = inverse.shape[1]
    turn = lax.broadcasted_iota(jnp.int32, (depth, rows), 0)
    index = lax.broadcasted_iota(jnp.int32, (depth, rows), 1)
    picks = []
    for j in range(groups):
        first = every[g, j]
        end = kgroup if j == groups - 1 else every[g, j + 1]
        begin = lax.div(first - member + groups - 1, groups)
        wanted = (index == turn + begin) & (index * groups + member < end)
        picks.append(jnp.where(wanted, 1.0, 0.0).astype(bf16))
    picked = jnp.dot(
        jnp.concatenate(picks, axis=0), inverse[0], preferred_element_type=f32
    ).astype(bf16)
    out[...] = jnp.dot(picked, columns[...], preferred_element_type=f32).astype(bf16)


def spread_inverse(every, coarse_inverse, depth):
    n_sub, share_rows, kgroup = coarse_inverse.shape
    groups = every.shape[1]
    coarse = groups * depth
    return pl.pallas_call(
        functools.partial(spread_kernel, (groups, depth, kgroup)),
        grid=(n_sub,),
        out_shape=pltpu.HBM((n_sub * coarse, groups * coarse), bf16),
        in_specs=[
            pl.BlockSpec(memory_space=pltpu.SMEM),
            pl.BlockSpec((1, share_rows, kgroup), lambda g: (g, 0, 0)),
        ],
        out_specs=pl.BlockSpec((coarse, groups * coarse), lambda g: (g, 0)),
        scratch_shapes=[pltpu.VMEM((kgroup, groups * coarse), bf16)],
        compiler_params=pltpu.CompilerParams(vmem_limit_bytes=10 << 20),
        cost_estimate=pl.CostEstimate(
            flops=2 * n_sub * coarse * groups * coarse * kgroup,
            bytes_accessed=4 * n_sub * coarse * groups * coarse,
            transcendentals=0,
        ),
    )(every, coarse_inverse)


def shards(rhs, start, stiffness, sub_inverse, basis, coarse_inverse, offsets):
    cells_s, cells_q, comps, layers, columns = rhs.shape
    n_sub, _, kgroup = coarse_inverse.shape
    groups = offsets.shape[1]
    depth = -(-basis.shape[2] // groups)
    coarse = groups * depth
    cells = cells_s * cells_q
    per_cell = comps * layers
    pad = -(-per_cell // 16) * 16
    wide = cells_q + 2
    shape = (cells_s, cells_q, comps, pad, columns)

    field = jax.ShapeDtypeStruct((cells, pad, columns), f32)
    column_message = jax.ShapeDtypeStruct((2, cells_s, pad, columns), bf16)
    row_message = jax.ShapeDtypeStruct((2, wide, pad, columns), bf16)

    rows = (cells_s + 2) * wide * pad

    solution, base, first, second, sent = call(
        functools.partial(open_kernel, shape, layers),
        (start, rhs, stiffness, offsets),
        (
            field,
            field,
            column_message,
            column_message,
            jax.ShapeDtypeStruct((n_sub, groups), jnp.int32),
        ),
        scratch=(pltpu.VMEM(field.shape, f32),),
    )
    basis_t, basis_p = pl.pallas_call(
        functools.partial(basis_kernel, (wide, per_cell, pad, groups, depth, kgroup)),
        out_shape=(pltpu.HBM((coarse, rows), bf16), pltpu.HBM((rows, coarse), bf16)),
        in_specs=[pl.BlockSpec(memory_space=pltpu.SMEM), VMEM],
        out_specs=(
            pl.BlockSpec((coarse, rows), lambda: (0, 0)),
            pl.BlockSpec((rows, coarse), lambda: (0, 0)),
        ),
        compiler_params=pltpu.CompilerParams(vmem_limit_bytes=12 << 20),
        cost_estimate=pl.CostEstimate(
            flops=6 * rows * coarse * wide * pad, bytes_accessed=6 * basis.size, transcendentals=0
        ),
    )(offsets, basis)
    sent, _ = lax.optimization_barrier((sent, basis_t))
    every = lax.all_to_all(sent, "sub", 0, 0, tiled=True)
    spread = spread_inverse(every, coarse_inverse, depth)

    for sweep in range(ITERS):
        first_q, second_q = swap(first, second, GROUP_AXES)
        if sweep == 0:
            first_q, second_q, basis_t = lax.optimization_barrier((first_q, second_q, basis_t))
        first, second = call(
            functools.partial(row_kernel, shape),
            (solution, base, first_q, second_q),
            (row_message, row_message),
        )
        first_s, second_s = swap(first, second, "sub")
        message, local = call(
            functools.partial(window_kernel, shape),
            (solution, base, first_q, second_q, first_s, second_s, basis_t),
            (
                pltpu.HBM((groups, coarse, columns), bf16),
                pltpu.HBM(((cells_s + 2) * wide, pad, columns), bf16),
            ),
            scratch=(
                pltpu.VMEM(((cells_s + 2) * wide, pad, columns), bf16),
                pltpu.VMEM((coarse, columns), bf16),
                pltpu.SemaphoreType.DMA((groups + 1,)),
            ),
            flops=2 * rows * coarse * columns,
        )
        gathered = lax.all_to_all(message, GROUP_AXES, 0, 0, tiled=True)
        (terms,) = call(
            terms_kernel,
            (spread, gathered.reshape(-1, columns)),
            (pltpu.HBM((spread.shape[0], columns), bf16),),
            scratch=(pltpu.VMEM((spread.shape[0], columns), bf16), pltpu.SemaphoreType.DMA),
            flops=2 * spread.size * columns,
        )
        arrived = lax.all_to_all(
            terms.reshape(n_sub * groups, depth, columns), ALL_AXES, 0, 0, tiled=True
        ).reshape(n_sub, coarse, columns)
        last = sweep == ITERS - 1
        kept = fine_product(
            shape, layers, local, sub_inverse, solution, base, stiffness, last
        )
        if last:
            (solution,) = call(
                functools.partial(close_kernel, shape, layers),
                (arrived, basis_p, *kept),
                (jax.ShapeDtypeStruct(rhs.shape, f32),),
                scratch=(
                    pltpu.VMEM((rows, coarse), bf16),
                    pltpu.VMEM(field.shape, f32),
                    pltpu.VMEM(field.shape, f32),
                    pltpu.SemaphoreType.DMA((2,)),
                ),
                held=(1, 2),
            )
        else:
            solution, base, first, second = call(
                functools.partial(step_kernel, shape, layers),
                (arrived, basis_p, *kept, stiffness),
                (field, field, column_message, column_message),
                scratch=(
                    pltpu.VMEM((rows, coarse), bf16),
                    pltpu.VMEM(field.shape, f32),
                    pltpu.VMEM(field.shape, f32),
                    pltpu.SemaphoreType.DMA((3,)),
                ),
                held=(1, 2, 3),
            )
    return solution


def solution(mesh):
    return jax.shard_map(
        shards,
        mesh=mesh,
        in_specs=(
            P("sub", ("crow", "ccol"), None, None, None),
            P("sub", ("crow", "ccol"), None, None, None),
            P("sub", ("crow", "ccol"), None, None),
            P(("sub", "crow", "ccol"), None, None),
            P(("sub", "crow", "ccol"), None, None),
            P(None, ("crow", "ccol"), "sub"),
            P("sub", None),
        ),
        out_specs=P("sub", ("crow", "ccol"), None, None, None),
        check_vma=False,
    )
```

```python
import functools
import math

import jax
import jax.numpy as jnp
from jax import lax
from jax.experimental import pallas as pl
from jax.experimental.pallas import tpu as pltpu
from jax.sharding import PartitionSpec as P

ITERS = 2
GROUP_AXES = ("crow", "ccol")
ALL_AXES = ("sub", "crow", "ccol")
bf16, f32 = jnp.bfloat16, jnp.float32
VMEM = pl.BlockSpec(memory_space=pltpu.VMEM)
HBM = pl.BlockSpec(memory_space=pltpu.HBM)


def sized(x):
    return math.prod(x.shape) * jnp.dtype(x.dtype).itemsize


def call(body, ins, outs, scratch=(), flops=0, held=()):
    size = sum(sized(x) for x in (*ins, *outs))
    room = size + sum(sized(x) for x in scratch if getattr(x, "dtype", None) in (bf16, f32))
    return pl.pallas_call(
        body,
        out_shape=tuple(outs),
        in_specs=[HBM if i in held else VMEM for i in range(len(ins))],
        out_specs=tuple(
            HBM if getattr(x, "memory_space", None) == pltpu.HBM else VMEM for x in outs
        ),
        scratch_shapes=list(scratch),
        compiler_params=pltpu.CompilerParams(vmem_limit_bytes=room + (4 << 20)),
        cost_estimate=pl.CostEstimate(flops=flops, bytes_accessed=size, transcendentals=0),
    )(
        *[
            pltpu.with_memory_space_constraint(x, pltpu.HBM) if i in held else x
            for i, x in enumerate(ins)
        ]
    )


def begun(source, target, sem):
    copy = pltpu.make_async_copy(source, target, sem)
    copy.start()
    return copy


def packing(cells, per_cell, pad, turned=False):
    shape = (cells * per_cell, cells * pad)
    shape = shape[::-1] if turned else shape
    row = lax.broadcasted_iota(jnp.int32, shape, 1 if turned else 0)
    column = lax.broadcasted_iota(jnp.int32, shape, 0 if turned else 1)
    for w in range(1, cells):
        column = column - jnp.where(row >= w * per_cell, pad - per_cell, 0)
    return jnp.where(row == column, 1.0, 0.0).astype(bf16)


def swap(first, second, axis):
    count = lax.axis_size(axis)
    even = [(i, i + 1) for i in range(0, count - 1, 2)]
    odd = [(i, i + 1) for i in range(1, count - 1, 2)]
    return (
        lax.ppermute(first, axis, even + [(b, a) for a, b in even]),
        lax.ppermute(second, axis, odd + [(b, a) for a, b in odd]),
    )


def doubled(held, step):
    count = lax.axis_size("sub")
    return held + lax.ppermute(held, "sub", [(i, i ^ step) for i in range(count)])


def diagonal_of(stiffness, s, q, comps, layers, pad, columns):
    at = lax.broadcasted_iota(jnp.int32, (pad, layers), 0)
    layer = lax.broadcasted_iota(jnp.int32, (pad, layers), 1)
    column = jnp.zeros((pad, layers), f32)
    for c in range(comps):
        column = jnp.where(at == layer + c * layers, stiffness[s, q, c : c + 1, :], column)
    column = 6.0 + jnp.sum(column, axis=1, keepdims=True)
    return jnp.broadcast_to(column, (pad, columns))


def write_base(layers, begin, stiffness, field, base, shape, only=None):
    cells_s, cells_q, comps, pad, columns = shape
    at = lax.broadcasted_iota(jnp.int32, (pad, columns), 0)
    has_up, has_down = at < comps * layers, at < comps * layers
    for c in range(comps):
        has_up = has_up & (at != c * layers)
        has_down = has_down & (at != c * layers + layers - 1)
    for s in range(cells_s):
        for q in only or range(cells_q):
            i = s * cells_q + q
            x = field[i]
            diagonal = diagonal_of(stiffness, s, q, comps, layers, pad, columns)
            total = begin[i] - diagonal * x
            total = total + jnp.where(has_up, pltpu.roll(x, 1, 0), 0.0)
            total = total + jnp.where(has_down, pltpu.roll(x, pad - 1, 0), 0.0)
            if q > 0:
                total = total + field[i - 1]
            if q < cells_q - 1:
                total = total + field[i + 1]
            if s > 0:
                total = total + field[i - cells_q]
            if s < cells_s - 1:
                total = total + field[i + cells_q]
            base[i] = total


def write_column_messages(sol, base, first, second, shape):
    cells_s, cells_q = shape[:2]
    even = lax.axis_index(GROUP_AXES) % 2 == 0
    for out, q in (
        (first, jnp.where(even, cells_q - 1, 0)),
        (second, jnp.where(even, 0, cells_q - 1)),
    ):
        for s in range(cells_s):
            out[0, s] = base[s * cells_q + q].astype(bf16)
            out[1, s] = sol[s * cells_q + q].astype(bf16)


def unpack_cell(source, target, i, shape, layers):
    _, _, comps, pad, columns = shape
    for c in range(comps):
        target[i, c * layers : (c + 1) * layers, :] = source[:, c, :]
    target[i, comps * layers :, :] = jnp.zeros((pad - comps * layers, columns), f32)


def open_sides_kernel(
    shape, layers, start, rhs, stiffness, first, second, raw, raw_rhs, stiff, sol, begin, base, sems
):
    cells_s, cells_q = shape[:2]
    sides = (0, cells_q - 1)
    near = (0, 1, cells_q - 2, cells_q - 1)
    copies = [
        begun(stiffness, stiff, sems.at[0]),
        begun(start.at[:, pl.ds(0, 2)], raw.at[:, pl.ds(0, 2)], sems.at[1]),
        begun(start.at[:, pl.ds(cells_q - 2, 2)], raw.at[:, pl.ds(2, 2)], sems.at[2]),
        begun(rhs.at[:, pl.ds(0, 1)], raw_rhs.at[:, pl.ds(0, 1)], sems.at[3]),
        begun(rhs.at[:, pl.ds(cells_q - 1, 1)], raw_rhs.at[:, pl.ds(1, 1)], sems.at[4]),
    ]
    for copy in copies:
        copy.wait()
    for s in range(cells_s):
        for k, q in enumerate(near):
            unpack_cell(raw.at[s, k], sol, s * cells_q + q, shape, layers)
        for k, q in enumerate(sides):
            unpack_cell(raw_rhs.at[s, k], begin, s * cells_q + q, shape, layers)
    write_base(layers, begin, stiff, sol, base, shape, sides)
    write_column_messages(sol, base, first, second, shape)


def open_kernel(
    shape, layers, start, rhs, stiffness, offsets, sol, base, sent, raw, raw_rhs, stiff, own, begin, sems
):
    cells_s, cells_q = shape[:2]
    sources, targets = (stiffness, offsets, start, rhs), (stiff, own, raw, raw_rhs)
    copies = [begun(a, b, sems.at[k]) for k, (a, b) in enumerate(zip(sources, targets))]
    for copy in copies:
        copy.wait()
    group = lax.broadcasted_iota(jnp.int32, sent.shape, 0)
    sent[...] = jnp.where(group == lax.axis_index("sub"), own[...], 0)
    for s in range(cells_s):
        for q in range(cells_q):
            unpack_cell(raw.at[s, q], sol, s * cells_q + q, shape, layers)
            unpack_cell(raw_rhs.at[s, q], begin, s * cells_q + q, shape, layers)
    write_base(layers, begin, stiff, sol, base, shape)


def column_sides(first, second):
    even = lax.axis_index(GROUP_AXES) % 2 == 0

    def low(kind, s):
        return jnp.where(even, second[kind, s].astype(f32), first[kind, s].astype(f32))

    def high(kind, s):
        return jnp.where(even, first[kind, s].astype(f32), second[kind, s].astype(f32))

    return low, high


def edge_cells(low, high, sol, s, cells_q):
    col, cols = lax.axis_index(GROUP_AXES), lax.axis_size(GROUP_AXES)
    left = jnp.where(col > 0, low(0, s) + sol[s * cells_q], 0.0)
    right = jnp.where(col < cols - 1, high(0, s) + sol[s * cells_q + cells_q - 1], 0.0)
    return left, right


def row_kernel(shape, sol, base, first_in, second_in, first, second):
    cells_s, cells_q = shape[:2]
    low, high = column_sides(first_in, second_in)
    even = lax.axis_index("sub") % 2 == 0
    for out, s in (
        (first, jnp.where(even, cells_s - 1, 0)),
        (second, jnp.where(even, 0, cells_s - 1)),
    ):
        left, right = edge_cells(low, high, sol, s, cells_q)
        out[0, 0] = left.astype(bf16)
        out[0, cells_q + 1] = right.astype(bf16)
        low_s, high_s = low(1, s), high(1, s)
        out[1, 0] = low_s.astype(bf16)
        out[1, cells_q + 1] = high_s.astype(bf16)
        for q in range(cells_q):
            value = base[s * cells_q + q]
            if q == 0:
                value = value + low_s
            if q == cells_q - 1:
                value = value + high_s
            out[0, q + 1] = value.astype(bf16)
            out[1, q + 1] = sol[s * cells_q + q].astype(bf16)


def window_kernel(
    shape,
    sol,
    base,
    first_q,
    second_q,
    first_s,
    second_s,
    basis_t,
    message,
    local_kept,
    local,
    restricted,
    sems,
):
    cells_s, cells_q, _, pad, columns = shape
    wide = cells_q + 2
    low, high = column_sides(first_q, second_q)
    row, rows = lax.axis_index("sub"), lax.axis_size("sub")
    even = row % 2 == 0

    def above(kind, w):
        return jnp.where(even, second_s[kind, w].astype(f32), first_s[kind, w].astype(f32))

    def below(kind, w):
        return jnp.where(even, first_s[kind, w].astype(f32), second_s[kind, w].astype(f32))

    for s in range(cells_s):
        left, right = edge_cells(low, high, sol, s, cells_q)
        values = [left] + [base[s * cells_q + q] for q in range(cells_q)] + [right]
        values[1] = values[1] + low(1, s)
        values[cells_q] = values[cells_q] + high(1, s)
        for w in range(wide):
            value = values[w]
            if s == 0:
                value = value + above(1, w)
            if s == cells_s - 1:
                value = value + below(1, w)
            local[(s + 1) * wide + w] = value.astype(bf16)
    for s, side, place, there in (
        (0, above, 0, row > 0),
        (cells_s - 1, below, (cells_s + 1) * wide, row < rows - 1),
    ):
        near = [low(1, s)] + [sol[s * cells_q + q] for q in range(cells_q)] + [high(1, s)]
        for w in range(wide):
            local[place + w] = jnp.where(there, side(0, w) + near[w], 0.0).astype(bf16)
    copies = [begun(local, local_kept, sems.at[0])]
    restricted[...] = jnp.dot(
        basis_t[...], local[...].reshape(-1, columns), preferred_element_type=f32
    ).astype(bf16)
    for j in range(message.shape[0]):
        copies.append(begun(restricted, message.at[j], sems.at[j + 1]))
    for copy in copies:
        copy.wait()


def terms_kernel(spread, gathered, out, kept, sem):
    kept[...] = jnp.dot(spread[...], gathered[...], preferred_element_type=f32).astype(bf16)
    begun(kept, out, sem).wait()


def fine_kernel(shape, layers, steps, last, local_kept, inverse_kept, sol_kept, *refs):
    cells_s, cells_q, comps, pad, columns = shape
    if last:
        out, local, inverse, packed, sol, fine, sems = refs
        fields = ((sol_kept, sol),)
    else:
        base_kept, stiffness, out, base_out, local, inverse, packed, sol, fine, base, sems = refs
        fields = ((sol_kept, sol), (base_kept, base))
    per_cell = comps * layers
    wide = cells_q + 2
    span, chunk = wide * per_cell, wide * pad
    size = cells_s // steps
    loaded = begun(local_kept, local, sems.at[0])
    arriving = [
        begun(
            inverse_kept.at[0, pl.ds((k * size + 1) * span, size * span)],
            inverse.at[pl.ds(k * size * span, size * span)],
            sems.at[k + 1],
        )
        for k in range(steps)
    ]
    others = [begun(a, b, sems.at[steps + 1 + k]) for k, (a, b) in enumerate(fields)]
    pack = packing(wide, per_cell, pad)
    loaded.wait()
    for s in range(packed.shape[0] // span):
        part = local[s * wide : (s + 1) * wide].reshape(chunk, columns)
        packed[s * span : (s + 1) * span, :] = jnp.dot(
            pack, part, preferred_element_type=f32
        ).astype(bf16)
    for k in range(steps):
        arriving[k].wait()
        rows = jnp.dot(
            inverse[k * size * span : (k + 1) * size * span, :],
            packed[...],
            preferred_element_type=f32,
        )
        for s in range(size):
            for q in range(cells_q):
                i = (k * size + s) * cells_q + q
                first = s * span + (q + 1) * per_cell
                fine[i, :per_cell, :] = rows[first : first + per_cell]
                fine[i, per_cell:, :] = jnp.zeros((pad - per_cell, columns), f32)
    for copy in others:
        copy.wait()
    for i in range(fine.shape[0]):
        sol[i] = sol[i] + fine[i]
    copies = [begun(sol, out, sems.at[steps + 3])]
    if not last:
        write_base(layers, base, stiffness, fine, base, shape)
        copies.append(begun(base, base_out, sems.at[steps + 4]))
    for copy in copies:
        copy.wait()


def fine_product(shape, layers, local, sub_inverse, sol, base, stiffness, last):
    cells_s, cells_q, comps, pad, columns = shape
    width = sub_inverse.shape[2]
    rows = cells_s * (cells_q + 2) * comps * layers
    steps = 3 if cells_s % 3 == 0 else 1
    kept = pltpu.HBM((cells_s * cells_q, pad, columns), f32)
    field = pltpu.VMEM(kept.shape, f32)
    return call(
        functools.partial(fine_kernel, shape, layers, steps, last),
        (local, sub_inverse, sol) if last else (local, sub_inverse, sol, base, stiffness),
        (kept,) if last else (kept, kept),
        scratch=(
            pltpu.VMEM(local.shape, bf16),
            pltpu.VMEM((rows, width), bf16),
            pltpu.VMEM((width, columns), bf16),
        )
        + ((field, field) if last else (field, field, field))
        + (pltpu.SemaphoreType.DMA((steps + 5,)),),
        flops=2 * rows * width * columns,
        held=(0, 1, 2) if last else (0, 1, 2, 3),
    )


def coarse_values(arrived):
    chosen = arrived[0].astype(f32)
    for h in range(1, arrived.shape[0]):
        chosen = chosen + arrived[h].astype(f32)
    return chosen.astype(bf16)


def step_sides_kernel(
    shape,
    layers,
    arrived,
    basis_kept,
    sol_kept,
    base_kept,
    stiffness,
    first,
    second,
    coarse,
    basis_p,
    stiff,
    sol,
    begin,
    base,
    sems,
):
    cells_s, cells_q, _, pad, columns = shape
    sides = (0, cells_q - 1)
    copies = [begun(basis_kept, basis_p, sems.at[0]), begun(stiffness, stiff, sems.at[1])]
    for s in range(cells_s):
        for q in sides:
            i = s * cells_q + q
            copies.append(begun(sol_kept.at[i], sol.at[i], sems.at[len(copies)]))
            copies.append(begun(base_kept.at[i], begin.at[i], sems.at[len(copies)]))
    chosen = coarse_values(arrived)
    copies[0].wait()
    span = cells_q * pad
    for s in range(cells_s):
        rows = jnp.dot(
            basis_p[s * span : (s + 1) * span, :], chosen, preferred_element_type=f32
        )
        coarse[s * cells_q : (s + 1) * cells_q] = rows.reshape(cells_q, pad, columns)
    for copy in copies[1:]:
        copy.wait()
    for s in range(cells_s):
        for q in sides:
            i = s * cells_q + q
            sol[i] = sol[i] + coarse[i]
    write_base(layers, begin, stiff, coarse, base, shape, sides)
    write_column_messages(sol, base, first, second, shape)


def step_kernel(shape, layers, coarse, sol_kept, base_kept, stiffness, new, base, stiff, begin, sems):
    sources, targets = (stiffness, sol_kept, base_kept), (stiff, new, begin)
    copies = [begun(a, b, sems.at[k]) for k, (a, b) in enumerate(zip(sources, targets))]
    for copy in copies:
        copy.wait()
    for i in range(new.shape[0]):
        new[i] = new[i] + coarse[i]
    write_base(layers, begin, stiff, coarse, base, shape)


def close_kernel(
    shape, layers, arrived, basis_kept, sol_kept, out_kept, basis_p, sol, out, sems
):
    cells_s, cells_q, comps, pad, columns = shape
    span = cells_q * pad
    copies = [begun(basis_kept, basis_p, sems.at[0])]
    for s in range(cells_s):
        part = pl.ds(s * cells_q, cells_q)
        copies.append(begun(sol_kept.at[part], sol.at[part], sems.at[s + 1]))
    chosen = coarse_values(arrived)
    copies[0].wait()
    results = []
    for s in range(cells_s):
        rows = jnp.dot(
            basis_p[s * span : (s + 1) * span, :], chosen, preferred_element_type=f32
        )
        copies[s + 1].wait()
        for q in range(cells_q):
            total = sol[s * cells_q + q] + rows[q * pad : (q + 1) * pad]
            for c in range(comps):
                out[s, q, :, c, :] = total[c * layers : (c + 1) * layers]
        results.append(begun(out.at[s], out_kept.at[s], sems.at[cells_s + 1 + s]))
    for copy in results:
        copy.wait()


def places(offsets, g, j, groups, depth, kgroup):
    first = offsets[g, j]
    end = kgroup if j == groups - 1 else offsets[g, j + 1]
    shape = (1, groups * depth)
    at = lax.broadcasted_iota(jnp.int32, shape, 1)
    turn = at
    member = jnp.zeros(shape, jnp.int32)
    for m in range(1, groups):
        member = member + jnp.where(at >= m * depth, 1, 0)
        turn = turn - jnp.where(at >= m * depth, depth, 0)
    shifted = member - lax.rem(first, groups)
    shifted = jnp.where(shifted < 0, shifted + groups, shifted)
    place = shifted + turn * groups
    return first, place, place < end - first


def ordering(dims, offsets):
    groups, depth, kgroup, count = dims
    member = lax.axis_index(GROUP_AXES)
    wanted = jnp.full((1, groups * depth), -1, jnp.int32)
    for j in range(groups):
        _, place, valid = places(offsets, 0, j, groups, depth, kgroup)
        wanted = jnp.where(valid & (member == j), place, wanted)
    row = lax.broadcasted_iota(jnp.int32, (count, groups * depth), 0)
    return jnp.where(row == wanted, 1.0, 0.0).astype(bf16)


def basis_turned_kernel(cell, dims, offsets, basis_kept, basis_t, kept, basis, sems):
    wide, per_cell, pad = cell
    span, chunk = wide * per_cell, wide * pad
    copy = begun(basis_kept.at[0], basis, sems.at[0])
    pack = packing(wide, per_cell, pad)
    order = ordering(dims, offsets)
    copy.wait()
    for s in range(basis.shape[0] // span):
        ordered = jnp.dot(
            basis[s * span : (s + 1) * span, :], order, preferred_element_type=f32
        ).astype(bf16)
        basis_t[:, s * chunk : (s + 1) * chunk] = lax.dot_general(
            ordered, pack, (((0,), (0,)), ((), ())), preferred_element_type=f32
        ).astype(bf16)
    begun(basis_t, kept, sems.at[1]).wait()


def basis_own_kernel(cell, dims, offsets, basis_kept, own_kept, basis, basis_p, sems):
    wide, per_cell, pad = cell
    span = wide * per_cell
    size = (wide - 2) * pad
    copy = begun(basis_kept.at[0], basis, sems.at[0])
    pack = packing(wide, per_cell, pad, True)[pad : pad + size]
    order = ordering(dims, offsets)
    copy.wait()
    for s in range(basis_p.shape[0] // size):
        ordered = jnp.dot(
            basis[(s + 1) * span : (s + 2) * span, :], order, preferred_element_type=f32
        ).astype(bf16)
        basis_p[s * size : (s + 1) * size, :] = jnp.dot(
            pack, ordered, preferred_element_type=f32
        ).astype(bf16)
    begun(basis_p, own_kept, sems.at[1]).wait()


def ordered_basis(body, cell, dims, offsets, basis, shape, both):
    held = [] if both else [pltpu.VMEM(shape, bf16)]
    return pl.pallas_call(
        functools.partial(body, cell, dims),
        out_shape=([jax.ShapeDtypeStruct(shape, bf16)] if both else []) + [pltpu.HBM(shape, bf16)],
        in_specs=[pl.BlockSpec(memory_space=pltpu.SMEM), HBM],
        out_specs=([VMEM] if both else []) + [HBM],
        scratch_shapes=[pltpu.VMEM(basis.shape[1:], bf16), *held, pltpu.SemaphoreType.DMA((2,))],
        compiler_params=pltpu.CompilerParams(vmem_limit_bytes=12 << 20),
        cost_estimate=pl.CostEstimate(
            flops=4 * shape[0] * shape[1] * cell[0] * cell[2],
            bytes_accessed=4 * basis.size,
            transcendentals=0,
        ),
    )(offsets, pltpu.with_memory_space_constraint(basis, pltpu.HBM))


def spread_kernel(dims, every, inverse, out, columns):
    groups, depth, kgroup = dims
    g = pl.program_id(0)
    member = lax.axis_index(GROUP_AXES)

    @pl.when(g == 0)
    def _():
        own = lax.axis_index("sub")
        slot = lax.broadcasted_iota(jnp.int32, (kgroup, groups * depth), 0)
        for j in range(groups):
            first, place, valid = places(every, own, j, groups, depth, kgroup)
            wanted = jnp.where(valid, place + first, -1)
            columns[:, j * groups * depth : (j + 1) * groups * depth] = jnp.where(
                slot == wanted, 1.0, 0.0
            ).astype(bf16)

    rows = inverse.shape[1]
    turn = lax.broadcasted_iota(jnp.int32, (depth, rows), 0)
    index = lax.broadcasted_iota(jnp.int32, (depth, rows), 1)
    picks = []
    for j in range(groups):
        first = every[g, j]
        end = kgroup if j == groups - 1 else every[g, j + 1]
        begin = lax.div(first - member + groups - 1, groups)
        wanted = (index == turn + begin) & (index * groups + member < end)
        picks.append(jnp.where(wanted, 1.0, 0.0).astype(bf16))
    picked = jnp.dot(
        jnp.concatenate(picks, axis=0), inverse[0], preferred_element_type=f32
    ).astype(bf16)
    out[...] = jnp.dot(picked, columns[...], preferred_element_type=f32).astype(bf16)


def spread_inverse(every, coarse_inverse, depth):
    n_sub, share_rows, kgroup = coarse_inverse.shape
    groups = every.shape[1]
    coarse = groups * depth
    return pl.pallas_call(
        functools.partial(spread_kernel, (groups, depth, kgroup)),
        grid=(n_sub,),
        out_shape=pltpu.HBM((n_sub * coarse, groups * coarse), bf16),
        in_specs=[
            pl.BlockSpec(memory_space=pltpu.SMEM),
            pl.BlockSpec((1, share_rows, kgroup), lambda g: (g, 0, 0)),
        ],
        out_specs=pl.BlockSpec((coarse, groups * coarse), lambda g: (g, 0)),
        scratch_shapes=[pltpu.VMEM((kgroup, groups * coarse), bf16)],
        compiler_params=pltpu.CompilerParams(vmem_limit_bytes=10 << 20),
        cost_estimate=pl.CostEstimate(
            flops=2 * n_sub * coarse * groups * coarse * kgroup,
            bytes_accessed=4 * n_sub * coarse * groups * coarse,
            transcendentals=0,
        ),
    )(every, coarse_inverse)


def shards(rhs, start, stiffness, sub_inverse, basis, coarse_inverse, offsets):
    cells_s, cells_q, comps, layers, columns = rhs.shape
    n_sub, _, kgroup = coarse_inverse.shape
    groups = offsets.shape[1]
    depth = -(-basis.shape[2] // groups)
    coarse = groups * depth
    cells = cells_s * cells_q
    per_cell = comps * layers
    pad = -(-per_cell // 16) * 16
    wide = cells_q + 2
    shape = (cells_s, cells_q, comps, pad, columns)

    field = jax.ShapeDtypeStruct((cells, pad, columns), f32)
    column_message = jax.ShapeDtypeStruct((2, cells_s, pad, columns), bf16)
    row_message = jax.ShapeDtypeStruct((2, wide, pad, columns), bf16)

    rows = (cells_s + 2) * wide * pad

    start_cells, rhs_cells = (x.transpose(0, 1, 3, 2, 4) for x in (start, rhs))
    tail = (layers, comps, columns)
    first, second = call(
        functools.partial(open_sides_kernel, shape, layers),
        (start_cells, rhs_cells, stiffness),
        (column_message, column_message),
        scratch=(
            pltpu.VMEM((cells_s, 4) + tail, f32),
            pltpu.VMEM((cells_s, 2) + tail, f32),
            pltpu.VMEM(stiffness.shape, f32),
            pltpu.VMEM(field.shape, f32),
            pltpu.VMEM(field.shape, f32),
            pltpu.VMEM(field.shape, f32),
            pltpu.SemaphoreType.DMA((5,)),
        ),
        held=(0, 1, 2),
    )
    solution, base, sent = call(
        functools.partial(open_kernel, shape, layers),
        (start_cells, rhs_cells, stiffness, offsets),
        (field, field, jax.ShapeDtypeStruct((n_sub, groups), jnp.int32)),
        scratch=(
            pltpu.VMEM((cells_s, cells_q) + tail, f32),
            pltpu.VMEM((cells_s, cells_q) + tail, f32),
            pltpu.VMEM(stiffness.shape, f32),
            pltpu.VMEM(offsets.shape, jnp.int32),
            pltpu.VMEM(field.shape, f32),
            pltpu.SemaphoreType.DMA((4,)),
        ),
        held=(0, 1, 2, 3),
    )
    cell = (wide, per_cell, pad)
    dims = (groups, depth, kgroup, basis.shape[2])
    basis_t = basis_kept = basis_p = every = spread = None

    for sweep in range(ITERS):
        last = sweep == ITERS - 1
        first_q, second_q = swap(first, second, GROUP_AXES)
        if sweep == 0:
            every = sent
            rounds = (n_sub - 1).bit_length()
            for power in range(rounds - 1):
                every = doubled(every, 1 << power)
            first_q, second_q, every = lax.optimization_barrier((first_q, second_q, every))
        first, second = call(
            functools.partial(row_kernel, shape),
            (solution, base, first_q, second_q),
            (row_message, row_message),
        )
        first_s, second_s = swap(first, second, "sub")
        if sweep == 0:
            later, _ = lax.optimization_barrier((basis, first))
            basis_t, basis_kept = ordered_basis(
                basis_turned_kernel, cell, dims, offsets, later, (coarse, rows), True
            )
            every = doubled(every, 1 << (rounds - 1))
            first_s, second_s, every = lax.optimization_barrier((first_s, second_s, every))
        message, local = call(
            functools.partial(window_kernel, shape),
            (solution, base, first_q, second_q, first_s, second_s, basis_t if sweep == 0 else basis_kept),
            (
                pltpu.HBM((groups, coarse, columns), bf16),
                pltpu.HBM(((cells_s + 2) * wide, pad, columns), bf16),
            ),
            scratch=(
                pltpu.VMEM(((cells_s + 2) * wide, pad, columns), bf16),
                pltpu.VMEM((coarse, columns), bf16),
                pltpu.SemaphoreType.DMA((groups + 1,)),
            ),
            flops=2 * rows * coarse * columns,
        )
        if sweep == 0:
            later, _ = lax.optimization_barrier((basis, message))
            (basis_p,) = ordered_basis(
                basis_own_kernel, cell, dims, offsets, later, (cells * pad, coarse), False
            )
            waited, basis_p = lax.optimization_barrier((every, basis_p))
            spread = spread_inverse(waited, coarse_inverse, depth)
        gathered = lax.all_to_all(message, GROUP_AXES, 0, 0, tiled=True)
        held = pltpu.VMEM((spread.shape[0], columns), bf16)
        (terms,) = call(
            terms_kernel,
            (spread, gathered.reshape(-1, columns)),
            (pltpu.HBM(held.shape, bf16),),
            scratch=(held, pltpu.SemaphoreType.DMA),
            flops=2 * spread.size * columns,
        )
        arrived = lax.all_to_all(
            terms.reshape(n_sub * groups, depth, columns), ALL_AXES, 0, 0, tiled=True
        ).reshape(n_sub, coarse, columns)
        kept = fine_product(
            shape, layers, local, sub_inverse, solution, base, stiffness, last
        )
        if last:
            (out,) = call(
                functools.partial(close_kernel, shape, layers),
                (arrived, basis_p, *kept),
                (pltpu.HBM((cells_s, cells_q) + tail, f32),),
                scratch=(
                    pltpu.VMEM(basis_p.shape, bf16),
                    pltpu.VMEM(field.shape, f32),
                    pltpu.VMEM((cells_s, cells_q) + tail, f32),
                    pltpu.SemaphoreType.DMA((2 * cells_s + 1,)),
                ),
                held=(1, 2),
            )
        else:
            first, second, change = call(
                functools.partial(step_sides_kernel, shape, layers),
                (arrived, basis_p, *kept, stiffness),
                (column_message, column_message, field),
                scratch=(
                    pltpu.VMEM(basis_p.shape, bf16),
                    pltpu.VMEM(stiffness.shape, f32),
                    pltpu.VMEM(field.shape, f32),
                    pltpu.VMEM(field.shape, f32),
                    pltpu.VMEM(field.shape, f32),
                    pltpu.SemaphoreType.DMA((4 * cells_s + 2,)),
                ),
                held=(1, 2, 3, 4),
            )
            solution, base = call(
                functools.partial(step_kernel, shape, layers),
                (change, *kept, stiffness),
                (field, field),
                scratch=(
                    pltpu.VMEM(stiffness.shape, f32),
                    pltpu.VMEM(field.shape, f32),
                    pltpu.SemaphoreType.DMA((3,)),
                ),
                held=(1, 2, 3),
            )
    return out.transpose(0, 1, 3, 2, 4)


def solution(mesh):
    return jax.shard_map(
        shards,
        mesh=mesh,
        in_specs=(
            P("sub", ("crow", "ccol"), None, None, None),
            P("sub", ("crow", "ccol"), None, None, None),
            P("sub", ("crow", "ccol"), None, None),
            P(("sub", "crow", "ccol"), None, None),
            P(("sub", "crow", "ccol"), None, None),
            P(None, ("crow", "ccol"), "sub"),
            P("sub", None),
        ),
        out_specs=P("sub", ("crow", "ccol"), None, None, None),
        check_vma=False,
    )
```

```python
import functools
import math

import jax
import jax.numpy as jnp
from jax import lax
from jax.experimental import pallas as pl
from jax.experimental.pallas import tpu as pltpu
from jax.sharding import PartitionSpec as P

ITERS = 2
PARTNER = 2
GROUP_AXES = ("crow", "ccol")
ALL_AXES = ("sub", "crow", "ccol")
bf16, f32 = jnp.bfloat16, jnp.float32
VMEM = pl.BlockSpec(memory_space=pltpu.VMEM)
HBM = pl.BlockSpec(memory_space=pltpu.HBM)


def sized(x):
    return math.prod(x.shape) * jnp.dtype(x.dtype).itemsize


def call(body, ins, outs, scratch=(), flops=0, held=()):
    size = sum(sized(x) for x in (*ins, *outs))
    room = size + sum(sized(x) for x in scratch if getattr(x, "dtype", None) in (bf16, f32))
    return pl.pallas_call(
        body,
        out_shape=tuple(outs),
        in_specs=[HBM if i in held else VMEM for i in range(len(ins))],
        out_specs=tuple(
            HBM if getattr(x, "memory_space", None) == pltpu.HBM else VMEM for x in outs
        ),
        scratch_shapes=list(scratch),
        compiler_params=pltpu.CompilerParams(vmem_limit_bytes=room + (4 << 20)),
        cost_estimate=pl.CostEstimate(flops=flops, bytes_accessed=size, transcendentals=0),
    )(
        *[
            pltpu.with_memory_space_constraint(x, pltpu.HBM) if i in held else x
            for i, x in enumerate(ins)
        ]
    )


def begun(source, target, sem):
    copy = pltpu.make_async_copy(source, target, sem)
    copy.start()
    return copy


def packing(cells, per_cell, pad, turned=False):
    shape = (cells * per_cell, cells * pad)
    shape = shape[::-1] if turned else shape
    row = lax.broadcasted_iota(jnp.int32, shape, 1 if turned else 0)
    column = lax.broadcasted_iota(jnp.int32, shape, 0 if turned else 1)
    for w in range(1, cells):
        column = column - jnp.where(row >= w * per_cell, pad - per_cell, 0)
    return jnp.where(row == column, 1.0, 0.0).astype(bf16)


def swap(first, second, axis):
    count = lax.axis_size(axis)
    even = [(i, i + 1) for i in range(0, count - 1, 2)]
    odd = [(i, i + 1) for i in range(1, count - 1, 2)]
    return (
        lax.ppermute(first, axis, even + [(b, a) for a, b in even]),
        lax.ppermute(second, axis, odd + [(b, a) for a, b in odd]),
    )


def doubled(held, step):
    count = lax.axis_size("sub")
    return held + lax.ppermute(held, "sub", [(i, i ^ step) for i in range(count)])


def diagonal_of(stiffness, s, q, comps, layers, pad, columns):
    at = lax.broadcasted_iota(jnp.int32, (pad, layers), 0)
    layer = lax.broadcasted_iota(jnp.int32, (pad, layers), 1)
    column = jnp.zeros((pad, layers), f32)
    for c in range(comps):
        column = jnp.where(at == layer + c * layers, stiffness[s, q, c : c + 1, :], column)
    column = 6.0 + jnp.sum(column, axis=1, keepdims=True)
    return jnp.broadcast_to(column, (pad, columns))


def write_base(layers, begin, stiffness, field, base, shape, only=None):
    cells_s, cells_q, comps, pad, columns = shape
    at = lax.broadcasted_iota(jnp.int32, (pad, columns), 0)
    has_up, has_down = at < comps * layers, at < comps * layers
    for c in range(comps):
        has_up = has_up & (at != c * layers)
        has_down = has_down & (at != c * layers + layers - 1)
    for s in range(cells_s):
        for q in only or range(cells_q):
            i = s * cells_q + q
            x = field[i]
            diagonal = diagonal_of(stiffness, s, q, comps, layers, pad, columns)
            total = begin[i] - diagonal * x
            total = total + jnp.where(has_up, pltpu.roll(x, 1, 0), 0.0)
            total = total + jnp.where(has_down, pltpu.roll(x, pad - 1, 0), 0.0)
            if q > 0:
                total = total + field[i - 1]
            if q < cells_q - 1:
                total = total + field[i + 1]
            if s > 0:
                total = total + field[i - cells_q]
            if s < cells_s - 1:
                total = total + field[i + cells_q]
            base[i] = total


def write_column_messages(sol, base, first, second, shape):
    cells_s, cells_q = shape[:2]
    even = lax.axis_index(GROUP_AXES) % 2 == 0
    for out, q in (
        (first, jnp.where(even, cells_q - 1, 0)),
        (second, jnp.where(even, 0, cells_q - 1)),
    ):
        for s in range(cells_s):
            out[0, s] = base[s * cells_q + q].astype(bf16)
            out[1, s] = sol[s * cells_q + q].astype(bf16)


def unpack_cell(source, target, i, shape, layers):
    _, _, comps, pad, columns = shape
    for c in range(comps):
        target[i, c * layers : (c + 1) * layers, :] = source[:, c, :]
    target[i, comps * layers :, :] = jnp.zeros((pad - comps * layers, columns), f32)


def open_sides_kernel(
    shape, layers, start, rhs, stiffness, first, second, raw, raw_rhs, stiff, sol, begin, base, sems
):
    cells_s, cells_q = shape[:2]
    sides = (0, cells_q - 1)
    near = (0, 1, cells_q - 2, cells_q - 1)
    copies = [
        begun(stiffness, stiff, sems.at[0]),
        begun(start.at[:, pl.ds(0, 2)], raw.at[:, pl.ds(0, 2)], sems.at[1]),
        begun(start.at[:, pl.ds(cells_q - 2, 2)], raw.at[:, pl.ds(2, 2)], sems.at[2]),
        begun(rhs.at[:, pl.ds(0, 1)], raw_rhs.at[:, pl.ds(0, 1)], sems.at[3]),
        begun(rhs.at[:, pl.ds(cells_q - 1, 1)], raw_rhs.at[:, pl.ds(1, 1)], sems.at[4]),
    ]
    for copy in copies:
        copy.wait()
    for s in range(cells_s):
        for k, q in enumerate(near):
            unpack_cell(raw.at[s, k], sol, s * cells_q + q, shape, layers)
        for k, q in enumerate(sides):
            unpack_cell(raw_rhs.at[s, k], begin, s * cells_q + q, shape, layers)
    write_base(layers, begin, stiff, sol, base, shape, sides)
    write_column_messages(sol, base, first, second, shape)


def open_kernel(
    shape, layers, start, rhs, stiffness, offsets, sol, base, sent, raw, raw_rhs, stiff, own, begin, sems
):
    cells_s, cells_q = shape[:2]
    sources, targets = (stiffness, offsets, start, rhs), (stiff, own, raw, raw_rhs)
    copies = [begun(a, b, sems.at[k]) for k, (a, b) in enumerate(zip(sources, targets))]
    for copy in copies:
        copy.wait()
    group = lax.broadcasted_iota(jnp.int32, sent.shape, 0)
    sent[...] = jnp.where(group == lax.axis_index("sub"), own[...], 0)
    for s in range(cells_s):
        for q in range(cells_q):
            unpack_cell(raw.at[s, q], sol, s * cells_q + q, shape, layers)
            unpack_cell(raw_rhs.at[s, q], begin, s * cells_q + q, shape, layers)
    write_base(layers, begin, stiff, sol, base, shape)


def column_sides(first, second):
    even = lax.axis_index(GROUP_AXES) % 2 == 0

    def low(kind, s):
        return jnp.where(even, second[kind, s].astype(f32), first[kind, s].astype(f32))

    def high(kind, s):
        return jnp.where(even, first[kind, s].astype(f32), second[kind, s].astype(f32))

    return low, high


def edge_cells(low, high, sol, s, cells_q):
    col, cols = lax.axis_index(GROUP_AXES), lax.axis_size(GROUP_AXES)
    left = jnp.where(col > 0, low(0, s) + sol[s * cells_q], 0.0)
    right = jnp.where(col < cols - 1, high(0, s) + sol[s * cells_q + cells_q - 1], 0.0)
    return left, right


def row_kernel(shape, sol, base, first_in, second_in, first, second):
    cells_s, cells_q = shape[:2]
    low, high = column_sides(first_in, second_in)
    even = lax.axis_index("sub") % 2 == 0
    for out, s in (
        (first, jnp.where(even, cells_s - 1, 0)),
        (second, jnp.where(even, 0, cells_s - 1)),
    ):
        left, right = edge_cells(low, high, sol, s, cells_q)
        out[0, 0] = left.astype(bf16)
        out[0, cells_q + 1] = right.astype(bf16)
        low_s, high_s = low(1, s), high(1, s)
        out[1, 0] = low_s.astype(bf16)
        out[1, cells_q + 1] = high_s.astype(bf16)
        for q in range(cells_q):
            value = base[s * cells_q + q]
            if q == 0:
                value = value + low_s
            if q == cells_q - 1:
                value = value + high_s
            out[0, q + 1] = value.astype(bf16)
            out[1, q + 1] = sol[s * cells_q + q].astype(bf16)


def side_of(member):
    return (member // PARTNER) % 2


def window_kernel(
    shape,
    sol,
    base,
    first_q,
    second_q,
    first_s,
    second_s,
    basis_t,
    message,
    local_kept,
    local,
    restricted,
    sems,
):
    cells_s, cells_q, _, pad, columns = shape
    wide = cells_q + 2
    low, high = column_sides(first_q, second_q)
    row, rows = lax.axis_index("sub"), lax.axis_size("sub")
    even = row % 2 == 0

    def above(kind, w):
        return jnp.where(even, second_s[kind, w].astype(f32), first_s[kind, w].astype(f32))

    def below(kind, w):
        return jnp.where(even, first_s[kind, w].astype(f32), second_s[kind, w].astype(f32))

    for s in range(cells_s):
        left, right = edge_cells(low, high, sol, s, cells_q)
        values = [left] + [base[s * cells_q + q] for q in range(cells_q)] + [right]
        values[1] = values[1] + low(1, s)
        values[cells_q] = values[cells_q] + high(1, s)
        for w in range(wide):
            value = values[w]
            if s == 0:
                value = value + above(1, w)
            if s == cells_s - 1:
                value = value + below(1, w)
            local[(s + 1) * wide + w] = value.astype(bf16)
    for s, side, place, there in (
        (0, above, 0, row > 0),
        (cells_s - 1, below, (cells_s + 1) * wide, row < rows - 1),
    ):
        near = [low(1, s)] + [sol[s * cells_q + q] for q in range(cells_q)] + [high(1, s)]
        for w in range(wide):
            local[place + w] = jnp.where(there, side(0, w) + near[w], 0.0).astype(bf16)
    copies = [begun(local, local_kept, sems.at[0])]
    product = jnp.dot(
        basis_t[...], local[...].reshape(-1, columns), preferred_element_type=f32
    ).astype(bf16)
    half = columns // 2
    for k in range(2):
        restricted[k] = product[:, k * half : (k + 1) * half]
    for j in range(message.shape[0]):
        copies.append(begun(restricted.at[side_of(j)], message.at[j], sems.at[j + 1]))
    for copy in copies:
        copy.wait()


def terms_kernel(spread, gathered, out, kept, sem):
    kept[...] = jnp.dot(spread[...], gathered[...], preferred_element_type=f32).astype(bf16)
    begun(kept, out, sem).wait()


def fine_kernel(shape, layers, steps, last, local_kept, inverse_kept, sol_kept, *refs):
    cells_s, cells_q, comps, pad, columns = shape
    if last:
        out, local, inverse, packed, sol, fine, sems = refs
        fields = ((sol_kept, sol),)
    else:
        base_kept, stiffness, out, base_out, local, inverse, packed, sol, fine, base, sems = refs
        fields = ((sol_kept, sol), (base_kept, base))
    per_cell = comps * layers
    wide = cells_q + 2
    span, chunk = wide * per_cell, wide * pad
    size = cells_s // steps
    loaded = begun(local_kept, local, sems.at[0])
    arriving = [
        begun(
            inverse_kept.at[0, pl.ds((k * size + 1) * span, size * span)],
            inverse.at[pl.ds(k * size * span, size * span)],
            sems.at[k + 1],
        )
        for k in range(steps)
    ]
    others = [begun(a, b, sems.at[steps + 1 + k]) for k, (a, b) in enumerate(fields)]
    pack = packing(wide, per_cell, pad)
    loaded.wait()
    for s in range(packed.shape[0] // span):
        part = local[s * wide : (s + 1) * wide].reshape(chunk, columns)
        packed[s * span : (s + 1) * span, :] = jnp.dot(
            pack, part, preferred_element_type=f32
        ).astype(bf16)
    for k in range(steps):
        arriving[k].wait()
        rows = jnp.dot(
            inverse[k * size * span : (k + 1) * size * span, :],
            packed[...],
            preferred_element_type=f32,
        )
        for s in range(size):
            for q in range(cells_q):
                i = (k * size + s) * cells_q + q
                first = s * span + (q + 1) * per_cell
                fine[i, :per_cell, :] = rows[first : first + per_cell]
                fine[i, per_cell:, :] = jnp.zeros((pad - per_cell, columns), f32)
    for copy in others:
        copy.wait()
    for i in range(fine.shape[0]):
        sol[i] = sol[i] + fine[i]
    copies = [begun(sol, out, sems.at[steps + 3])]
    if not last:
        write_base(layers, base, stiffness, fine, base, shape)
        copies.append(begun(base, base_out, sems.at[steps + 4]))
    for copy in copies:
        copy.wait()


def fine_product(shape, layers, local, sub_inverse, sol, base, stiffness, last):
    cells_s, cells_q, comps, pad, columns = shape
    width = sub_inverse.shape[2]
    rows = cells_s * (cells_q + 2) * comps * layers
    steps = 3 if cells_s % 3 == 0 else 1
    kept = pltpu.HBM((cells_s * cells_q, pad, columns), f32)
    field = pltpu.VMEM(kept.shape, f32)
    return call(
        functools.partial(fine_kernel, shape, layers, steps, last),
        (local, sub_inverse, sol) if last else (local, sub_inverse, sol, base, stiffness),
        (kept,) if last else (kept, kept),
        scratch=(
            pltpu.VMEM(local.shape, bf16),
            pltpu.VMEM((rows, width), bf16),
            pltpu.VMEM((width, columns), bf16),
        )
        + ((field, field) if last else (field, field, field))
        + (pltpu.SemaphoreType.DMA((steps + 5,)),),
        flops=2 * rows * width * columns,
        held=(0, 1, 2) if last else (0, 1, 2, 3),
    )


def coarse_values(arrived, depth):
    sums = []
    for c in range(arrived.shape[1]):
        total = arrived[0, c].astype(f32)
        for h in range(1, arrived.shape[0]):
            total = total + arrived[h, c].astype(f32)
        sums.append(total)
    rows = []
    for m in range(arrived.shape[1]):
        part = slice(side_of(m) * depth, (side_of(m) + 1) * depth)
        low = m - side_of(m) * PARTNER
        rows.append(jnp.concatenate([sums[low][part], sums[low + PARTNER][part]], axis=1))
    return jnp.concatenate(rows, axis=0).astype(bf16)


def step_sides_kernel(
    shape,
    layers,
    arrived,
    basis_kept,
    sol_kept,
    base_kept,
    stiffness,
    first,
    second,
    coarse,
    basis_p,
    stiff,
    sol,
    begin,
    base,
    sems,
):
    cells_s, cells_q, _, pad, columns = shape
    sides = (0, cells_q - 1)
    copies = [begun(basis_kept, basis_p, sems.at[0]), begun(stiffness, stiff, sems.at[1])]
    for s in range(cells_s):
        for q in sides:
            i = s * cells_q + q
            copies.append(begun(sol_kept.at[i], sol.at[i], sems.at[len(copies)]))
            copies.append(begun(base_kept.at[i], begin.at[i], sems.at[len(copies)]))
    chosen = coarse_values(arrived, arrived.shape[2] // 2)
    copies[0].wait()
    span = cells_q * pad
    for s in range(cells_s):
        rows = jnp.dot(
            basis_p[s * span : (s + 1) * span, :], chosen, preferred_element_type=f32
        )
        coarse[s * cells_q : (s + 1) * cells_q] = rows.reshape(cells_q, pad, columns)
    for copy in copies[1:]:
        copy.wait()
    for s in range(cells_s):
        for q in sides:
            i = s * cells_q + q
            sol[i] = sol[i] + coarse[i]
    write_base(layers, begin, stiff, coarse, base, shape, sides)
    write_column_messages(sol, base, first, second, shape)


def step_kernel(shape, layers, coarse, sol_kept, base_kept, stiffness, new, base, stiff, begin, sems):
    sources, targets = (stiffness, sol_kept, base_kept), (stiff, new, begin)
    copies = [begun(a, b, sems.at[k]) for k, (a, b) in enumerate(zip(sources, targets))]
    for copy in copies:
        copy.wait()
    for i in range(new.shape[0]):
        new[i] = new[i] + coarse[i]
    write_base(layers, begin, stiff, coarse, base, shape)


def close_kernel(
    shape, layers, arrived, basis_kept, sol_kept, out_kept, basis_p, sol, out, sems
):
    cells_s, cells_q, comps, pad, columns = shape
    span = cells_q * pad
    copies = [begun(basis_kept, basis_p, sems.at[0])]
    for s in range(cells_s):
        part = pl.ds(s * cells_q, cells_q)
        copies.append(begun(sol_kept.at[part], sol.at[part], sems.at[s + 1]))
    chosen = coarse_values(arrived, arrived.shape[2] // 2)
    copies[0].wait()
    results = []
    for s in range(cells_s):
        rows = jnp.dot(
            basis_p[s * span : (s + 1) * span, :], chosen, preferred_element_type=f32
        )
        copies[s + 1].wait()
        for q in range(cells_q):
            total = sol[s * cells_q + q] + rows[q * pad : (q + 1) * pad]
            for c in range(comps):
                out[s, q, :, c, :] = total[c * layers : (c + 1) * layers]
        results.append(begun(out.at[s], out_kept.at[s], sems.at[cells_s + 1 + s]))
    for copy in results:
        copy.wait()


def places(offsets, g, j, groups, depth, kgroup):
    first = offsets[g, j]
    end = kgroup if j == groups - 1 else offsets[g, j + 1]
    shape = (1, groups * depth)
    at = lax.broadcasted_iota(jnp.int32, shape, 1)
    turn = at
    member = jnp.zeros(shape, jnp.int32)
    for m in range(1, groups):
        member = member + jnp.where(at >= m * depth, 1, 0)
        turn = turn - jnp.where(at >= m * depth, depth, 0)
    shifted = member - lax.rem(first, groups)
    shifted = jnp.where(shifted < 0, shifted + groups, shifted)
    place = shifted + turn * groups
    return first, place, place < end - first


def ordering(dims, offsets):
    groups, depth, kgroup, count = dims
    member = lax.axis_index(GROUP_AXES)
    wanted = jnp.full((1, groups * depth), -1, jnp.int32)
    for j in range(groups):
        _, place, valid = places(offsets, 0, j, groups, depth, kgroup)
        wanted = jnp.where(valid & (member == j), place, wanted)
    row = lax.broadcasted_iota(jnp.int32, (count, groups * depth), 0)
    return jnp.where(row == wanted, 1.0, 0.0).astype(bf16)


def basis_kernel(cell, dims, offsets, basis_kept, basis_t, turned_kept, own_kept, basis, own, sems):
    wide, per_cell, pad = cell
    span, chunk = wide * per_cell, wide * pad
    size = chunk - 2 * pad
    copy = begun(basis_kept.at[0], basis, sems.at[0])
    pack = packing(wide, per_cell, pad)
    pack_own = packing(wide, per_cell, pad, True)[pad : pad + size]
    order = ordering(dims, offsets)
    rows = basis.shape[0] // span
    copy.wait()
    for s in range(rows):
        ordered = jnp.dot(
            basis[s * span : (s + 1) * span, :], order, preferred_element_type=f32
        ).astype(bf16)
        basis_t[:, s * chunk : (s + 1) * chunk] = lax.dot_general(
            ordered, pack, (((0,), (0,)), ((), ())), preferred_element_type=f32
        ).astype(bf16)
        if 0 < s < rows - 1:
            own[(s - 1) * size : s * size, :] = jnp.dot(
                pack_own, ordered, preferred_element_type=f32
            ).astype(bf16)
    copies = [begun(basis_t, turned_kept, sems.at[1]), begun(own, own_kept, sems.at[2])]
    for copy in copies:
        copy.wait()


def ordered_basis(cell, dims, offsets, basis, turned, own):
    return pl.pallas_call(
        functools.partial(basis_kernel, cell, dims),
        out_shape=(jax.ShapeDtypeStruct(turned, bf16), pltpu.HBM(turned, bf16), pltpu.HBM(own, bf16)),
        in_specs=[pl.BlockSpec(memory_space=pltpu.SMEM), HBM],
        out_specs=(VMEM, HBM, HBM),
        scratch_shapes=[
            pltpu.VMEM(basis.shape[1:], bf16),
            pltpu.VMEM(own, bf16),
            pltpu.SemaphoreType.DMA((3,)),
        ],
        compiler_params=pltpu.CompilerParams(vmem_limit_bytes=12 << 20),
        cost_estimate=pl.CostEstimate(
            flops=6 * turned[0] * turned[1] * cell[0] * cell[2],
            bytes_accessed=6 * basis.size,
            transcendentals=0,
        ),
    )(offsets, pltpu.with_memory_space_constraint(basis, pltpu.HBM))


def first_index(first, member, groups):
    if groups & (groups - 1) == 0:
        return lax.shift_right_logical(first - member + groups - 1, groups.bit_length() - 1)
    return lax.div(first - member + groups - 1, groups)


def spread_kernel(dims, every, inverse_kept, partner_kept, out_kept, inverse, columns, picked, out, sems):
    groups, depth, kgroup = dims
    coarse = groups * depth
    member = lax.axis_index(GROUP_AXES)
    own = lax.axis_index("sub")
    side = side_of(member)
    copies = [
        begun(inverse_kept, inverse.at[side], sems.at[0]),
        begun(partner_kept, inverse.at[1 - side], sems.at[1]),
    ]
    slot = lax.broadcasted_iota(jnp.int32, (kgroup, coarse), 0)
    for j in range(groups):
        first, place, valid = places(every, own, j, groups, depth, kgroup)
        wanted = jnp.where(valid, place + first, -1)
        columns[:, j * coarse : (j + 1) * coarse] = jnp.where(slot == wanted, 1.0, 0.0).astype(bf16)
    _, n_sub, rows, _ = inverse.shape
    turn = lax.broadcasted_iota(jnp.int32, (depth, rows), 0)
    index = lax.broadcasted_iota(jnp.int32, (depth, rows), 1)
    for copy in copies:
        copy.wait()
    span = 2 * coarse
    steps = max(n_sub // 4, 1)
    size = n_sub // steps

    def some(k, _):
        for t in range(size):
            g = k * size + t
            for b in range(2):
                m = member + (b - side) * PARTNER
                picks = []
                for j in range(groups):
                    first = every[g, j]
                    end = kgroup if j == groups - 1 else every[g, j + 1]
                    begin = first_index(first, m, groups)
                    wanted = (index == turn + begin) & (index * groups + m < end)
                    picks.append(jnp.where(wanted, 1.0, 0.0).astype(bf16))
                part = jnp.dot(
                    jnp.concatenate(picks, axis=0), inverse[b, g], preferred_element_type=f32
                ).astype(bf16)
                for j in range(groups):
                    at = t * span + (2 * j + b) * depth
                    picked[at : at + depth, :] = part[j * depth : (j + 1) * depth]
        out[...] = jnp.dot(picked[...], columns[...], preferred_element_type=f32).astype(bf16)
        begun(out, out_kept.at[pl.ds(k * size * span, size * span)], sems.at[2]).wait()
        return 0

    lax.fori_loop(0, steps, some, 0)


def spread_inverse(every, coarse_inverse, partner, depth):
    n_sub, share_rows, kgroup = coarse_inverse.shape
    groups = every.shape[1]
    coarse = groups * depth
    rows = n_sub * 2 * coarse
    part = rows // max(n_sub // 4, 1)
    return pl.pallas_call(
        functools.partial(spread_kernel, (groups, depth, kgroup)),
        out_shape=pltpu.HBM((rows, groups * coarse), bf16),
        in_specs=[pl.BlockSpec(memory_space=pltpu.SMEM), HBM, HBM],
        out_specs=HBM,
        scratch_shapes=[
            pltpu.VMEM((2,) + coarse_inverse.shape, bf16),
            pltpu.VMEM((kgroup, groups * coarse), bf16),
            pltpu.VMEM((part, kgroup), bf16),
            pltpu.VMEM((part, groups * coarse), bf16),
            pltpu.SemaphoreType.DMA((3,)),
        ],
        compiler_params=pltpu.CompilerParams(
            vmem_limit_bytes=(16 << 20) + 4 * coarse_inverse.size + 8 * part * groups * coarse
        ),
        cost_estimate=pl.CostEstimate(
            flops=2 * rows * groups * coarse * kgroup,
            bytes_accessed=2 * rows * groups * coarse,
            transcendentals=0,
        ),
    )(
        every,
        pltpu.with_memory_space_constraint(coarse_inverse, pltpu.HBM),
        pltpu.with_memory_space_constraint(partner, pltpu.HBM),
    )


def shards(rhs, start, stiffness, sub_inverse, basis, coarse_inverse, offsets):
    cells_s, cells_q, comps, layers, columns = rhs.shape
    n_sub, _, kgroup = coarse_inverse.shape
    groups = offsets.shape[1]
    depth = -(-basis.shape[2] // groups)
    coarse = groups * depth
    cells = cells_s * cells_q
    per_cell = comps * layers
    pad = -(-per_cell // 16) * 16
    wide = cells_q + 2
    shape = (cells_s, cells_q, comps, pad, columns)

    field = jax.ShapeDtypeStruct((cells, pad, columns), f32)
    column_message = jax.ShapeDtypeStruct((2, cells_s, pad, columns), bf16)
    row_message = jax.ShapeDtypeStruct((2, wide, pad, columns), bf16)

    rows = (cells_s + 2) * wide * pad

    start_cells, rhs_cells = (x.transpose(0, 1, 3, 2, 4) for x in (start, rhs))
    tail = (layers, comps, columns)
    first, second = call(
        functools.partial(open_sides_kernel, shape, layers),
        (start_cells, rhs_cells, stiffness),
        (column_message, column_message),
        scratch=(
            pltpu.VMEM((cells_s, 4) + tail, f32),
            pltpu.VMEM((cells_s, 2) + tail, f32),
            pltpu.VMEM(stiffness.shape, f32),
            pltpu.VMEM(field.shape, f32),
            pltpu.VMEM(field.shape, f32),
            pltpu.VMEM(field.shape, f32),
            pltpu.SemaphoreType.DMA((5,)),
        ),
        held=(0, 1, 2),
    )
    solution, base, sent = call(
        functools.partial(open_kernel, shape, layers),
        (start_cells, rhs_cells, stiffness, offsets),
        (field, field, jax.ShapeDtypeStruct((n_sub, groups), jnp.int32)),
        scratch=(
            pltpu.VMEM((cells_s, cells_q) + tail, f32),
            pltpu.VMEM((cells_s, cells_q) + tail, f32),
            pltpu.VMEM(stiffness.shape, f32),
            pltpu.VMEM(offsets.shape, jnp.int32),
            pltpu.VMEM(field.shape, f32),
            pltpu.SemaphoreType.DMA((4,)),
        ),
        held=(0, 1, 2, 3),
    )
    cell = (wide, per_cell, pad)
    dims = (groups, depth, kgroup, basis.shape[2])
    basis_t = basis_kept = basis_p = every = spread = None

    for sweep in range(ITERS):
        last = sweep == ITERS - 1
        first_q, second_q = swap(first, second, GROUP_AXES)
        if sweep == 0:
            every = sent
            rounds = (n_sub - 1).bit_length()
            for power in range(rounds - 1):
                every = doubled(every, 1 << power)
            first_q, second_q, every = lax.optimization_barrier((first_q, second_q, every))
        first, second = call(
            functools.partial(row_kernel, shape),
            (solution, base, first_q, second_q),
            (row_message, row_message),
        )
        first_s, second_s = swap(first, second, "sub")
        if sweep == 0:
            later, _ = lax.optimization_barrier((basis, first))
            basis_t, basis_kept, basis_p = ordered_basis(
                cell, dims, offsets, later, (coarse, rows), (cells * pad, coarse)
            )
            shared, _ = lax.optimization_barrier((coarse_inverse, basis_t))
            pairs = [(i, i ^ PARTNER) for i in range(groups)]
            partner = lax.ppermute(shared, GROUP_AXES, pairs)
            every = doubled(every, 1 << (rounds - 1))
            first_s, second_s, every, partner = lax.optimization_barrier(
                (first_s, second_s, every, partner)
            )
        message, local = call(
            functools.partial(window_kernel, shape),
            (solution, base, first_q, second_q, first_s, second_s, basis_t if sweep == 0 else basis_kept),
            (
                pltpu.HBM((groups, coarse, columns // 2), bf16),
                pltpu.HBM(((cells_s + 2) * wide, pad, columns), bf16),
            ),
            scratch=(
                pltpu.VMEM(((cells_s + 2) * wide, pad, columns), bf16),
                pltpu.VMEM((2, coarse, columns // 2), bf16),
                pltpu.SemaphoreType.DMA((groups + 1,)),
            ),
            flops=2 * rows * coarse * columns,
        )
        if sweep == 0:
            waited, _ = lax.optimization_barrier((every, message))
            spread = spread_inverse(waited, coarse_inverse, partner, depth)
        gathered = lax.all_to_all(message, GROUP_AXES, 0, 0, tiled=True)
        held = pltpu.VMEM((spread.shape[0], columns // 2), bf16)
        (terms,) = call(
            terms_kernel,
            (spread, gathered.reshape(-1, columns // 2)),
            (pltpu.HBM(held.shape, bf16),),
            scratch=(held, pltpu.SemaphoreType.DMA),
            flops=2 * spread.size * columns // 2,
        )
        arrived = lax.all_to_all(
            terms.reshape(n_sub * groups, 2 * depth, columns // 2), ALL_AXES, 0, 0, tiled=True
        ).reshape(n_sub, groups, 2 * depth, columns // 2)
        kept = fine_product(
            shape, layers, local, sub_inverse, solution, base, stiffness, last
        )
        if last:
            (out,) = call(
                functools.partial(close_kernel, shape, layers),
                (arrived, basis_p, *kept),
                (pltpu.HBM((cells_s, cells_q) + tail, f32),),
                scratch=(
                    pltpu.VMEM(basis_p.shape, bf16),
                    pltpu.VMEM(field.shape, f32),
                    pltpu.VMEM((cells_s, cells_q) + tail, f32),
                    pltpu.SemaphoreType.DMA((2 * cells_s + 1,)),
                ),
                held=(1, 2),
            )
        else:
            first, second, change = call(
                functools.partial(step_sides_kernel, shape, layers),
                (arrived, basis_p, *kept, stiffness),
                (column_message, column_message, field),
                scratch=(
                    pltpu.VMEM(basis_p.shape, bf16),
                    pltpu.VMEM(stiffness.shape, f32),
                    pltpu.VMEM(field.shape, f32),
                    pltpu.VMEM(field.shape, f32),
                    pltpu.VMEM(field.shape, f32),
                    pltpu.SemaphoreType.DMA((4 * cells_s + 2,)),
                ),
                held=(1, 2, 3, 4),
            )
            solution, base = call(
                functools.partial(step_kernel, shape, layers),
                (change, *kept, stiffness),
                (field, field),
                scratch=(
                    pltpu.VMEM(stiffness.shape, f32),
                    pltpu.VMEM(field.shape, f32),
                    pltpu.SemaphoreType.DMA((3,)),
                ),
                held=(1, 2, 3),
            )
    return out.transpose(0, 1, 3, 2, 4)


def solution(mesh):
    return jax.shard_map(
        shards,
        mesh=mesh,
        in_specs=(
            P("sub", ("crow", "ccol"), None, None, None),
            P("sub", ("crow", "ccol"), None, None, None),
            P("sub", ("crow", "ccol"), None, None),
            P(("sub", "crow", "ccol"), None, None),
            P(("sub", "crow", "ccol"), None, None),
            P(None, ("crow", "ccol"), "sub"),
            P("sub", None),
        ),
        out_specs=P("sub", ("crow", "ccol"), None, None, None),
        check_vma=False,
    )
```

```python
import functools
import math

import jax
import jax.numpy as jnp
from jax import lax
from jax.experimental import pallas as pl
from jax.experimental.pallas import tpu as pltpu
from jax.sharding import PartitionSpec as P

ITERS = 2
PARTNER = 2
GROUP_AXES = ("crow", "ccol")
ALL_AXES = ("sub", "crow", "ccol")
bf16, f32 = jnp.bfloat16, jnp.float32
VMEM = pl.BlockSpec(memory_space=pltpu.VMEM)
HBM = pl.BlockSpec(memory_space=pltpu.HBM)


def sized(x):
    return math.prod(x.shape) * jnp.dtype(x.dtype).itemsize


def call(body, ins, outs, scratch=(), flops=0, held=()):
    size = sum(sized(x) for x in (*ins, *outs))
    room = size + sum(sized(x) for x in scratch if getattr(x, "dtype", None) in (bf16, f32))
    return pl.pallas_call(
        body,
        out_shape=tuple(outs),
        in_specs=[HBM if i in held else VMEM for i in range(len(ins))],
        out_specs=tuple(
            HBM if getattr(x, "memory_space", None) == pltpu.HBM else VMEM for x in outs
        ),
        scratch_shapes=list(scratch),
        compiler_params=pltpu.CompilerParams(vmem_limit_bytes=room + (4 << 20)),
        cost_estimate=pl.CostEstimate(flops=flops, bytes_accessed=size, transcendentals=0),
    )(
        *[
            pltpu.with_memory_space_constraint(x, pltpu.HBM) if i in held else x
            for i, x in enumerate(ins)
        ]
    )


def begun(source, target, sem):
    copy = pltpu.make_async_copy(source, target, sem)
    copy.start()
    return copy


def packing(cells, per_cell, pad, turned=False):
    shape = (cells * per_cell, cells * pad)
    shape = shape[::-1] if turned else shape
    row = lax.broadcasted_iota(jnp.int32, shape, 1 if turned else 0)
    column = lax.broadcasted_iota(jnp.int32, shape, 0 if turned else 1)
    for w in range(1, cells):
        column = column - jnp.where(row >= w * per_cell, pad - per_cell, 0)
    return jnp.where(row == column, 1.0, 0.0).astype(bf16)


def swap(first, second, axis):
    count = lax.axis_size(axis)
    even = [(i, i + 1) for i in range(0, count - 1, 2)]
    odd = [(i, i + 1) for i in range(1, count - 1, 2)]
    return (
        lax.ppermute(first, axis, even + [(b, a) for a, b in even]),
        lax.ppermute(second, axis, odd + [(b, a) for a, b in odd]),
    )


def doubled(held, step):
    count = lax.axis_size("sub")
    return held + lax.ppermute(held, "sub", [(i, i ^ step) for i in range(count)])


def diagonal_of(stiffness, s, q, comps, layers, pad, columns):
    at = lax.broadcasted_iota(jnp.int32, (pad, layers), 0)
    layer = lax.broadcasted_iota(jnp.int32, (pad, layers), 1)
    column = jnp.zeros((pad, layers), f32)
    for c in range(comps):
        column = jnp.where(at == layer + c * layers, stiffness[s, q, c : c + 1, :], column)
    column = 6.0 + jnp.sum(column, axis=1, keepdims=True)
    return jnp.broadcast_to(column, (pad, columns))


def write_base(layers, begin, stiffness, field, base, shape, only=None):
    cells_s, cells_q, comps, pad, columns = shape
    at = lax.broadcasted_iota(jnp.int32, (pad, columns), 0)
    has_up, has_down = at < comps * layers, at < comps * layers
    for c in range(comps):
        has_up = has_up & (at != c * layers)
        has_down = has_down & (at != c * layers + layers - 1)
    for s in range(cells_s):
        for q in only or range(cells_q):
            i = s * cells_q + q
            x = field[i]
            diagonal = diagonal_of(stiffness, s, q, comps, layers, pad, columns)
            total = begin[i] - diagonal * x
            total = total + jnp.where(has_up, pltpu.roll(x, 1, 0), 0.0)
            total = total + jnp.where(has_down, pltpu.roll(x, pad - 1, 0), 0.0)
            if q > 0:
                total = total + field[i - 1]
            if q < cells_q - 1:
                total = total + field[i + 1]
            if s > 0:
                total = total + field[i - cells_q]
            if s < cells_s - 1:
                total = total + field[i + cells_q]
            base[i] = total


def write_column_messages(sol, base, first, second, shape):
    cells_s, cells_q = shape[:2]
    even = lax.axis_index(GROUP_AXES) % 2 == 0
    for out, q in (
        (first, jnp.where(even, cells_q - 1, 0)),
        (second, jnp.where(even, 0, cells_q - 1)),
    ):
        for s in range(cells_s):
            out[0, s] = base[s * cells_q + q].astype(bf16)
            out[1, s] = sol[s * cells_q + q].astype(bf16)


def unpack_cell(source, target, i, shape, layers):
    _, _, comps, pad, columns = shape
    for c in range(comps):
        target[i, c * layers : (c + 1) * layers, :] = source[:, c, :]
    target[i, comps * layers :, :] = jnp.zeros((pad - comps * layers, columns), f32)


def open_sides_kernel(
    shape, layers, start, rhs, stiffness, first, second, raw, raw_rhs, stiff, sol, begin, base, sems
):
    cells_s, cells_q = shape[:2]
    sides = (0, cells_q - 1)
    near = (0, 1, cells_q - 2, cells_q - 1)
    copies = [
        begun(stiffness, stiff, sems.at[0]),
        begun(start.at[:, pl.ds(0, 2)], raw.at[:, pl.ds(0, 2)], sems.at[1]),
        begun(start.at[:, pl.ds(cells_q - 2, 2)], raw.at[:, pl.ds(2, 2)], sems.at[2]),
        begun(rhs.at[:, pl.ds(0, 1)], raw_rhs.at[:, pl.ds(0, 1)], sems.at[3]),
        begun(rhs.at[:, pl.ds(cells_q - 1, 1)], raw_rhs.at[:, pl.ds(1, 1)], sems.at[4]),
    ]
    for copy in copies:
        copy.wait()
    for s in range(cells_s):
        for k, q in enumerate(near):
            unpack_cell(raw.at[s, k], sol, s * cells_q + q, shape, layers)
        for k, q in enumerate(sides):
            unpack_cell(raw_rhs.at[s, k], begin, s * cells_q + q, shape, layers)
    write_base(layers, begin, stiff, sol, base, shape, sides)
    write_column_messages(sol, base, first, second, shape)


def open_kernel(
    shape, layers, start, rhs, stiffness, offsets, sol, base, sent, raw, raw_rhs, stiff, own, begin, sems
):
    cells_s, cells_q = shape[:2]
    sources, targets = (stiffness, offsets, start, rhs), (stiff, own, raw, raw_rhs)
    copies = [begun(a, b, sems.at[k]) for k, (a, b) in enumerate(zip(sources, targets))]
    for copy in copies:
        copy.wait()
    group = lax.broadcasted_iota(jnp.int32, sent.shape, 0)
    sent[...] = jnp.where(group == lax.axis_index("sub"), own[...], 0)
    for s in range(cells_s):
        for q in range(cells_q):
            unpack_cell(raw.at[s, q], sol, s * cells_q + q, shape, layers)
            unpack_cell(raw_rhs.at[s, q], begin, s * cells_q + q, shape, layers)
    write_base(layers, begin, stiff, sol, base, shape)


def column_sides(first, second):
    even = lax.axis_index(GROUP_AXES) % 2 == 0

    def low(kind, s):
        return jnp.where(even, second[kind, s].astype(f32), first[kind, s].astype(f32))

    def high(kind, s):
        return jnp.where(even, first[kind, s].astype(f32), second[kind, s].astype(f32))

    return low, high


def edge_cells(low, high, sol, s, cells_q):
    col, cols = lax.axis_index(GROUP_AXES), lax.axis_size(GROUP_AXES)
    left = jnp.where(col > 0, low(0, s) + sol[s * cells_q], 0.0)
    right = jnp.where(col < cols - 1, high(0, s) + sol[s * cells_q + cells_q - 1], 0.0)
    return left, right


def row_kernel(shape, sol, base, first_in, second_in, first, second):
    cells_s, cells_q = shape[:2]
    low, high = column_sides(first_in, second_in)
    even = lax.axis_index("sub") % 2 == 0
    for out, s in (
        (first, jnp.where(even, cells_s - 1, 0)),
        (second, jnp.where(even, 0, cells_s - 1)),
    ):
        left, right = edge_cells(low, high, sol, s, cells_q)
        out[0, 0] = left.astype(bf16)
        out[0, cells_q + 1] = right.astype(bf16)
        low_s, high_s = low(1, s), high(1, s)
        out[1, 0] = low_s.astype(bf16)
        out[1, cells_q + 1] = high_s.astype(bf16)
        for q in range(cells_q):
            value = base[s * cells_q + q]
            if q == 0:
                value = value + low_s
            if q == cells_q - 1:
                value = value + high_s
            out[0, q + 1] = value.astype(bf16)
            out[1, q + 1] = sol[s * cells_q + q].astype(bf16)


def side_of(member):
    return (member // PARTNER) % 2


def window_kernel(
    shape,
    sol,
    base,
    first_q,
    second_q,
    first_s,
    second_s,
    basis_t,
    message,
    local_kept,
    local,
    restricted,
    sems,
):
    cells_s, cells_q, _, pad, columns = shape
    wide = cells_q + 2
    low, high = column_sides(first_q, second_q)
    row, rows = lax.axis_index("sub"), lax.axis_size("sub")
    even = row % 2 == 0

    def above(kind, w):
        return jnp.where(even, second_s[kind, w].astype(f32), first_s[kind, w].astype(f32))

    def below(kind, w):
        return jnp.where(even, first_s[kind, w].astype(f32), second_s[kind, w].astype(f32))

    copies = []
    for s in range(cells_s):
        left, right = edge_cells(low, high, sol, s, cells_q)
        values = [left] + [base[s * cells_q + q] for q in range(cells_q)] + [right]
        values[1] = values[1] + low(1, s)
        values[cells_q] = values[cells_q] + high(1, s)
        for w in range(wide):
            value = values[w]
            if s == 0:
                value = value + above(1, w)
            if s == cells_s - 1:
                value = value + below(1, w)
            local[(s + 1) * wide + w] = value.astype(bf16)
        part = pl.ds((s + 1) * wide, wide)
        copies.append(begun(local.at[part], local_kept.at[part], sems.at[len(copies)]))
    for s, side, place, there in (
        (0, above, 0, row > 0),
        (cells_s - 1, below, (cells_s + 1) * wide, row < rows - 1),
    ):
        near = [low(1, s)] + [sol[s * cells_q + q] for q in range(cells_q)] + [high(1, s)]
        for w in range(wide):
            local[place + w] = jnp.where(there, side(0, w) + near[w], 0.0).astype(bf16)
        part = pl.ds(place, wide)
        copies.append(begun(local.at[part], local_kept.at[part], sems.at[len(copies)]))
    product = jnp.dot(
        basis_t[...], local[...].reshape(-1, columns), preferred_element_type=f32
    ).astype(bf16)
    half = columns // 2
    for k in range(2):
        restricted[k] = product[:, k * half : (k + 1) * half]
    for j in range(message.shape[0]):
        copies.append(begun(restricted.at[side_of(j)], message.at[j], sems.at[len(copies)]))
    for copy in copies:
        copy.wait()


def terms_kernel(spread, gathered, out, kept, sem):
    kept[...] = jnp.dot(spread[...], gathered[...], preferred_element_type=f32).astype(bf16)
    begun(kept, out, sem).wait()


def fine_kernel(shape, layers, steps, last, local_kept, inverse_kept, sol_kept, *refs):
    cells_s, cells_q, comps, pad, columns = shape
    if last:
        out, local, inverse, packed, sol, fine, sems = refs
        fields = ((sol_kept, sol),)
    else:
        base_kept, stiffness, out, base_out, local, inverse, packed, sol, fine, base, sems = refs
        fields = ((sol_kept, sol), (base_kept, base))
    per_cell = comps * layers
    wide = cells_q + 2
    span, chunk = wide * per_cell, wide * pad
    size = cells_s // steps
    loaded = begun(local_kept, local, sems.at[0])
    arriving = [
        begun(
            inverse_kept.at[0, pl.ds((k * size + 1) * span, size * span)],
            inverse.at[pl.ds(k * size * span, size * span)],
            sems.at[k + 1],
        )
        for k in range(steps)
    ]
    others = [begun(a, b, sems.at[steps + 1 + k]) for k, (a, b) in enumerate(fields)]
    pack = packing(wide, per_cell, pad)
    loaded.wait()
    for s in range(packed.shape[0] // span):
        part = local[s * wide : (s + 1) * wide].reshape(chunk, columns)
        packed[s * span : (s + 1) * span, :] = jnp.dot(
            pack, part, preferred_element_type=f32
        ).astype(bf16)
    for k in range(steps):
        arriving[k].wait()
        rows = jnp.dot(
            inverse[k * size * span : (k + 1) * size * span, :],
            packed[...],
            preferred_element_type=f32,
        )
        for s in range(size):
            for q in range(cells_q):
                i = (k * size + s) * cells_q + q
                first = s * span + (q + 1) * per_cell
                fine[i, :per_cell, :] = rows[first : first + per_cell]
                fine[i, per_cell:, :] = jnp.zeros((pad - per_cell, columns), f32)
    for copy in others:
        copy.wait()
    for i in range(fine.shape[0]):
        sol[i] = sol[i] + fine[i]
    copies = [begun(sol, out, sems.at[steps + 3])]
    if not last:
        write_base(layers, base, stiffness, fine, base, shape)
        copies.append(begun(base, base_out, sems.at[steps + 4]))
    for copy in copies:
        copy.wait()


def fine_product(shape, layers, local, sub_inverse, sol, base, stiffness, last):
    cells_s, cells_q, comps, pad, columns = shape
    width = sub_inverse.shape[2]
    rows = cells_s * (cells_q + 2) * comps * layers
    steps = 3 if cells_s % 3 == 0 else 1
    kept = pltpu.HBM((cells_s * cells_q, pad, columns), f32)
    field = pltpu.VMEM(kept.shape, f32)
    return call(
        functools.partial(fine_kernel, shape, layers, steps, last),
        (local, sub_inverse, sol) if last else (local, sub_inverse, sol, base, stiffness),
        (kept,) if last else (kept, kept),
        scratch=(
            pltpu.VMEM(local.shape, bf16),
            pltpu.VMEM((rows, width), bf16),
            pltpu.VMEM((width, columns), bf16),
        )
        + ((field, field) if last else (field, field, field))
        + (pltpu.SemaphoreType.DMA((steps + 5,)),),
        flops=2 * rows * width * columns,
        held=(0, 1, 2) if last else (0, 1, 2, 3),
    )


def coarse_values(arrived, depth):
    sums = []
    for c in range(arrived.shape[1]):
        total = arrived[0, c].astype(f32)
        for h in range(1, arrived.shape[0]):
            total = total + arrived[h, c].astype(f32)
        sums.append(total)
    rows = []
    for m in range(arrived.shape[1]):
        part = slice(side_of(m) * depth, (side_of(m) + 1) * depth)
        low = m - side_of(m) * PARTNER
        rows.append(jnp.concatenate([sums[low][part], sums[low + PARTNER][part]], axis=1))
    return jnp.concatenate(rows, axis=0).astype(bf16)


def step_sides_kernel(
    shape,
    layers,
    arrived,
    basis_kept,
    sol_kept,
    base_kept,
    stiffness,
    first,
    second,
    coarse,
    basis_p,
    stiff,
    sol,
    begin,
    base,
    sems,
):
    cells_s, cells_q, _, pad, columns = shape
    sides = (0, cells_q - 1)
    copies = [begun(basis_kept, basis_p, sems.at[0]), begun(stiffness, stiff, sems.at[1])]
    for q in sides:
        copies.append(begun(sol_kept.at[:, q], sol.at[:, q], sems.at[len(copies)]))
        copies.append(begun(base_kept.at[:, q], begin.at[:, q], sems.at[len(copies)]))
    sol, begin = (x.reshape(cells_s * cells_q, pad, columns) for x in (sol, begin))
    chosen = coarse_values(arrived, arrived.shape[2] // 2)
    copies[0].wait()
    span = cells_q * pad
    for s in range(cells_s):
        rows = jnp.dot(
            basis_p[s * span : (s + 1) * span, :], chosen, preferred_element_type=f32
        )
        coarse[s * cells_q : (s + 1) * cells_q] = rows.reshape(cells_q, pad, columns)
    for copy in copies[1:]:
        copy.wait()
    for s in range(cells_s):
        for q in sides:
            i = s * cells_q + q
            sol[i] = sol[i] + coarse[i]
    write_base(layers, begin, stiff, coarse, base, shape, sides)
    write_column_messages(sol, base, first, second, shape)


def step_kernel(shape, layers, coarse, sol_kept, base_kept, stiffness, new, base, stiff, begin, sems):
    sources, targets = (stiffness, sol_kept, base_kept), (stiff, new, begin)
    copies = [begun(a, b, sems.at[k]) for k, (a, b) in enumerate(zip(sources, targets))]
    for copy in copies:
        copy.wait()
    for i in range(new.shape[0]):
        new[i] = new[i] + coarse[i]
    write_base(layers, begin, stiff, coarse, base, shape)


def close_kernel(
    shape, layers, arrived, basis_kept, sol_kept, out_kept, basis_p, sol, out, sems
):
    cells_s, cells_q, comps, pad, columns = shape
    span = cells_q * pad
    copies = [begun(basis_kept, basis_p, sems.at[0])]
    for s in range(cells_s):
        part = pl.ds(s * cells_q, cells_q)
        copies.append(begun(sol_kept.at[part], sol.at[part], sems.at[s + 1]))
    chosen = coarse_values(arrived, arrived.shape[2] // 2)
    copies[0].wait()
    results = []
    for s in range(cells_s):
        rows = jnp.dot(
            basis_p[s * span : (s + 1) * span, :], chosen, preferred_element_type=f32
        )
        copies[s + 1].wait()
        for q in range(cells_q):
            total = sol[s * cells_q + q] + rows[q * pad : (q + 1) * pad]
            for c in range(comps):
                out[s, q, :, c, :] = total[c * layers : (c + 1) * layers]
        results.append(begun(out.at[s], out_kept.at[s], sems.at[cells_s + 1 + s]))
    for copy in results:
        copy.wait()


def places(offsets, g, j, groups, depth, kgroup):
    first = offsets[g, j]
    end = kgroup if j == groups - 1 else offsets[g, j + 1]
    shape = (1, groups * depth)
    at = lax.broadcasted_iota(jnp.int32, shape, 1)
    turn = at
    member = jnp.zeros(shape, jnp.int32)
    for m in range(1, groups):
        member = member + jnp.where(at >= m * depth, 1, 0)
        turn = turn - jnp.where(at >= m * depth, depth, 0)
    shifted = member - lax.rem(first, groups)
    shifted = jnp.where(shifted < 0, shifted + groups, shifted)
    place = shifted + turn * groups
    return first, place, place < end - first


def ordering(dims, offsets):
    groups, depth, kgroup, count = dims
    member = lax.axis_index(GROUP_AXES)
    wanted = jnp.full((1, groups * depth), -1, jnp.int32)
    for j in range(groups):
        _, place, valid = places(offsets, 0, j, groups, depth, kgroup)
        wanted = jnp.where(valid & (member == j), place, wanted)
    row = lax.broadcasted_iota(jnp.int32, (count, groups * depth), 0)
    return jnp.where(row == wanted, 1.0, 0.0).astype(bf16)


def basis_kernel(cell, dims, offsets, basis_kept, basis_t, turned_kept, own_kept, basis, own, sems):
    wide, per_cell, pad = cell
    span, chunk = wide * per_cell, wide * pad
    size = chunk - 2 * pad
    copy = begun(basis_kept.at[0], basis, sems.at[0])
    pack = packing(wide, per_cell, pad)
    pack_own = packing(wide, per_cell, pad, True)[pad : pad + size]
    order = ordering(dims, offsets)
    rows = basis.shape[0] // span
    copy.wait()
    for s in range(rows):
        ordered = jnp.dot(
            basis[s * span : (s + 1) * span, :], order, preferred_element_type=f32
        ).astype(bf16)
        basis_t[:, s * chunk : (s + 1) * chunk] = lax.dot_general(
            ordered, pack, (((0,), (0,)), ((), ())), preferred_element_type=f32
        ).astype(bf16)
        if 0 < s < rows - 1:
            own[(s - 1) * size : s * size, :] = jnp.dot(
                pack_own, ordered, preferred_element_type=f32
            ).astype(bf16)
    copies = [begun(basis_t, turned_kept, sems.at[1]), begun(own, own_kept, sems.at[2])]
    for copy in copies:
        copy.wait()


def ordered_basis(cell, dims, offsets, basis, turned, own):
    return pl.pallas_call(
        functools.partial(basis_kernel, cell, dims),
        out_shape=(jax.ShapeDtypeStruct(turned, bf16), pltpu.HBM(turned, bf16), pltpu.HBM(own, bf16)),
        in_specs=[pl.BlockSpec(memory_space=pltpu.SMEM), HBM],
        out_specs=(VMEM, HBM, HBM),
        scratch_shapes=[
            pltpu.VMEM(basis.shape[1:], bf16),
            pltpu.VMEM(own, bf16),
            pltpu.SemaphoreType.DMA((3,)),
        ],
        compiler_params=pltpu.CompilerParams(vmem_limit_bytes=12 << 20),
        cost_estimate=pl.CostEstimate(
            flops=6 * turned[0] * turned[1] * cell[0] * cell[2],
            bytes_accessed=6 * basis.size,
            transcendentals=0,
        ),
    )(offsets, pltpu.with_memory_space_constraint(basis, pltpu.HBM))


def first_index(first, member, groups):
    if groups & (groups - 1) == 0:
        return lax.shift_right_logical(first - member + groups - 1, groups.bit_length() - 1)
    return lax.div(first - member + groups - 1, groups)


def spread_kernel(dims, every, inverse_kept, partner_kept, out_kept, inverse, columns, picked, out, sems):
    groups, depth, kgroup = dims
    coarse = groups * depth
    member = lax.axis_index(GROUP_AXES)
    own = lax.axis_index("sub")
    side = side_of(member)
    copies = [
        begun(inverse_kept, inverse.at[side], sems.at[0]),
        begun(partner_kept, inverse.at[1 - side], sems.at[1]),
    ]
    slot = lax.broadcasted_iota(jnp.int32, (kgroup, coarse), 0)
    for j in range(groups):
        first, place, valid = places(every, own, j, groups, depth, kgroup)
        wanted = jnp.where(valid, place + first, -1)
        columns[:, j * coarse : (j + 1) * coarse] = jnp.where(slot == wanted, 1.0, 0.0).astype(bf16)
    _, n_sub, rows, _ = inverse.shape
    turn = lax.broadcasted_iota(jnp.int32, (depth, rows), 0)
    index = lax.broadcasted_iota(jnp.int32, (depth, rows), 1)
    for copy in copies:
        copy.wait()
    span = 2 * coarse
    steps = max(n_sub // 4, 1)
    size = n_sub // steps

    def some(k, _):
        for t in range(size):
            g = k * size + t
            for b in range(2):
                m = member + (b - side) * PARTNER
                picks = []
                for j in range(groups):
                    first = every[g, j]
                    end = kgroup if j == groups - 1 else every[g, j + 1]
                    begin = first_index(first, m, groups)
                    wanted = (index == turn + begin) & (index * groups + m < end)
                    picks.append(jnp.where(wanted, 1.0, 0.0).astype(bf16))
                part = jnp.dot(
                    jnp.concatenate(picks, axis=0), inverse[b, g], preferred_element_type=f32
                ).astype(bf16)
                for j in range(groups):
                    at = t * span + (2 * j + b) * depth
                    picked[at : at + depth, :] = part[j * depth : (j + 1) * depth]
        out[...] = jnp.dot(picked[...], columns[...], preferred_element_type=f32).astype(bf16)
        begun(out, out_kept.at[pl.ds(k * size * span, size * span)], sems.at[2]).wait()
        return 0

    lax.fori_loop(0, steps, some, 0)


def spread_inverse(every, coarse_inverse, partner, depth):
    n_sub, share_rows, kgroup = coarse_inverse.shape
    groups = every.shape[1]
    coarse = groups * depth
    rows = n_sub * 2 * coarse
    part = rows // max(n_sub // 4, 1)
    return pl.pallas_call(
        functools.partial(spread_kernel, (groups, depth, kgroup)),
        out_shape=pltpu.HBM((rows, groups * coarse), bf16),
        in_specs=[pl.BlockSpec(memory_space=pltpu.SMEM), HBM, HBM],
        out_specs=HBM,
        scratch_shapes=[
            pltpu.VMEM((2,) + coarse_inverse.shape, bf16),
            pltpu.VMEM((kgroup, groups * coarse), bf16),
            pltpu.VMEM((part, kgroup), bf16),
            pltpu.VMEM((part, groups * coarse), bf16),
            pltpu.SemaphoreType.DMA((3,)),
        ],
        compiler_params=pltpu.CompilerParams(
            vmem_limit_bytes=(16 << 20) + 4 * coarse_inverse.size + 8 * part * groups * coarse
        ),
        cost_estimate=pl.CostEstimate(
            flops=2 * rows * groups * coarse * kgroup,
            bytes_accessed=2 * rows * groups * coarse,
            transcendentals=0,
        ),
    )(
        every,
        pltpu.with_memory_space_constraint(coarse_inverse, pltpu.HBM),
        pltpu.with_memory_space_constraint(partner, pltpu.HBM),
    )


def shards(rhs, start, stiffness, sub_inverse, basis, coarse_inverse, offsets):
    cells_s, cells_q, comps, layers, columns = rhs.shape
    n_sub, _, kgroup = coarse_inverse.shape
    groups = offsets.shape[1]
    depth = -(-basis.shape[2] // groups)
    coarse = groups * depth
    cells = cells_s * cells_q
    per_cell = comps * layers
    pad = -(-per_cell // 16) * 16
    wide = cells_q + 2
    shape = (cells_s, cells_q, comps, pad, columns)

    field = jax.ShapeDtypeStruct((cells, pad, columns), f32)
    column_message = jax.ShapeDtypeStruct((2, cells_s, pad, columns), bf16)
    row_message = jax.ShapeDtypeStruct((2, wide, pad, columns), bf16)

    rows = (cells_s + 2) * wide * pad

    start_cells, rhs_cells = (x.transpose(0, 1, 3, 2, 4) for x in (start, rhs))
    tail = (layers, comps, columns)
    first, second = call(
        functools.partial(open_sides_kernel, shape, layers),
        (start_cells, rhs_cells, stiffness),
        (column_message, column_message),
        scratch=(
            pltpu.VMEM((cells_s, 4) + tail, f32),
            pltpu.VMEM((cells_s, 2) + tail, f32),
            pltpu.VMEM(stiffness.shape, f32),
            pltpu.VMEM(field.shape, f32),
            pltpu.VMEM(field.shape, f32),
            pltpu.VMEM(field.shape, f32),
            pltpu.SemaphoreType.DMA((5,)),
        ),
        held=(0, 1, 2),
    )
    solution, base, sent = call(
        functools.partial(open_kernel, shape, layers),
        (start_cells, rhs_cells, stiffness, offsets),
        (field, field, jax.ShapeDtypeStruct((n_sub, groups), jnp.int32)),
        scratch=(
            pltpu.VMEM((cells_s, cells_q) + tail, f32),
            pltpu.VMEM((cells_s, cells_q) + tail, f32),
            pltpu.VMEM(stiffness.shape, f32),
            pltpu.VMEM(offsets.shape, jnp.int32),
            pltpu.VMEM(field.shape, f32),
            pltpu.SemaphoreType.DMA((4,)),
        ),
        held=(0, 1, 2, 3),
    )
    cell = (wide, per_cell, pad)
    dims = (groups, depth, kgroup, basis.shape[2])
    basis_t = basis_kept = basis_p = every = spread = None

    for sweep in range(ITERS):
        last = sweep == ITERS - 1
        first_q, second_q = swap(first, second, GROUP_AXES)
        if sweep == 0:
            every = sent
            rounds = (n_sub - 1).bit_length()
            for power in range(rounds - 1):
                every = doubled(every, 1 << power)
            first_q, second_q, every = lax.optimization_barrier((first_q, second_q, every))
        first, second = call(
            functools.partial(row_kernel, shape),
            (solution, base, first_q, second_q),
            (row_message, row_message),
        )
        first_s, second_s = swap(first, second, "sub")
        if sweep == 0:
            later, _ = lax.optimization_barrier((basis, first))
            basis_t, basis_kept, basis_p = ordered_basis(
                cell, dims, offsets, later, (coarse, rows), (cells * pad, coarse)
            )
            shared, _ = lax.optimization_barrier((coarse_inverse, first))
            pairs = [(i, i ^ PARTNER) for i in range(groups)]
            partner = lax.ppermute(shared, GROUP_AXES, pairs)
            every = doubled(every, 1 << (rounds - 1))
            first_s, second_s, every = lax.optimization_barrier((first_s, second_s, every))
        message, local = call(
            functools.partial(window_kernel, shape),
            (solution, base, first_q, second_q, first_s, second_s, basis_t if sweep == 0 else basis_kept),
            (
                pltpu.HBM((groups, coarse, columns // 2), bf16),
                pltpu.HBM(((cells_s + 2) * wide, pad, columns), bf16),
            ),
            scratch=(
                pltpu.VMEM(((cells_s + 2) * wide, pad, columns), bf16),
                pltpu.VMEM((2, coarse, columns // 2), bf16),
                pltpu.SemaphoreType.DMA((groups + cells_s + 2,)),
            ),
            flops=2 * rows * coarse * columns,
        )
        if sweep == 0:
            waited, _ = lax.optimization_barrier((every, message))
            spread = spread_inverse(waited, coarse_inverse, partner, depth)
        gathered = lax.all_to_all(message, GROUP_AXES, 0, 0, tiled=True)
        held = pltpu.VMEM((spread.shape[0], columns // 2), bf16)
        (terms,) = call(
            terms_kernel,
            (spread, gathered.reshape(-1, columns // 2)),
            (pltpu.HBM(held.shape, bf16),),
            scratch=(held, pltpu.SemaphoreType.DMA),
            flops=2 * spread.size * columns // 2,
        )
        arrived = lax.all_to_all(
            terms.reshape(n_sub * groups, 2 * depth, columns // 2), ALL_AXES, 0, 0, tiled=True
        ).reshape(n_sub, groups, 2 * depth, columns // 2)
        kept = fine_product(
            shape, layers, local, sub_inverse, solution, base, stiffness, last
        )
        if last:
            (out,) = call(
                functools.partial(close_kernel, shape, layers),
                (arrived, basis_p, *kept),
                (pltpu.HBM((cells_s, cells_q) + tail, f32),),
                scratch=(
                    pltpu.VMEM(basis_p.shape, bf16),
                    pltpu.VMEM(field.shape, f32),
                    pltpu.VMEM((cells_s, cells_q) + tail, f32),
                    pltpu.SemaphoreType.DMA((2 * cells_s + 1,)),
                ),
                held=(1, 2),
            )
        else:
            first, second, change = call(
                functools.partial(step_sides_kernel, shape, layers),
                (
                    arrived,
                    basis_p,
                    *(x.reshape(cells_s, cells_q, pad, columns) for x in kept),
                    stiffness,
                ),
                (column_message, column_message, field),
                scratch=(
                    pltpu.VMEM(basis_p.shape, bf16),
                    pltpu.VMEM(stiffness.shape, f32),
                    pltpu.VMEM((cells_s, cells_q, pad, columns), f32),
                    pltpu.VMEM((cells_s, cells_q, pad, columns), f32),
                    pltpu.VMEM(field.shape, f32),
                    pltpu.SemaphoreType.DMA((6,)),
                ),
                held=(1, 2, 3, 4),
            )
            solution, base = call(
                functools.partial(step_kernel, shape, layers),
                (change, *kept, stiffness),
                (field, field),
                scratch=(
                    pltpu.VMEM(stiffness.shape, f32),
                    pltpu.VMEM(field.shape, f32),
                    pltpu.SemaphoreType.DMA((3,)),
                ),
                held=(1, 2, 3),
            )
    return out.transpose(0, 1, 3, 2, 4)


def solution(mesh):
    return jax.shard_map(
        shards,
        mesh=mesh,
        in_specs=(
            P("sub", ("crow", "ccol"), None, None, None),
            P("sub", ("crow", "ccol"), None, None, None),
            P("sub", ("crow", "ccol"), None, None),
            P(("sub", "crow", "ccol"), None, None),
            P(("sub", "crow", "ccol"), None, None),
            P(None, ("crow", "ccol"), "sub"),
            P("sub", None),
        ),
        out_specs=P("sub", ("crow", "ccol"), None, None, None),
        check_vma=False,
    )
```

```python
import functools
import math

import jax
import jax.numpy as jnp
from jax import lax
from jax.experimental import pallas as pl
from jax.experimental.pallas import tpu as pltpu
from jax.sharding import PartitionSpec as P

ITERS = 2
PARTNER = 2
GROUP_AXES = ("crow", "ccol")
ALL_AXES = ("sub", "crow", "ccol")
bf16, f32 = jnp.bfloat16, jnp.float32
VMEM = pl.BlockSpec(memory_space=pltpu.VMEM)
HBM = pl.BlockSpec(memory_space=pltpu.HBM)


def sized(x):
    return math.prod(x.shape) * jnp.dtype(x.dtype).itemsize


def call(body, ins, outs, scratch=(), flops=0, held=()):
    size = sum(sized(x) for x in (*ins, *outs))
    room = size + sum(sized(x) for x in scratch if getattr(x, "dtype", None) in (bf16, f32))
    return pl.pallas_call(
        body,
        out_shape=tuple(outs),
        in_specs=[HBM if i in held else VMEM for i in range(len(ins))],
        out_specs=tuple(
            HBM if getattr(x, "memory_space", None) == pltpu.HBM else VMEM for x in outs
        ),
        scratch_shapes=list(scratch),
        compiler_params=pltpu.CompilerParams(vmem_limit_bytes=room + (4 << 20)),
        cost_estimate=pl.CostEstimate(flops=flops, bytes_accessed=size, transcendentals=0),
    )(
        *[
            pltpu.with_memory_space_constraint(x, pltpu.HBM) if i in held else x
            for i, x in enumerate(ins)
        ]
    )


def begun(source, target, sem):
    copy = pltpu.make_async_copy(source, target, sem)
    copy.start()
    return copy


def packing(cells, per_cell, pad, turned=False):
    shape = (cells * per_cell, cells * pad)
    shape = shape[::-1] if turned else shape
    row = lax.broadcasted_iota(jnp.int32, shape, 1 if turned else 0)
    column = lax.broadcasted_iota(jnp.int32, shape, 0 if turned else 1)
    for w in range(1, cells):
        column = column - jnp.where(row >= w * per_cell, pad - per_cell, 0)
    return jnp.where(row == column, 1.0, 0.0).astype(bf16)


def swap(first, second, axis):
    count = lax.axis_size(axis)
    even = [(i, i + 1) for i in range(0, count - 1, 2)]
    odd = [(i, i + 1) for i in range(1, count - 1, 2)]
    return (
        lax.ppermute(first, axis, even + [(b, a) for a, b in even]),
        lax.ppermute(second, axis, odd + [(b, a) for a, b in odd]),
    )


def doubled(held, step):
    count = lax.axis_size("sub")
    return held + lax.ppermute(held, "sub", [(i, i ^ step) for i in range(count)])


def diagonal_of(stiffness, s, q, comps, layers, pad, columns):
    at = lax.broadcasted_iota(jnp.int32, (pad, layers), 0)
    layer = lax.broadcasted_iota(jnp.int32, (pad, layers), 1)
    column = jnp.zeros((pad, layers), f32)
    for c in range(comps):
        column = jnp.where(at == layer + c * layers, stiffness[s, q, c : c + 1, :], column)
    column = 6.0 + jnp.sum(column, axis=1, keepdims=True)
    return jnp.broadcast_to(column, (pad, columns))


def write_base(layers, begin, stiffness, field, base, shape, only=None):
    cells_s, cells_q, comps, pad, columns = shape
    at = lax.broadcasted_iota(jnp.int32, (pad, columns), 0)
    has_up, has_down = at < comps * layers, at < comps * layers
    for c in range(comps):
        has_up = has_up & (at != c * layers)
        has_down = has_down & (at != c * layers + layers - 1)
    for s in range(cells_s):
        for q in only or range(cells_q):
            i = s * cells_q + q
            x = field[i]
            diagonal = diagonal_of(stiffness, s, q, comps, layers, pad, columns)
            total = begin[i] - diagonal * x
            total = total + jnp.where(has_up, pltpu.roll(x, 1, 0), 0.0)
            total = total + jnp.where(has_down, pltpu.roll(x, pad - 1, 0), 0.0)
            if q > 0:
                total = total + field[i - 1]
            if q < cells_q - 1:
                total = total + field[i + 1]
            if s > 0:
                total = total + field[i - cells_q]
            if s < cells_s - 1:
                total = total + field[i + cells_q]
            base[i] = total


def write_column_messages(sol, base, first, second, shape):
    cells_s, cells_q = shape[:2]
    even = lax.axis_index(GROUP_AXES) % 2 == 0
    for out, q in (
        (first, jnp.where(even, cells_q - 1, 0)),
        (second, jnp.where(even, 0, cells_q - 1)),
    ):
        for s in range(cells_s):
            out[0, s] = base[s * cells_q + q].astype(bf16)
            out[1, s] = sol[s * cells_q + q].astype(bf16)


def unpack_cell(source, target, i, shape, layers):
    _, _, comps, pad, columns = shape
    for c in range(comps):
        target[i, c * layers : (c + 1) * layers, :] = source[:, c, :]
    target[i, comps * layers :, :] = jnp.zeros((pad - comps * layers, columns), f32)


def open_sides_kernel(
    shape, layers, start, rhs, stiffness, first, second, raw, raw_rhs, stiff, sol, begin, base, sems
):
    cells_s, cells_q = shape[:2]
    sides = (0, cells_q - 1)
    near = (0, 1, cells_q - 2, cells_q - 1)
    copies = [
        begun(stiffness, stiff, sems.at[0]),
        begun(start.at[:, pl.ds(0, 2)], raw.at[:, pl.ds(0, 2)], sems.at[1]),
        begun(start.at[:, pl.ds(cells_q - 2, 2)], raw.at[:, pl.ds(2, 2)], sems.at[2]),
        begun(rhs.at[:, pl.ds(0, 1)], raw_rhs.at[:, pl.ds(0, 1)], sems.at[3]),
        begun(rhs.at[:, pl.ds(cells_q - 1, 1)], raw_rhs.at[:, pl.ds(1, 1)], sems.at[4]),
    ]
    for copy in copies:
        copy.wait()
    for s in range(cells_s):
        for k, q in enumerate(near):
            unpack_cell(raw.at[s, k], sol, s * cells_q + q, shape, layers)
        for k, q in enumerate(sides):
            unpack_cell(raw_rhs.at[s, k], begin, s * cells_q + q, shape, layers)
    write_base(layers, begin, stiff, sol, base, shape, sides)
    write_column_messages(sol, base, first, second, shape)


def open_kernel(
    shape, layers, start, rhs, stiffness, offsets, sol, base, sent, raw, raw_rhs, stiff, own, begin, sems
):
    cells_s, cells_q = shape[:2]
    sources, targets = (stiffness, offsets, start, rhs), (stiff, own, raw, raw_rhs)
    copies = [begun(a, b, sems.at[k]) for k, (a, b) in enumerate(zip(sources, targets))]
    for copy in copies:
        copy.wait()
    group = lax.broadcasted_iota(jnp.int32, sent.shape, 0)
    sent[...] = jnp.where(group == lax.axis_index("sub"), own[...], 0)
    for s in range(cells_s):
        for q in range(cells_q):
            unpack_cell(raw.at[s, q], sol, s * cells_q + q, shape, layers)
            unpack_cell(raw_rhs.at[s, q], begin, s * cells_q + q, shape, layers)
    write_base(layers, begin, stiff, sol, base, shape)


def column_sides(first, second):
    even = lax.axis_index(GROUP_AXES) % 2 == 0

    def low(kind, s):
        return jnp.where(even, second[kind, s].astype(f32), first[kind, s].astype(f32))

    def high(kind, s):
        return jnp.where(even, first[kind, s].astype(f32), second[kind, s].astype(f32))

    return low, high


def edge_cells(low, high, sol, s, cells_q):
    col, cols = lax.axis_index(GROUP_AXES), lax.axis_size(GROUP_AXES)
    left = jnp.where(col > 0, low(0, s) + sol[s * cells_q], 0.0)
    right = jnp.where(col < cols - 1, high(0, s) + sol[s * cells_q + cells_q - 1], 0.0)
    return left, right


def row_kernel(shape, sol, base, first_in, second_in, first, second):
    cells_s, cells_q = shape[:2]
    low, high = column_sides(first_in, second_in)
    even = lax.axis_index("sub") % 2 == 0
    for out, s in (
        (first, jnp.where(even, cells_s - 1, 0)),
        (second, jnp.where(even, 0, cells_s - 1)),
    ):
        left, right = edge_cells(low, high, sol, s, cells_q)
        out[0, 0] = left.astype(bf16)
        out[0, cells_q + 1] = right.astype(bf16)
        low_s, high_s = low(1, s), high(1, s)
        out[1, 0] = low_s.astype(bf16)
        out[1, cells_q + 1] = high_s.astype(bf16)
        for q in range(cells_q):
            value = base[s * cells_q + q]
            if q == 0:
                value = value + low_s
            if q == cells_q - 1:
                value = value + high_s
            out[0, q + 1] = value.astype(bf16)
            out[1, q + 1] = sol[s * cells_q + q].astype(bf16)


def side_of(member):
    return (member // PARTNER) % 2


def window_kernel(
    shape,
    sol,
    base,
    first_q,
    second_q,
    first_s,
    second_s,
    basis_t,
    message,
    local_kept,
    local,
    restricted,
    sems,
):
    cells_s, cells_q, _, pad, columns = shape
    wide = cells_q + 2
    low, high = column_sides(first_q, second_q)
    row, rows = lax.axis_index("sub"), lax.axis_size("sub")
    even = row % 2 == 0

    def above(kind, w):
        return jnp.where(even, second_s[kind, w].astype(f32), first_s[kind, w].astype(f32))

    def below(kind, w):
        return jnp.where(even, first_s[kind, w].astype(f32), second_s[kind, w].astype(f32))

    copies = []
    for s in range(cells_s):
        left, right = edge_cells(low, high, sol, s, cells_q)
        values = [left] + [base[s * cells_q + q] for q in range(cells_q)] + [right]
        values[1] = values[1] + low(1, s)
        values[cells_q] = values[cells_q] + high(1, s)
        for w in range(wide):
            value = values[w]
            if s == 0:
                value = value + above(1, w)
            if s == cells_s - 1:
                value = value + below(1, w)
            local[(s + 1) * wide + w] = value.astype(bf16)
        part = pl.ds((s + 1) * wide, wide)
        copies.append(begun(local.at[part], local_kept.at[part], sems.at[len(copies)]))
    for s, side, place, there in (
        (0, above, 0, row > 0),
        (cells_s - 1, below, (cells_s + 1) * wide, row < rows - 1),
    ):
        near = [low(1, s)] + [sol[s * cells_q + q] for q in range(cells_q)] + [high(1, s)]
        for w in range(wide):
            local[place + w] = jnp.where(there, side(0, w) + near[w], 0.0).astype(bf16)
        part = pl.ds(place, wide)
        copies.append(begun(local.at[part], local_kept.at[part], sems.at[len(copies)]))
    product = jnp.dot(
        basis_t[...], local[...].reshape(-1, columns), preferred_element_type=f32
    ).astype(bf16)
    half = columns // 2
    for k in range(2):
        restricted[k] = product[:, k * half : (k + 1) * half]
    for j in range(message.shape[0]):
        copies.append(begun(restricted.at[side_of(j)], message.at[j], sems.at[len(copies)]))
    for copy in copies:
        copy.wait()


def terms_kernel(spread, gathered, out, kept, sem):
    kept[...] = jnp.dot(spread[...], gathered[...], preferred_element_type=f32).astype(bf16)
    begun(kept, out, sem).wait()


def fine_kernel(shape, layers, steps, last, local_kept, inverse_kept, sol_kept, *refs):
    cells_s, cells_q, comps, pad, columns = shape
    if last:
        out, local, inverse, packed, sol, fine, sems = refs
        fields = ((sol_kept, sol),)
    else:
        base_kept, stiffness, out, base_out, local, inverse, packed, sol, fine, base, sems = refs
        fields = ((sol_kept, sol), (base_kept, base))
    per_cell = comps * layers
    wide = cells_q + 2
    span, chunk = wide * per_cell, wide * pad
    size = cells_s // steps
    loaded = begun(local_kept, local, sems.at[0])
    arriving = [
        begun(
            inverse_kept.at[0, pl.ds((k * size + 1) * span, size * span)],
            inverse.at[pl.ds(k * size * span, size * span)],
            sems.at[k + 1],
        )
        for k in range(steps)
    ]
    others = [begun(a, b, sems.at[steps + 1 + k]) for k, (a, b) in enumerate(fields)]
    pack = packing(wide, per_cell, pad)
    loaded.wait()
    for s in range(packed.shape[0] // span):
        part = local[s * wide : (s + 1) * wide].reshape(chunk, columns)
        packed[s * span : (s + 1) * span, :] = jnp.dot(
            pack, part, preferred_element_type=f32
        ).astype(bf16)
    for k in range(steps):
        arriving[k].wait()
        rows = jnp.dot(
            inverse[k * size * span : (k + 1) * size * span, :],
            packed[...],
            preferred_element_type=f32,
        )
        for s in range(size):
            for q in range(cells_q):
                i = (k * size + s) * cells_q + q
                first = s * span + (q + 1) * per_cell
                fine[i, :per_cell, :] = rows[first : first + per_cell]
                fine[i, per_cell:, :] = jnp.zeros((pad - per_cell, columns), f32)
    for copy in others:
        copy.wait()
    for i in range(fine.shape[0]):
        sol[i] = sol[i] + fine[i]
    copies = [begun(sol, out, sems.at[steps + 3])]
    if not last:
        write_base(layers, base, stiffness, fine, base, shape)
        copies.append(begun(base, base_out, sems.at[steps + 4]))
    for copy in copies:
        copy.wait()


def fine_product(shape, layers, local, sub_inverse, sol, base, stiffness, last):
    cells_s, cells_q, comps, pad, columns = shape
    width = sub_inverse.shape[2]
    rows = cells_s * (cells_q + 2) * comps * layers
    steps = 3 if cells_s % 3 == 0 else 1
    kept = pltpu.HBM((cells_s * cells_q, pad, columns), f32)
    field = pltpu.VMEM(kept.shape, f32)
    return call(
        functools.partial(fine_kernel, shape, layers, steps, last),
        (local, sub_inverse, sol) if last else (local, sub_inverse, sol, base, stiffness),
        (kept,) if last else (kept, kept),
        scratch=(
            pltpu.VMEM(local.shape, bf16),
            pltpu.VMEM((rows, width), bf16),
            pltpu.VMEM((width, columns), bf16),
        )
        + ((field, field) if last else (field, field, field))
        + (pltpu.SemaphoreType.DMA((steps + 5,)),),
        flops=2 * rows * width * columns,
        held=(0, 1, 2) if last else (0, 1, 2, 3),
    )


def coarse_values(arrived, depth):
    sums = []
    for c in range(arrived.shape[1]):
        total = arrived[0, c].astype(f32)
        for h in range(1, arrived.shape[0]):
            total = total + arrived[h, c].astype(f32)
        sums.append(total)
    rows = []
    for m in range(arrived.shape[1]):
        part = slice(side_of(m) * depth, (side_of(m) + 1) * depth)
        low = m - side_of(m) * PARTNER
        rows.append(jnp.concatenate([sums[low][part], sums[low + PARTNER][part]], axis=1))
    return jnp.concatenate(rows, axis=0).astype(bf16)


def step_sides_kernel(
    shape,
    layers,
    arrived,
    basis_kept,
    sol_kept,
    base_kept,
    stiffness,
    first,
    second,
    coarse,
    basis_p,
    stiff,
    sol,
    begin,
    base,
    sems,
):
    cells_s, cells_q, _, pad, columns = shape
    sides = (0, cells_q - 1)
    copies = [begun(basis_kept, basis_p, sems.at[0]), begun(stiffness, stiff, sems.at[1])]
    for q in sides:
        copies.append(begun(sol_kept.at[:, q], sol.at[:, q], sems.at[len(copies)]))
        copies.append(begun(base_kept.at[:, q], begin.at[:, q], sems.at[len(copies)]))
    sol, begin = (x.reshape(cells_s * cells_q, pad, columns) for x in (sol, begin))
    chosen = coarse_values(arrived, arrived.shape[2] // 2)
    copies[0].wait()
    span = cells_q * pad
    for s in range(cells_s):
        rows = jnp.dot(
            basis_p[s * span : (s + 1) * span, :], chosen, preferred_element_type=f32
        )
        coarse[s * cells_q : (s + 1) * cells_q] = rows.reshape(cells_q, pad, columns)
    for copy in copies[1:]:
        copy.wait()
    for s in range(cells_s):
        for q in sides:
            i = s * cells_q + q
            sol[i] = sol[i] + coarse[i]
    write_base(layers, begin, stiff, coarse, base, shape, sides)
    write_column_messages(sol, base, first, second, shape)


def step_kernel(shape, layers, coarse, sol_kept, base_kept, stiffness, new, base, stiff, begin, sems):
    sources, targets = (stiffness, sol_kept, base_kept), (stiff, new, begin)
    copies = [begun(a, b, sems.at[k]) for k, (a, b) in enumerate(zip(sources, targets))]
    for copy in copies:
        copy.wait()
    for i in range(new.shape[0]):
        new[i] = new[i] + coarse[i]
    write_base(layers, begin, stiff, coarse, base, shape)


def close_kernel(
    shape, layers, arrived, basis_kept, sol_kept, out_kept, basis_p, sol, out, sems
):
    cells_s, cells_q, comps, pad, columns = shape
    span = cells_q * pad
    copies = [begun(basis_kept, basis_p, sems.at[0])]
    for s in range(cells_s):
        part = pl.ds(s * cells_q, cells_q)
        copies.append(begun(sol_kept.at[part], sol.at[part], sems.at[s + 1]))
    chosen = coarse_values(arrived, arrived.shape[2] // 2)
    copies[0].wait()
    results = []
    for s in range(cells_s):
        rows = jnp.dot(
            basis_p[s * span : (s + 1) * span, :], chosen, preferred_element_type=f32
        )
        copies[s + 1].wait()
        for q in range(cells_q):
            total = sol[s * cells_q + q] + rows[q * pad : (q + 1) * pad]
            for c in range(comps):
                out[s, q, :, c, :] = total[c * layers : (c + 1) * layers]
        results.append(begun(out.at[s], out_kept.at[s], sems.at[cells_s + 1 + s]))
    for copy in results:
        copy.wait()


def places(offsets, g, j, groups, depth, kgroup):
    first = offsets[g, j]
    end = kgroup if j == groups - 1 else offsets[g, j + 1]
    shape = (1, groups * depth)
    at = lax.broadcasted_iota(jnp.int32, shape, 1)
    turn = at
    member = jnp.zeros(shape, jnp.int32)
    for m in range(1, groups):
        member = member + jnp.where(at >= m * depth, 1, 0)
        turn = turn - jnp.where(at >= m * depth, depth, 0)
    shifted = member - lax.rem(first, groups)
    shifted = jnp.where(shifted < 0, shifted + groups, shifted)
    place = shifted + turn * groups
    return first, place, place < end - first


def ordering(dims, offsets):
    groups, depth, kgroup, count = dims
    member = lax.axis_index(GROUP_AXES)
    wanted = jnp.full((1, groups * depth), -1, jnp.int32)
    for j in range(groups):
        _, place, valid = places(offsets, 0, j, groups, depth, kgroup)
        wanted = jnp.where(valid & (member == j), place, wanted)
    row = lax.broadcasted_iota(jnp.int32, (count, groups * depth), 0)
    return jnp.where(row == wanted, 1.0, 0.0).astype(bf16)


def basis_kernel(cell, dims, offsets, basis_kept, basis_t, turned_kept, own_kept, basis, own, sems):
    wide, per_cell, pad = cell
    span, chunk = wide * per_cell, wide * pad
    size = chunk - 2 * pad
    copy = begun(basis_kept.at[0], basis, sems.at[0])
    pack = packing(wide, per_cell, pad)
    pack_own = packing(wide, per_cell, pad, True)[pad : pad + size]
    order = ordering(dims, offsets)
    rows = basis.shape[0] // span
    copy.wait()
    for s in range(rows):
        ordered = jnp.dot(
            basis[s * span : (s + 1) * span, :], order, preferred_element_type=f32
        ).astype(bf16)
        basis_t[:, s * chunk : (s + 1) * chunk] = lax.dot_general(
            ordered, pack, (((0,), (0,)), ((), ())), preferred_element_type=f32
        ).astype(bf16)
        if 0 < s < rows - 1:
            own[(s - 1) * size : s * size, :] = jnp.dot(
                pack_own, ordered, preferred_element_type=f32
            ).astype(bf16)
    copies = [begun(basis_t, turned_kept, sems.at[1]), begun(own, own_kept, sems.at[2])]
    for copy in copies:
        copy.wait()


def ordered_basis(cell, dims, offsets, basis, turned, own):
    return pl.pallas_call(
        functools.partial(basis_kernel, cell, dims),
        out_shape=(jax.ShapeDtypeStruct(turned, bf16), pltpu.HBM(turned, bf16), pltpu.HBM(own, bf16)),
        in_specs=[pl.BlockSpec(memory_space=pltpu.SMEM), HBM],
        out_specs=(VMEM, HBM, HBM),
        scratch_shapes=[
            pltpu.VMEM(basis.shape[1:], bf16),
            pltpu.VMEM(own, bf16),
            pltpu.SemaphoreType.DMA((3,)),
        ],
        compiler_params=pltpu.CompilerParams(vmem_limit_bytes=12 << 20),
        cost_estimate=pl.CostEstimate(
            flops=6 * turned[0] * turned[1] * cell[0] * cell[2],
            bytes_accessed=6 * basis.size,
            transcendentals=0,
        ),
    )(offsets, pltpu.with_memory_space_constraint(basis, pltpu.HBM))


def first_index(first, member, groups):
    if groups & (groups - 1) == 0:
        return lax.shift_right_logical(first - member + groups - 1, groups.bit_length() - 1)
    return lax.div(first - member + groups - 1, groups)


def spread_kernel(dims, every, inverse_kept, partner_kept, out_kept, inverse, columns, picked, out, sems):
    groups, depth, kgroup = dims
    coarse = groups * depth
    member = lax.axis_index(GROUP_AXES)
    own = lax.axis_index("sub")
    side = side_of(member)
    copies = [
        begun(inverse_kept, inverse.at[side], sems.at[0]),
        begun(partner_kept, inverse.at[1 - side], sems.at[1]),
    ]
    slot = lax.broadcasted_iota(jnp.int32, (kgroup, coarse), 0)
    for j in range(groups):
        first, place, valid = places(every, own, j, groups, depth, kgroup)
        wanted = jnp.where(valid, place + first, -1)
        columns[:, j * coarse : (j + 1) * coarse] = jnp.where(slot == wanted, 1.0, 0.0).astype(bf16)
    _, n_sub, rows, _ = inverse.shape
    turn = lax.broadcasted_iota(jnp.int32, (depth, rows), 0)
    index = lax.broadcasted_iota(jnp.int32, (depth, rows), 1)
    for copy in copies:
        copy.wait()
    span = 2 * coarse
    steps = max(n_sub // 4, 1)
    size = n_sub // steps

    def some(k, _):
        for t in range(size):
            g = k * size + t
            for b in range(2):
                m = member + (b - side) * PARTNER
                picks = []
                for j in range(groups):
                    first = every[g, j]
                    end = kgroup if j == groups - 1 else every[g, j + 1]
                    begin = first_index(first, m, groups)
                    wanted = (index == turn + begin) & (index * groups + m < end)
                    picks.append(jnp.where(wanted, 1.0, 0.0).astype(bf16))
                part = jnp.dot(
                    jnp.concatenate(picks, axis=0), inverse[b, g], preferred_element_type=f32
                ).astype(bf16)
                for j in range(groups):
                    at = t * span + (2 * j + b) * depth
                    picked[at : at + depth, :] = part[j * depth : (j + 1) * depth]
        results = []
        for t in range(size):
            part = pl.ds(t * span, span)
            out[part, :] = jnp.dot(
                picked[part, :], columns[...], preferred_element_type=f32
            ).astype(bf16)
            there = pl.ds((k * size + t) * span, span)
            results.append(begun(out.at[part], out_kept.at[there], sems.at[2 + t]))
        for copy in results:
            copy.wait()
        return 0

    lax.fori_loop(0, steps, some, 0)


def spread_inverse(every, coarse_inverse, partner, depth):
    n_sub, share_rows, kgroup = coarse_inverse.shape
    groups = every.shape[1]
    coarse = groups * depth
    rows = n_sub * 2 * coarse
    part = rows // max(n_sub // 4, 1)
    return pl.pallas_call(
        functools.partial(spread_kernel, (groups, depth, kgroup)),
        out_shape=pltpu.HBM((rows, groups * coarse), bf16),
        in_specs=[pl.BlockSpec(memory_space=pltpu.SMEM), HBM, HBM],
        out_specs=HBM,
        scratch_shapes=[
            pltpu.VMEM((2,) + coarse_inverse.shape, bf16),
            pltpu.VMEM((kgroup, groups * coarse), bf16),
            pltpu.VMEM((part, kgroup), bf16),
            pltpu.VMEM((part, groups * coarse), bf16),
            pltpu.SemaphoreType.DMA((2 + part // (2 * coarse),)),
        ],
        compiler_params=pltpu.CompilerParams(
            vmem_limit_bytes=(16 << 20) + 4 * coarse_inverse.size + 8 * part * groups * coarse
        ),
        cost_estimate=pl.CostEstimate(
            flops=2 * rows * groups * coarse * kgroup,
            bytes_accessed=2 * rows * groups * coarse,
            transcendentals=0,
        ),
    )(
        every,
        pltpu.with_memory_space_constraint(coarse_inverse, pltpu.HBM),
        pltpu.with_memory_space_constraint(partner, pltpu.HBM),
    )


def shards(rhs, start, stiffness, sub_inverse, basis, coarse_inverse, offsets):
    cells_s, cells_q, comps, layers, columns = rhs.shape
    n_sub, _, kgroup = coarse_inverse.shape
    groups = offsets.shape[1]
    depth = -(-basis.shape[2] // groups)
    coarse = groups * depth
    cells = cells_s * cells_q
    per_cell = comps * layers
    pad = -(-per_cell // 16) * 16
    wide = cells_q + 2
    shape = (cells_s, cells_q, comps, pad, columns)

    field = jax.ShapeDtypeStruct((cells, pad, columns), f32)
    column_message = jax.ShapeDtypeStruct((2, cells_s, pad, columns), bf16)
    row_message = jax.ShapeDtypeStruct((2, wide, pad, columns), bf16)

    rows = (cells_s + 2) * wide * pad

    start_cells, rhs_cells = (x.transpose(0, 1, 3, 2, 4) for x in (start, rhs))
    tail = (layers, comps, columns)
    first, second = call(
        functools.partial(open_sides_kernel, shape, layers),
        (start_cells, rhs_cells, stiffness),
        (column_message, column_message),
        scratch=(
            pltpu.VMEM((cells_s, 4) + tail, f32),
            pltpu.VMEM((cells_s, 2) + tail, f32),
            pltpu.VMEM(stiffness.shape, f32),
            pltpu.VMEM(field.shape, f32),
            pltpu.VMEM(field.shape, f32),
            pltpu.VMEM(field.shape, f32),
            pltpu.SemaphoreType.DMA((5,)),
        ),
        held=(0, 1, 2),
    )
    solution, base, sent = call(
        functools.partial(open_kernel, shape, layers),
        (start_cells, rhs_cells, stiffness, offsets),
        (field, field, jax.ShapeDtypeStruct((n_sub, groups), jnp.int32)),
        scratch=(
            pltpu.VMEM((cells_s, cells_q) + tail, f32),
            pltpu.VMEM((cells_s, cells_q) + tail, f32),
            pltpu.VMEM(stiffness.shape, f32),
            pltpu.VMEM(offsets.shape, jnp.int32),
            pltpu.VMEM(field.shape, f32),
            pltpu.SemaphoreType.DMA((4,)),
        ),
        held=(0, 1, 2, 3),
    )
    cell = (wide, per_cell, pad)
    dims = (groups, depth, kgroup, basis.shape[2])
    basis_t = basis_kept = basis_p = every = spread = None

    for sweep in range(ITERS):
        last = sweep == ITERS - 1
        first_q, second_q = swap(first, second, GROUP_AXES)
        if sweep == 0:
            every = sent
            rounds = (n_sub - 1).bit_length()
            for power in range(rounds - 1):
                every = doubled(every, 1 << power)
            first_q, second_q, every = lax.optimization_barrier((first_q, second_q, every))
        first, second = call(
            functools.partial(row_kernel, shape),
            (solution, base, first_q, second_q),
            (row_message, row_message),
        )
        first_s, second_s = swap(first, second, "sub")
        if sweep == 0:
            later, _ = lax.optimization_barrier((basis, first))
            basis_t, basis_kept, basis_p = ordered_basis(
                cell, dims, offsets, later, (coarse, rows), (cells * pad, coarse)
            )
            shared, _ = lax.optimization_barrier((coarse_inverse, first))
            pairs = [(i, i ^ PARTNER) for i in range(groups)]
            partner = lax.ppermute(shared, GROUP_AXES, pairs)
            every = doubled(every, 1 << (rounds - 1))
            first_s, second_s, every = lax.optimization_barrier((first_s, second_s, every))
        message, local = call(
            functools.partial(window_kernel, shape),
            (solution, base, first_q, second_q, first_s, second_s, basis_t if sweep == 0 else basis_kept),
            (
                pltpu.HBM((groups, coarse, columns // 2), bf16),
                pltpu.HBM(((cells_s + 2) * wide, pad, columns), bf16),
            ),
            scratch=(
                pltpu.VMEM(((cells_s + 2) * wide, pad, columns), bf16),
                pltpu.VMEM((2, coarse, columns // 2), bf16),
                pltpu.SemaphoreType.DMA((groups + cells_s + 2,)),
            ),
            flops=2 * rows * coarse * columns,
        )
        if sweep == 0:
            waited, _ = lax.optimization_barrier((every, message))
            spread = spread_inverse(waited, coarse_inverse, partner, depth)
        gathered = lax.all_to_all(message, GROUP_AXES, 0, 0, tiled=True)
        held = pltpu.VMEM((spread.shape[0], columns // 2), bf16)
        (terms,) = call(
            terms_kernel,
            (spread, gathered.reshape(-1, columns // 2)),
            (pltpu.HBM(held.shape, bf16),),
            scratch=(held, pltpu.SemaphoreType.DMA),
            flops=2 * spread.size * columns // 2,
        )
        arrived = lax.all_to_all(
            terms.reshape(n_sub * groups, 2 * depth, columns // 2), ALL_AXES, 0, 0, tiled=True
        ).reshape(n_sub, groups, 2 * depth, columns // 2)
        kept = fine_product(
            shape, layers, local, sub_inverse, solution, base, stiffness, last
        )
        if last:
            (out,) = call(
                functools.partial(close_kernel, shape, layers),
                (arrived, basis_p, *kept),
                (pltpu.HBM((cells_s, cells_q) + tail, f32),),
                scratch=(
                    pltpu.VMEM(basis_p.shape, bf16),
                    pltpu.VMEM(field.shape, f32),
                    pltpu.VMEM((cells_s, cells_q) + tail, f32),
                    pltpu.SemaphoreType.DMA((2 * cells_s + 1,)),
                ),
                held=(1, 2),
            )
        else:
            first, second, change = call(
                functools.partial(step_sides_kernel, shape, layers),
                (
                    arrived,
                    basis_p,
                    *(x.reshape(cells_s, cells_q, pad, columns) for x in kept),
                    stiffness,
                ),
                (column_message, column_message, field),
                scratch=(
                    pltpu.VMEM(basis_p.shape, bf16),
                    pltpu.VMEM(stiffness.shape, f32),
                    pltpu.VMEM((cells_s, cells_q, pad, columns), f32),
                    pltpu.VMEM((cells_s, cells_q, pad, columns), f32),
                    pltpu.VMEM(field.shape, f32),
                    pltpu.SemaphoreType.DMA((6,)),
                ),
                held=(1, 2, 3, 4),
            )
            solution, base = call(
                functools.partial(step_kernel, shape, layers),
                (change, *kept, stiffness),
                (field, field),
                scratch=(
                    pltpu.VMEM(stiffness.shape, f32),
                    pltpu.VMEM(field.shape, f32),
                    pltpu.SemaphoreType.DMA((3,)),
                ),
                held=(1, 2, 3),
            )
    return out.transpose(0, 1, 3, 2, 4)


def solution(mesh):
    return jax.shard_map(
        shards,
        mesh=mesh,
        in_specs=(
            P("sub", ("crow", "ccol"), None, None, None),
            P("sub", ("crow", "ccol"), None, None, None),
            P("sub", ("crow", "ccol"), None, None),
            P(("sub", "crow", "ccol"), None, None),
            P(("sub", "crow", "ccol"), None, None),
            P(None, ("crow", "ccol"), "sub"),
            P("sub", None),
        ),
        out_specs=P("sub", ("crow", "ccol"), None, None, None),
        check_vma=False,
    )
```

```python
import functools
import math

import jax
import jax.numpy as jnp
from jax import lax
from jax.experimental import pallas as pl
from jax.experimental.pallas import tpu as pltpu
from jax.sharding import PartitionSpec as P

ITERS = 2
PARTNER = 2
GROUP_AXES = ("crow", "ccol")
ALL_AXES = ("sub", "crow", "ccol")
bf16, f32 = jnp.bfloat16, jnp.float32
VMEM = pl.BlockSpec(memory_space=pltpu.VMEM)
HBM = pl.BlockSpec(memory_space=pltpu.HBM)


def sized(x):
    return math.prod(x.shape) * jnp.dtype(x.dtype).itemsize


def call(body, ins, outs, scratch=(), flops=0, held=(), aliases=None):
    size = sum(sized(x) for x in (*ins, *outs))
    room = size + sum(sized(x) for x in scratch if getattr(x, "dtype", None) in (bf16, f32))
    return pl.pallas_call(
        body,
        out_shape=tuple(outs),
        in_specs=[HBM if i in held else VMEM for i in range(len(ins))],
        out_specs=tuple(
            HBM if getattr(x, "memory_space", None) == pltpu.HBM else VMEM for x in outs
        ),
        scratch_shapes=list(scratch),
        input_output_aliases=aliases or {},
        compiler_params=pltpu.CompilerParams(vmem_limit_bytes=room + (4 << 20)),
        cost_estimate=pl.CostEstimate(flops=flops, bytes_accessed=size, transcendentals=0),
    )(
        *[
            pltpu.with_memory_space_constraint(x, pltpu.HBM) if i in held else x
            for i, x in enumerate(ins)
        ]
    )


def begun(source, target, sem):
    copy = pltpu.make_async_copy(source, target, sem)
    copy.start()
    return copy


def packing(cells, per_cell, pad, turned=False):
    shape = (cells * per_cell, cells * pad)
    shape = shape[::-1] if turned else shape
    row = lax.broadcasted_iota(jnp.int32, shape, 1 if turned else 0)
    column = lax.broadcasted_iota(jnp.int32, shape, 0 if turned else 1)
    for w in range(1, cells):
        column = column - jnp.where(row >= w * per_cell, pad - per_cell, 0)
    return jnp.where(row == column, 1.0, 0.0).astype(bf16)


def swap(first, second, axis):
    count = lax.axis_size(axis)
    even = [(i, i + 1) for i in range(0, count - 1, 2)]
    odd = [(i, i + 1) for i in range(1, count - 1, 2)]
    return (
        lax.ppermute(first, axis, even + [(b, a) for a, b in even]),
        lax.ppermute(second, axis, odd + [(b, a) for a, b in odd]),
    )


def doubled(held, step):
    count = lax.axis_size("sub")
    return held + lax.ppermute(held, "sub", [(i, i ^ step) for i in range(count)])


def diagonal_of(stiffness, s, q, comps, layers, pad, columns):
    at = lax.broadcasted_iota(jnp.int32, (pad, layers), 0)
    layer = lax.broadcasted_iota(jnp.int32, (pad, layers), 1)
    column = jnp.zeros((pad, layers), f32)
    for c in range(comps):
        column = jnp.where(at == layer + c * layers, stiffness[s, q, c : c + 1, :], column)
    column = 6.0 + jnp.sum(column, axis=1, keepdims=True)
    return jnp.broadcast_to(column, (pad, columns))


def write_base(layers, begin, stiffness, field, base, shape, only=None):
    cells_s, cells_q, comps, pad, columns = shape
    at = lax.broadcasted_iota(jnp.int32, (pad, columns), 0)
    has_up, has_down = at < comps * layers, at < comps * layers
    for c in range(comps):
        has_up = has_up & (at != c * layers)
        has_down = has_down & (at != c * layers + layers - 1)
    for s in range(cells_s):
        for q in only or range(cells_q):
            i = s * cells_q + q
            x = field[i]
            diagonal = diagonal_of(stiffness, s, q, comps, layers, pad, columns)
            total = begin[i] - diagonal * x
            total = total + jnp.where(has_up, pltpu.roll(x, 1, 0), 0.0)
            total = total + jnp.where(has_down, pltpu.roll(x, pad - 1, 0), 0.0)
            if q > 0:
                total = total + field[i - 1]
            if q < cells_q - 1:
                total = total + field[i + 1]
            if s > 0:
                total = total + field[i - cells_q]
            if s < cells_s - 1:
                total = total + field[i + cells_q]
            base[i] = total


def write_column_messages(sol, base, first, second, shape):
    cells_s, cells_q = shape[:2]
    even = lax.axis_index(GROUP_AXES) % 2 == 0
    for out, q in (
        (first, jnp.where(even, cells_q - 1, 0)),
        (second, jnp.where(even, 0, cells_q - 1)),
    ):
        for s in range(cells_s):
            out[0, s] = base[s * cells_q + q].astype(bf16)
            out[1, s] = sol[s * cells_q + q].astype(bf16)


def unpack_cell(source, target, i, shape, layers):
    _, _, comps, pad, columns = shape
    for c in range(comps):
        target[i, c * layers : (c + 1) * layers, :] = source[:, c, :]
    target[i, comps * layers :, :] = jnp.zeros((pad - comps * layers, columns), f32)


def open_sides_kernel(
    shape, layers, start, rhs, stiffness, first, second, raw, raw_rhs, stiff, sol, begin, base, sems
):
    cells_s, cells_q = shape[:2]
    sides = (0, cells_q - 1)
    near = (0, 1, cells_q - 2, cells_q - 1)
    copies = [
        begun(stiffness, stiff, sems.at[0]),
        begun(start.at[:, pl.ds(0, 2)], raw.at[:, pl.ds(0, 2)], sems.at[1]),
        begun(start.at[:, pl.ds(cells_q - 2, 2)], raw.at[:, pl.ds(2, 2)], sems.at[2]),
        begun(rhs.at[:, pl.ds(0, 1)], raw_rhs.at[:, pl.ds(0, 1)], sems.at[3]),
        begun(rhs.at[:, pl.ds(cells_q - 1, 1)], raw_rhs.at[:, pl.ds(1, 1)], sems.at[4]),
    ]
    for copy in copies:
        copy.wait()
    for s in range(cells_s):
        for k, q in enumerate(near):
            unpack_cell(raw.at[s, k], sol, s * cells_q + q, shape, layers)
        for k, q in enumerate(sides):
            unpack_cell(raw_rhs.at[s, k], begin, s * cells_q + q, shape, layers)
    write_base(layers, begin, stiff, sol, base, shape, sides)
    write_column_messages(sol, base, first, second, shape)


def open_kernel(
    shape, layers, start, rhs, stiffness, offsets, sol, base, sent, raw, raw_rhs, stiff, own, begin, sems
):
    cells_s, cells_q = shape[:2]
    sources, targets = (stiffness, offsets, start, rhs), (stiff, own, raw, raw_rhs)
    copies = [begun(a, b, sems.at[k]) for k, (a, b) in enumerate(zip(sources, targets))]
    for copy in copies:
        copy.wait()
    group = lax.broadcasted_iota(jnp.int32, sent.shape, 0)
    sent[...] = jnp.where(group == lax.axis_index("sub"), own[...], 0)
    for s in range(cells_s):
        for q in range(cells_q):
            unpack_cell(raw.at[s, q], sol, s * cells_q + q, shape, layers)
            unpack_cell(raw_rhs.at[s, q], begin, s * cells_q + q, shape, layers)
    write_base(layers, begin, stiff, sol, base, shape)


def column_sides(first, second):
    even = lax.axis_index(GROUP_AXES) % 2 == 0

    def low(kind, s):
        return jnp.where(even, second[kind, s].astype(f32), first[kind, s].astype(f32))

    def high(kind, s):
        return jnp.where(even, first[kind, s].astype(f32), second[kind, s].astype(f32))

    return low, high


def edge_cells(low, high, sol, s, cells_q):
    col, cols = lax.axis_index(GROUP_AXES), lax.axis_size(GROUP_AXES)
    left = jnp.where(col > 0, low(0, s) + sol[s * cells_q], 0.0)
    right = jnp.where(col < cols - 1, high(0, s) + sol[s * cells_q + cells_q - 1], 0.0)
    return left, right


def row_kernel(shape, sol, base, first_in, second_in, first, second):
    cells_s, cells_q = shape[:2]
    low, high = column_sides(first_in, second_in)
    even = lax.axis_index("sub") % 2 == 0
    for out, s in (
        (first, jnp.where(even, cells_s - 1, 0)),
        (second, jnp.where(even, 0, cells_s - 1)),
    ):
        left, right = edge_cells(low, high, sol, s, cells_q)
        out[0, 0] = left.astype(bf16)
        out[0, cells_q + 1] = right.astype(bf16)
        low_s, high_s = low(1, s), high(1, s)
        out[1, 0] = low_s.astype(bf16)
        out[1, cells_q + 1] = high_s.astype(bf16)
        for q in range(cells_q):
            value = base[s * cells_q + q]
            if q == 0:
                value = value + low_s
            if q == cells_q - 1:
                value = value + high_s
            out[0, q + 1] = value.astype(bf16)
            out[1, q + 1] = sol[s * cells_q + q].astype(bf16)


def side_of(member):
    return (member // PARTNER) % 2


def middle_window_kernel(
    shape, sol, base, first_q, second_q, basis_t, local_kept, product, local, sems
):
    cells_s, cells_q, _, pad, columns = shape
    wide = cells_q + 2
    low, high = column_sides(first_q, second_q)
    copies = []
    for s in range(1, cells_s - 1):
        left, right = edge_cells(low, high, sol, s, cells_q)
        values = [left] + [base[s * cells_q + q] for q in range(cells_q)] + [right]
        values[1] = values[1] + low(1, s)
        values[cells_q] = values[cells_q] + high(1, s)
        for w in range(wide):
            local[(s - 1) * wide + w] = values[w].astype(bf16)
        part, there = pl.ds((s - 1) * wide, wide), pl.ds((s + 1) * wide, wide)
        copies.append(begun(local.at[part], local_kept.at[there], sems.at[len(copies)]))
    chunk = wide * pad
    product[...] = jnp.dot(
        basis_t[:, 2 * chunk : cells_s * chunk],
        local[...].reshape(-1, columns),
        preferred_element_type=f32,
    )
    for copy in copies:
        copy.wait()


def window_kernel(
    shape,
    sol,
    base,
    first_q,
    second_q,
    first_s,
    second_s,
    basis_t,
    message,
    local_kept,
    local,
    restricted,
    sems,
):
    cells_s, cells_q, _, pad, columns = shape
    wide = cells_q + 2
    low, high = column_sides(first_q, second_q)
    row, rows = lax.axis_index("sub"), lax.axis_size("sub")
    even = row % 2 == 0

    def above(kind, w):
        return jnp.where(even, second_s[kind, w].astype(f32), first_s[kind, w].astype(f32))

    def below(kind, w):
        return jnp.where(even, first_s[kind, w].astype(f32), second_s[kind, w].astype(f32))

    copies = []
    for s in range(cells_s):
        left, right = edge_cells(low, high, sol, s, cells_q)
        values = [left] + [base[s * cells_q + q] for q in range(cells_q)] + [right]
        values[1] = values[1] + low(1, s)
        values[cells_q] = values[cells_q] + high(1, s)
        for w in range(wide):
            value = values[w]
            if s == 0:
                value = value + above(1, w)
            if s == cells_s - 1:
                value = value + below(1, w)
            local[(s + 1) * wide + w] = value.astype(bf16)
        part = pl.ds((s + 1) * wide, wide)
        copies.append(begun(local.at[part], local_kept.at[part], sems.at[len(copies)]))
    for s, side, place, there in (
        (0, above, 0, row > 0),
        (cells_s - 1, below, (cells_s + 1) * wide, row < rows - 1),
    ):
        near = [low(1, s)] + [sol[s * cells_q + q] for q in range(cells_q)] + [high(1, s)]
        for w in range(wide):
            local[place + w] = jnp.where(there, side(0, w) + near[w], 0.0).astype(bf16)
        part = pl.ds(place, wide)
        copies.append(begun(local.at[part], local_kept.at[part], sems.at[len(copies)]))
    product = jnp.dot(
        basis_t[...], local[...].reshape(-1, columns), preferred_element_type=f32
    ).astype(bf16)
    half = columns // 2
    for k in range(2):
        restricted[k] = product[:, k * half : (k + 1) * half]
    for j in range(message.shape[0]):
        copies.append(begun(restricted.at[side_of(j)], message.at[j], sems.at[len(copies)]))
    for copy in copies:
        copy.wait()


def outer_window_kernel(
    shape,
    sol,
    base,
    first_q,
    second_q,
    first_s,
    second_s,
    basis_t,
    middle,
    begun_kept,
    message,
    local_kept,
    local,
    restricted,
    sems,
):
    cells_s, cells_q, _, pad, columns = shape
    wide = cells_q + 2
    low, high = column_sides(first_q, second_q)
    row, rows = lax.axis_index("sub"), lax.axis_size("sub")
    even = row % 2 == 0

    def above(kind, w):
        return jnp.where(even, second_s[kind, w].astype(f32), first_s[kind, w].astype(f32))

    def below(kind, w):
        return jnp.where(even, first_s[kind, w].astype(f32), second_s[kind, w].astype(f32))

    copies = []
    for s in (0, cells_s - 1):
        left, right = edge_cells(low, high, sol, s, cells_q)
        values = [left] + [base[s * cells_q + q] for q in range(cells_q)] + [right]
        values[1] = values[1] + low(1, s)
        values[cells_q] = values[cells_q] + high(1, s)
        for w in range(wide):
            value = values[w]
            if s == 0:
                value = value + above(1, w)
            if s == cells_s - 1:
                value = value + below(1, w)
            local[(s + 1) * wide + w] = value.astype(bf16)
        part = pl.ds((s + 1) * wide, wide)
        copies.append(begun(local.at[part], local_kept.at[part], sems.at[len(copies)]))
    for s, side, place, there in (
        (0, above, 0, row > 0),
        (cells_s - 1, below, (cells_s + 1) * wide, row < rows - 1),
    ):
        near = [low(1, s)] + [sol[s * cells_q + q] for q in range(cells_q)] + [high(1, s)]
        for w in range(wide):
            local[place + w] = jnp.where(there, side(0, w) + near[w], 0.0).astype(bf16)
        part = pl.ds(place, wide)
        copies.append(begun(local.at[part], local_kept.at[part], sems.at[len(copies)]))
    chunk = wide * pad
    product = middle[...]
    for r in (0, cells_s):
        product = product + jnp.dot(
            basis_t[:, r * chunk : (r + 2) * chunk],
            local[r * wide : (r + 2) * wide].reshape(-1, columns),
            preferred_element_type=f32,
        )
    product = product.astype(bf16)
    half = columns // 2
    for k in range(2):
        restricted[k] = product[:, k * half : (k + 1) * half]
    for j in range(message.shape[0]):
        copies.append(begun(restricted.at[side_of(j)], message.at[j], sems.at[len(copies)]))
    for copy in copies:
        copy.wait()


def terms_kernel(spread, gathered, out, kept, sem):
    kept[...] = jnp.dot(spread[...], gathered[...], preferred_element_type=f32).astype(bf16)
    begun(kept, out, sem).wait()


def fine_kernel(shape, layers, steps, last, local_kept, inverse_kept, sol_kept, *refs):
    cells_s, cells_q, comps, pad, columns = shape
    if last:
        out, local, inverse, packed, sol, fine, sems = refs
        fields = ((sol_kept, sol),)
    else:
        base_kept, stiffness, out, base_out, local, inverse, packed, sol, fine, base, sems = refs
        fields = ((sol_kept, sol), (base_kept, base))
    per_cell = comps * layers
    wide = cells_q + 2
    span, chunk = wide * per_cell, wide * pad
    size = cells_s // steps
    loaded = begun(local_kept, local, sems.at[0])
    arriving = [
        begun(
            inverse_kept.at[0, pl.ds((k * size + 1) * span, size * span)],
            inverse.at[pl.ds(k * size * span, size * span)],
            sems.at[k + 1],
        )
        for k in range(steps)
    ]
    others = [begun(a, b, sems.at[steps + 1 + k]) for k, (a, b) in enumerate(fields)]
    pack = packing(wide, per_cell, pad)
    loaded.wait()
    for s in range(packed.shape[0] // span):
        part = local[s * wide : (s + 1) * wide].reshape(chunk, columns)
        packed[s * span : (s + 1) * span, :] = jnp.dot(
            pack, part, preferred_element_type=f32
        ).astype(bf16)
    for k in range(steps):
        arriving[k].wait()
        rows = jnp.dot(
            inverse[k * size * span : (k + 1) * size * span, :],
            packed[...],
            preferred_element_type=f32,
        )
        for s in range(size):
            for q in range(cells_q):
                i = (k * size + s) * cells_q + q
                first = s * span + (q + 1) * per_cell
                fine[i, :per_cell, :] = rows[first : first + per_cell]
                fine[i, per_cell:, :] = jnp.zeros((pad - per_cell, columns), f32)
    for copy in others:
        copy.wait()
    for i in range(fine.shape[0]):
        sol[i] = sol[i] + fine[i]
    copies = [begun(sol, out, sems.at[steps + 3])]
    if not last:
        write_base(layers, base, stiffness, fine, base, shape)
        copies.append(begun(base, base_out, sems.at[steps + 4]))
    for copy in copies:
        copy.wait()


def fine_product(shape, layers, local, sub_inverse, sol, base, stiffness, last):
    cells_s, cells_q, comps, pad, columns = shape
    width = sub_inverse.shape[2]
    rows = cells_s * (cells_q + 2) * comps * layers
    steps = 3 if cells_s % 3 == 0 else 1
    kept = pltpu.HBM((cells_s * cells_q, pad, columns), f32)
    field = pltpu.VMEM(kept.shape, f32)
    return call(
        functools.partial(fine_kernel, shape, layers, steps, last),
        (local, sub_inverse, sol) if last else (local, sub_inverse, sol, base, stiffness),
        (kept,) if last else (kept, kept),
        scratch=(
            pltpu.VMEM(local.shape, bf16),
            pltpu.VMEM((rows, width), bf16),
            pltpu.VMEM((width, columns), bf16),
        )
        + ((field, field) if last else (field, field, field))
        + (pltpu.SemaphoreType.DMA((steps + 5,)),),
        flops=2 * rows * width * columns,
        held=(0, 1, 2) if last else (0, 1, 2, 3),
    )


def coarse_values(arrived, depth):
    sums = []
    for c in range(arrived.shape[1]):
        total = arrived[0, c].astype(f32)
        for h in range(1, arrived.shape[0]):
            total = total + arrived[h, c].astype(f32)
        sums.append(total)
    rows = []
    for m in range(arrived.shape[1]):
        part = slice(side_of(m) * depth, (side_of(m) + 1) * depth)
        low = m - side_of(m) * PARTNER
        rows.append(jnp.concatenate([sums[low][part], sums[low + PARTNER][part]], axis=1))
    return jnp.concatenate(rows, axis=0).astype(bf16)


def step_sides_kernel(
    shape,
    layers,
    arrived,
    basis_kept,
    sol_kept,
    base_kept,
    stiffness,
    first,
    second,
    coarse,
    basis_p,
    stiff,
    sol,
    begin,
    base,
    sems,
):
    cells_s, cells_q, _, pad, columns = shape
    sides = (0, cells_q - 1)
    copies = [begun(basis_kept, basis_p, sems.at[0]), begun(stiffness, stiff, sems.at[1])]
    for q in sides:
        copies.append(begun(sol_kept.at[:, q], sol.at[:, q], sems.at[len(copies)]))
        copies.append(begun(base_kept.at[:, q], begin.at[:, q], sems.at[len(copies)]))
    sol, begin = (x.reshape(cells_s * cells_q, pad, columns) for x in (sol, begin))
    chosen = coarse_values(arrived, arrived.shape[2] // 2)
    copies[0].wait()
    span = cells_q * pad
    for s in range(cells_s):
        rows = jnp.dot(
            basis_p[s * span : (s + 1) * span, :], chosen, preferred_element_type=f32
        )
        coarse[s * cells_q : (s + 1) * cells_q] = rows.reshape(cells_q, pad, columns)
    for copy in copies[1:]:
        copy.wait()
    for s in range(cells_s):
        for q in sides:
            i = s * cells_q + q
            sol[i] = sol[i] + coarse[i]
    write_base(layers, begin, stiff, coarse, base, shape, sides)
    write_column_messages(sol, base, first, second, shape)


def step_kernel(shape, layers, coarse, sol_kept, base_kept, stiffness, new, base, stiff, begin, sems):
    sources, targets = (stiffness, sol_kept, base_kept), (stiff, new, begin)
    copies = [begun(a, b, sems.at[k]) for k, (a, b) in enumerate(zip(sources, targets))]
    for copy in copies:
        copy.wait()
    for i in range(new.shape[0]):
        new[i] = new[i] + coarse[i]
    write_base(layers, begin, stiff, coarse, base, shape)


def close_kernel(
    shape, layers, arrived, basis_kept, sol_kept, out_kept, basis_p, sol, out, sems
):
    cells_s, cells_q, comps, pad, columns = shape
    span = cells_q * pad
    copies = [begun(basis_kept, basis_p, sems.at[0])]
    for s in range(cells_s):
        part = pl.ds(s * cells_q, cells_q)
        copies.append(begun(sol_kept.at[part], sol.at[part], sems.at[s + 1]))
    chosen = coarse_values(arrived, arrived.shape[2] // 2)
    copies[0].wait()
    results = []
    for s in range(cells_s):
        rows = jnp.dot(
            basis_p[s * span : (s + 1) * span, :], chosen, preferred_element_type=f32
        )
        copies[s + 1].wait()
        for q in range(cells_q):
            total = sol[s * cells_q + q] + rows[q * pad : (q + 1) * pad]
            for c in range(comps):
                out[s, q, :, c, :] = total[c * layers : (c + 1) * layers]
        results.append(begun(out.at[s], out_kept.at[s], sems.at[cells_s + 1 + s]))
    for copy in results:
        copy.wait()


def places(offsets, g, j, groups, depth, kgroup):
    first = offsets[g, j]
    end = kgroup if j == groups - 1 else offsets[g, j + 1]
    shape = (1, groups * depth)
    at = lax.broadcasted_iota(jnp.int32, shape, 1)
    turn = at
    member = jnp.zeros(shape, jnp.int32)
    for m in range(1, groups):
        member = member + jnp.where(at >= m * depth, 1, 0)
        turn = turn - jnp.where(at >= m * depth, depth, 0)
    shifted = member - lax.rem(first, groups)
    shifted = jnp.where(shifted < 0, shifted + groups, shifted)
    place = shifted + turn * groups
    return first, place, place < end - first


def ordering(dims, offsets):
    groups, depth, kgroup, count = dims
    member = lax.axis_index(GROUP_AXES)
    wanted = jnp.full((1, groups * depth), -1, jnp.int32)
    for j in range(groups):
        _, place, valid = places(offsets, 0, j, groups, depth, kgroup)
        wanted = jnp.where(valid & (member == j), place, wanted)
    row = lax.broadcasted_iota(jnp.int32, (count, groups * depth), 0)
    return jnp.where(row == wanted, 1.0, 0.0).astype(bf16)


def basis_kernel(cell, dims, offsets, basis_kept, basis_t, turned_kept, own_kept, basis, own, sems):
    wide, per_cell, pad = cell
    span, chunk = wide * per_cell, wide * pad
    size = chunk - 2 * pad
    copy = begun(basis_kept.at[0], basis, sems.at[0])
    pack = packing(wide, per_cell, pad)
    pack_own = packing(wide, per_cell, pad, True)[pad : pad + size]
    order = ordering(dims, offsets)
    rows = basis.shape[0] // span
    copy.wait()
    for s in range(rows):
        ordered = jnp.dot(
            basis[s * span : (s + 1) * span, :], order, preferred_element_type=f32
        ).astype(bf16)
        basis_t[:, s * chunk : (s + 1) * chunk] = lax.dot_general(
            ordered, pack, (((0,), (0,)), ((), ())), preferred_element_type=f32
        ).astype(bf16)
        if 0 < s < rows - 1:
            own[(s - 1) * size : s * size, :] = jnp.dot(
                pack_own, ordered, preferred_element_type=f32
            ).astype(bf16)
    copies = [begun(basis_t, turned_kept, sems.at[1]), begun(own, own_kept, sems.at[2])]
    for copy in copies:
        copy.wait()


def ordered_basis(cell, dims, offsets, basis, turned, own):
    return pl.pallas_call(
        functools.partial(basis_kernel, cell, dims),
        out_shape=(jax.ShapeDtypeStruct(turned, bf16), pltpu.HBM(turned, bf16), pltpu.HBM(own, bf16)),
        in_specs=[pl.BlockSpec(memory_space=pltpu.SMEM), HBM],
        out_specs=(VMEM, HBM, HBM),
        scratch_shapes=[
            pltpu.VMEM(basis.shape[1:], bf16),
            pltpu.VMEM(own, bf16),
            pltpu.SemaphoreType.DMA((3,)),
        ],
        compiler_params=pltpu.CompilerParams(vmem_limit_bytes=12 << 20),
        cost_estimate=pl.CostEstimate(
            flops=6 * turned[0] * turned[1] * cell[0] * cell[2],
            bytes_accessed=6 * basis.size,
            transcendentals=0,
        ),
    )(offsets, pltpu.with_memory_space_constraint(basis, pltpu.HBM))


def first_index(first, member, groups):
    if groups & (groups - 1) == 0:
        return lax.shift_right_logical(first - member + groups - 1, groups.bit_length() - 1)
    return lax.div(first - member + groups - 1, groups)


def spread_kernel(dims, every, inverse_kept, partner_kept, out_kept, inverse, columns, picked, out, sems):
    groups, depth, kgroup = dims
    coarse = groups * depth
    member = lax.axis_index(GROUP_AXES)
    own = lax.axis_index("sub")
    side = side_of(member)
    copies = [
        begun(inverse_kept, inverse.at[side], sems.at[0]),
        begun(partner_kept, inverse.at[1 - side], sems.at[1]),
    ]
    slot = lax.broadcasted_iota(jnp.int32, (kgroup, coarse), 0)
    for j in range(groups):
        first, place, valid = places(every, own, j, groups, depth, kgroup)
        wanted = jnp.where(valid, place + first, -1)
        columns[:, j * coarse : (j + 1) * coarse] = jnp.where(slot == wanted, 1.0, 0.0).astype(bf16)
    _, n_sub, rows, _ = inverse.shape
    turn = lax.broadcasted_iota(jnp.int32, (depth, rows), 0)
    index = lax.broadcasted_iota(jnp.int32, (depth, rows), 1)
    for copy in copies:
        copy.wait()
    span = 2 * coarse
    steps = max(n_sub // 4, 1)
    size = n_sub // steps

    def some(k, _):
        for t in range(size):
            g = k * size + t
            for b in range(2):
                m = member + (b - side) * PARTNER
                picks = []
                for j in range(groups):
                    first = every[g, j]
                    end = kgroup if j == groups - 1 else every[g, j + 1]
                    begin = first_index(first, m, groups)
                    wanted = (index == turn + begin) & (index * groups + m < end)
                    picks.append(jnp.where(wanted, 1.0, 0.0).astype(bf16))
                part = jnp.dot(
                    jnp.concatenate(picks, axis=0), inverse[b, g], preferred_element_type=f32
                ).astype(bf16)
                for j in range(groups):
                    at = t * span + (2 * j + b) * depth
                    picked[at : at + depth, :] = part[j * depth : (j + 1) * depth]
        results = []
        for t in range(size):
            part = pl.ds(t * span, span)
            out[part, :] = jnp.dot(
                picked[part, :], columns[...], preferred_element_type=f32
            ).astype(bf16)
            there = pl.ds((k * size + t) * span, span)
            results.append(begun(out.at[part], out_kept.at[there], sems.at[2 + t]))
        for copy in results:
            copy.wait()
        return 0

    lax.fori_loop(0, steps, some, 0)


def spread_inverse(every, coarse_inverse, partner, depth):
    n_sub, share_rows, kgroup = coarse_inverse.shape
    groups = every.shape[1]
    coarse = groups * depth
    rows = n_sub * 2 * coarse
    part = rows // max(n_sub // 4, 1)
    return pl.pallas_call(
        functools.partial(spread_kernel, (groups, depth, kgroup)),
        out_shape=pltpu.HBM((rows, groups * coarse), bf16),
        in_specs=[pl.BlockSpec(memory_space=pltpu.SMEM), HBM, HBM],
        out_specs=HBM,
        scratch_shapes=[
            pltpu.VMEM((2,) + coarse_inverse.shape, bf16),
            pltpu.VMEM((kgroup, groups * coarse), bf16),
            pltpu.VMEM((part, kgroup), bf16),
            pltpu.VMEM((part, groups * coarse), bf16),
            pltpu.SemaphoreType.DMA((2 + part // (2 * coarse),)),
        ],
        compiler_params=pltpu.CompilerParams(
            vmem_limit_bytes=(16 << 20) + 4 * coarse_inverse.size + 8 * part * groups * coarse
        ),
        cost_estimate=pl.CostEstimate(
            flops=2 * rows * groups * coarse * kgroup,
            bytes_accessed=2 * rows * groups * coarse,
            transcendentals=0,
        ),
    )(
        every,
        pltpu.with_memory_space_constraint(coarse_inverse, pltpu.HBM),
        pltpu.with_memory_space_constraint(partner, pltpu.HBM),
    )


def shards(rhs, start, stiffness, sub_inverse, basis, coarse_inverse, offsets):
    cells_s, cells_q, comps, layers, columns = rhs.shape
    n_sub, _, kgroup = coarse_inverse.shape
    groups = offsets.shape[1]
    depth = -(-basis.shape[2] // groups)
    coarse = groups * depth
    cells = cells_s * cells_q
    per_cell = comps * layers
    pad = -(-per_cell // 16) * 16
    wide = cells_q + 2
    shape = (cells_s, cells_q, comps, pad, columns)

    field = jax.ShapeDtypeStruct((cells, pad, columns), f32)
    column_message = jax.ShapeDtypeStruct((2, cells_s, pad, columns), bf16)
    row_message = jax.ShapeDtypeStruct((2, wide, pad, columns), bf16)

    rows = (cells_s + 2) * wide * pad

    start_cells, rhs_cells = (x.transpose(0, 1, 3, 2, 4) for x in (start, rhs))
    tail = (layers, comps, columns)
    first, second = call(
        functools.partial(open_sides_kernel, shape, layers),
        (start_cells, rhs_cells, stiffness),
        (column_message, column_message),
        scratch=(
            pltpu.VMEM((cells_s, 4) + tail, f32),
            pltpu.VMEM((cells_s, 2) + tail, f32),
            pltpu.VMEM(stiffness.shape, f32),
            pltpu.VMEM(field.shape, f32),
            pltpu.VMEM(field.shape, f32),
            pltpu.VMEM(field.shape, f32),
            pltpu.SemaphoreType.DMA((5,)),
        ),
        held=(0, 1, 2),
    )
    solution, base, sent = call(
        functools.partial(open_kernel, shape, layers),
        (start_cells, rhs_cells, stiffness, offsets),
        (field, field, jax.ShapeDtypeStruct((n_sub, groups), jnp.int32)),
        scratch=(
            pltpu.VMEM((cells_s, cells_q) + tail, f32),
            pltpu.VMEM((cells_s, cells_q) + tail, f32),
            pltpu.VMEM(stiffness.shape, f32),
            pltpu.VMEM(offsets.shape, jnp.int32),
            pltpu.VMEM(field.shape, f32),
            pltpu.SemaphoreType.DMA((4,)),
        ),
        held=(0, 1, 2, 3),
    )
    cell = (wide, per_cell, pad)
    dims = (groups, depth, kgroup, basis.shape[2])
    basis_t = basis_kept = basis_p = every = spread = None

    for sweep in range(ITERS):
        last = sweep == ITERS - 1
        first_q, second_q = swap(first, second, GROUP_AXES)
        if sweep == 0:
            every = sent
            rounds = (n_sub - 1).bit_length()
            for power in range(rounds - 1):
                every = doubled(every, 1 << power)
            first_q, second_q, every = lax.optimization_barrier((first_q, second_q, every))
        first, second = call(
            functools.partial(row_kernel, shape),
            (solution, base, first_q, second_q),
            (row_message, row_message),
        )
        first_s, second_s = swap(first, second, "sub")
        if sweep == 0:
            later, _ = lax.optimization_barrier((basis, first))
            basis_t, basis_kept, basis_p = ordered_basis(
                cell, dims, offsets, later, (coarse, rows), (cells * pad, coarse)
            )
            shared, _ = lax.optimization_barrier((coarse_inverse, first))
            pairs = [(i, i ^ PARTNER) for i in range(groups)]
            partner = lax.ppermute(shared, GROUP_AXES, pairs)
            every = doubled(every, 1 << (rounds - 1))
            first_s, second_s, every = lax.optimization_barrier((first_s, second_s, every))
        if last:
            begun_kept, middle = call(
                functools.partial(middle_window_kernel, shape),
                (solution, base, first_q, second_q, basis_kept),
                (
                    pltpu.HBM(((cells_s + 2) * wide, pad, columns), bf16),
                    jax.ShapeDtypeStruct((coarse, columns), f32),
                ),
                scratch=(
                    pltpu.VMEM(((cells_s - 2) * wide, pad, columns), bf16),
                    pltpu.SemaphoreType.DMA((cells_s - 2,)),
                ),
                flops=rows * coarse * columns,
            )
            message, local = call(
                functools.partial(outer_window_kernel, shape),
                (solution, base, first_q, second_q, first_s, second_s, basis_kept, middle, begun_kept),
                (
                    pltpu.HBM((groups, coarse, columns // 2), bf16),
                    pltpu.HBM(((cells_s + 2) * wide, pad, columns), bf16),
                ),
                scratch=(
                    pltpu.VMEM(((cells_s + 2) * wide, pad, columns), bf16),
                    pltpu.VMEM((2, coarse, columns // 2), bf16),
                    pltpu.SemaphoreType.DMA((groups + cells_s + 2,)),
                ),
                flops=rows * coarse * columns,
                held=(8,),
                aliases={8: 1},
            )
        else:
            message, local = call(
                functools.partial(window_kernel, shape),
                (solution, base, first_q, second_q, first_s, second_s, basis_t if sweep == 0 else basis_kept),
                (
                    pltpu.HBM((groups, coarse, columns // 2), bf16),
                    pltpu.HBM(((cells_s + 2) * wide, pad, columns), bf16),
                ),
                scratch=(
                    pltpu.VMEM(((cells_s + 2) * wide, pad, columns), bf16),
                    pltpu.VMEM((2, coarse, columns // 2), bf16),
                    pltpu.SemaphoreType.DMA((groups + cells_s + 2,)),
                ),
                flops=2 * rows * coarse * columns,
            )
        if sweep == 0:
            waited, _ = lax.optimization_barrier((every, message))
            spread = spread_inverse(waited, coarse_inverse, partner, depth)
        gathered = lax.all_to_all(message, GROUP_AXES, 0, 0, tiled=True)
        held = pltpu.VMEM((spread.shape[0], columns // 2), bf16)
        (terms,) = call(
            terms_kernel,
            (spread, gathered.reshape(-1, columns // 2)),
            (pltpu.HBM(held.shape, bf16),),
            scratch=(held, pltpu.SemaphoreType.DMA),
            flops=2 * spread.size * columns // 2,
        )
        arrived = lax.all_to_all(
            terms.reshape(n_sub * groups, 2 * depth, columns // 2), ALL_AXES, 0, 0, tiled=True
        ).reshape(n_sub, groups, 2 * depth, columns // 2)
        kept = fine_product(
            shape, layers, local, sub_inverse, solution, base, stiffness, last
        )
        if last:
            (out,) = call(
                functools.partial(close_kernel, shape, layers),
                (arrived, basis_p, *kept),
                (pltpu.HBM((cells_s, cells_q) + tail, f32),),
                scratch=(
                    pltpu.VMEM(basis_p.shape, bf16),
                    pltpu.VMEM(field.shape, f32),
                    pltpu.VMEM((cells_s, cells_q) + tail, f32),
                    pltpu.SemaphoreType.DMA((2 * cells_s + 1,)),
                ),
                held=(1, 2),
            )
        else:
            first, second, change = call(
                functools.partial(step_sides_kernel, shape, layers),
                (
                    arrived,
                    basis_p,
                    *(x.reshape(cells_s, cells_q, pad, columns) for x in kept),
                    stiffness,
                ),
                (column_message, column_message, field),
                scratch=(
                    pltpu.VMEM(basis_p.shape, bf16),
                    pltpu.VMEM(stiffness.shape, f32),
                    pltpu.VMEM((cells_s, cells_q, pad, columns), f32),
                    pltpu.VMEM((cells_s, cells_q, pad, columns), f32),
                    pltpu.VMEM(field.shape, f32),
                    pltpu.SemaphoreType.DMA((6,)),
                ),
                held=(1, 2, 3, 4),
            )
            solution, base = call(
                functools.partial(step_kernel, shape, layers),
                (change, *kept, stiffness),
                (field, field),
                scratch=(
                    pltpu.VMEM(stiffness.shape, f32),
                    pltpu.VMEM(field.shape, f32),
                    pltpu.SemaphoreType.DMA((3,)),
                ),
                held=(1, 2, 3),
            )
    return out.transpose(0, 1, 3, 2, 4)


def solution(mesh):
    return jax.shard_map(
        shards,
        mesh=mesh,
        in_specs=(
            P("sub", ("crow", "ccol"), None, None, None),
            P("sub", ("crow", "ccol"), None, None, None),
            P("sub", ("crow", "ccol"), None, None),
            P(("sub", "crow", "ccol"), None, None),
            P(("sub", "crow", "ccol"), None, None),
            P(None, ("crow", "ccol"), "sub"),
            P("sub", None),
        ),
        out_specs=P("sub", ("crow", "ccol"), None, None, None),
        check_vma=False,
    )
```

```python
import functools
import math

import jax
import jax.numpy as jnp
from jax import lax
from jax.experimental import pallas as pl
from jax.experimental.pallas import tpu as pltpu
from jax.sharding import PartitionSpec as P

ITERS = 2
PARTNER = 2
GROUP_AXES = ("crow", "ccol")
ALL_AXES = ("sub", "crow", "ccol")
bf16, f32 = jnp.bfloat16, jnp.float32
VMEM = pl.BlockSpec(memory_space=pltpu.VMEM)
HBM = pl.BlockSpec(memory_space=pltpu.HBM)


def sized(x):
    return math.prod(x.shape) * jnp.dtype(x.dtype).itemsize


def call(body, ins, outs, scratch=(), flops=0, held=(), aliases=None):
    size = sum(sized(x) for x in (*ins, *outs))
    room = size + sum(sized(x) for x in scratch if getattr(x, "dtype", None) in (bf16, f32))
    return pl.pallas_call(
        body,
        out_shape=tuple(outs),
        in_specs=[HBM if i in held else VMEM for i in range(len(ins))],
        out_specs=tuple(
            HBM if getattr(x, "memory_space", None) == pltpu.HBM else VMEM for x in outs
        ),
        scratch_shapes=list(scratch),
        input_output_aliases=aliases or {},
        compiler_params=pltpu.CompilerParams(vmem_limit_bytes=room + (4 << 20)),
        cost_estimate=pl.CostEstimate(flops=flops, bytes_accessed=size, transcendentals=0),
    )(
        *[
            pltpu.with_memory_space_constraint(x, pltpu.HBM) if i in held else x
            for i, x in enumerate(ins)
        ]
    )


def begun(source, target, sem):
    copy = pltpu.make_async_copy(source, target, sem)
    copy.start()
    return copy


def packing(cells, per_cell, pad, turned=False):
    shape = (cells * per_cell, cells * pad)
    shape = shape[::-1] if turned else shape
    row = lax.broadcasted_iota(jnp.int32, shape, 1 if turned else 0)
    column = lax.broadcasted_iota(jnp.int32, shape, 0 if turned else 1)
    for w in range(1, cells):
        column = column - jnp.where(row >= w * per_cell, pad - per_cell, 0)
    return jnp.where(row == column, 1.0, 0.0).astype(bf16)


def swap(first, second, axis):
    count = lax.axis_size(axis)
    even = [(i, i + 1) for i in range(0, count - 1, 2)]
    odd = [(i, i + 1) for i in range(1, count - 1, 2)]
    return (
        lax.ppermute(first, axis, even + [(b, a) for a, b in even]),
        lax.ppermute(second, axis, odd + [(b, a) for a, b in odd]),
    )


def doubled(held, step):
    count = lax.axis_size("sub")
    return held + lax.ppermute(held, "sub", [(i, i ^ step) for i in range(count)])


def diagonal_of(stiffness, s, q, comps, layers, pad, columns):
    at = lax.broadcasted_iota(jnp.int32, (pad, layers), 0)
    layer = lax.broadcasted_iota(jnp.int32, (pad, layers), 1)
    column = jnp.zeros((pad, layers), f32)
    for c in range(comps):
        column = jnp.where(at == layer + c * layers, stiffness[s, q, c : c + 1, :], column)
    column = 6.0 + jnp.sum(column, axis=1, keepdims=True)
    return jnp.broadcast_to(column, (pad, columns))


def write_base(layers, begin, stiffness, field, base, shape, only=None):
    cells_s, cells_q, comps, pad, columns = shape
    at = lax.broadcasted_iota(jnp.int32, (pad, columns), 0)
    has_up, has_down = at < comps * layers, at < comps * layers
    for c in range(comps):
        has_up = has_up & (at != c * layers)
        has_down = has_down & (at != c * layers + layers - 1)
    for s in range(cells_s):
        for q in only or range(cells_q):
            i = s * cells_q + q
            x = field[i]
            diagonal = diagonal_of(stiffness, s, q, comps, layers, pad, columns)
            total = begin[i] - diagonal * x
            total = total + jnp.where(has_up, pltpu.roll(x, 1, 0), 0.0)
            total = total + jnp.where(has_down, pltpu.roll(x, pad - 1, 0), 0.0)
            if q > 0:
                total = total + field[i - 1]
            if q < cells_q - 1:
                total = total + field[i + 1]
            if s > 0:
                total = total + field[i - cells_q]
            if s < cells_s - 1:
                total = total + field[i + cells_q]
            base[i] = total


def write_column_messages(sol, base, first, second, shape):
    cells_s, cells_q = shape[:2]
    even = lax.axis_index(GROUP_AXES) % 2 == 0
    for out, q in (
        (first, jnp.where(even, cells_q - 1, 0)),
        (second, jnp.where(even, 0, cells_q - 1)),
    ):
        for s in range(cells_s):
            out[0, s] = base[s * cells_q + q].astype(bf16)
            out[1, s] = sol[s * cells_q + q].astype(bf16)


def unpack_cell(source, target, i, shape, layers):
    _, _, comps, pad, columns = shape
    for c in range(comps):
        target[i, c * layers : (c + 1) * layers, :] = source[:, c, :]
    target[i, comps * layers :, :] = jnp.zeros((pad - comps * layers, columns), f32)


def open_sides_kernel(
    shape, layers, start, rhs, stiffness, first, second, raw, raw_rhs, stiff, sol, begin, base, sems
):
    cells_s, cells_q = shape[:2]
    sides = (0, cells_q - 1)
    near = (0, 1, cells_q - 2, cells_q - 1)
    copies = [
        begun(stiffness, stiff, sems.at[0]),
        begun(start.at[:, pl.ds(0, 2)], raw.at[:, pl.ds(0, 2)], sems.at[1]),
        begun(start.at[:, pl.ds(cells_q - 2, 2)], raw.at[:, pl.ds(2, 2)], sems.at[2]),
        begun(rhs.at[:, pl.ds(0, 1)], raw_rhs.at[:, pl.ds(0, 1)], sems.at[3]),
        begun(rhs.at[:, pl.ds(cells_q - 1, 1)], raw_rhs.at[:, pl.ds(1, 1)], sems.at[4]),
    ]
    for copy in copies:
        copy.wait()
    for s in range(cells_s):
        for k, q in enumerate(near):
            unpack_cell(raw.at[s, k], sol, s * cells_q + q, shape, layers)
        for k, q in enumerate(sides):
            unpack_cell(raw_rhs.at[s, k], begin, s * cells_q + q, shape, layers)
    write_base(layers, begin, stiff, sol, base, shape, sides)
    write_column_messages(sol, base, first, second, shape)


def open_kernel(
    shape, layers, start, rhs, stiffness, offsets, sol, base, sent, raw, raw_rhs, stiff, own, begin, sems
):
    cells_s, cells_q = shape[:2]
    sources, targets = (stiffness, offsets, start, rhs), (stiff, own, raw, raw_rhs)
    copies = [begun(a, b, sems.at[k]) for k, (a, b) in enumerate(zip(sources, targets))]
    for copy in copies:
        copy.wait()
    group = lax.broadcasted_iota(jnp.int32, sent.shape, 0)
    sent[...] = jnp.where(group == lax.axis_index("sub"), own[...], 0)
    for s in range(cells_s):
        for q in range(cells_q):
            unpack_cell(raw.at[s, q], sol, s * cells_q + q, shape, layers)
            unpack_cell(raw_rhs.at[s, q], begin, s * cells_q + q, shape, layers)
    write_base(layers, begin, stiff, sol, base, shape)


def column_sides(first, second):
    even = lax.axis_index(GROUP_AXES) % 2 == 0

    def low(kind, s):
        return jnp.where(even, second[kind, s].astype(f32), first[kind, s].astype(f32))

    def high(kind, s):
        return jnp.where(even, first[kind, s].astype(f32), second[kind, s].astype(f32))

    return low, high


def edge_cells(low, high, sol, s, cells_q):
    col, cols = lax.axis_index(GROUP_AXES), lax.axis_size(GROUP_AXES)
    left = jnp.where(col > 0, low(0, s) + sol[s * cells_q], 0.0)
    right = jnp.where(col < cols - 1, high(0, s) + sol[s * cells_q + cells_q - 1], 0.0)
    return left, right


def row_kernel(shape, sol, base, first_in, second_in, first, second):
    cells_s, cells_q = shape[:2]
    low, high = column_sides(first_in, second_in)
    even = lax.axis_index("sub") % 2 == 0
    for out, s in (
        (first, jnp.where(even, cells_s - 1, 0)),
        (second, jnp.where(even, 0, cells_s - 1)),
    ):
        left, right = edge_cells(low, high, sol, s, cells_q)
        out[0, 0] = left.astype(bf16)
        out[0, cells_q + 1] = right.astype(bf16)
        low_s, high_s = low(1, s), high(1, s)
        out[1, 0] = low_s.astype(bf16)
        out[1, cells_q + 1] = high_s.astype(bf16)
        for q in range(cells_q):
            value = base[s * cells_q + q]
            if q == 0:
                value = value + low_s
            if q == cells_q - 1:
                value = value + high_s
            out[0, q + 1] = value.astype(bf16)
            out[1, q + 1] = sol[s * cells_q + q].astype(bf16)


def side_of(member):
    return (member // PARTNER) % 2


def middle_window_kernel(
    shape, sol, base, first_q, second_q, basis_t, local_kept, product, local, sems
):
    cells_s, cells_q, _, pad, columns = shape
    wide = cells_q + 2
    low, high = column_sides(first_q, second_q)
    copies = []
    for s in range(1, cells_s - 1):
        left, right = edge_cells(low, high, sol, s, cells_q)
        values = [left] + [base[s * cells_q + q] for q in range(cells_q)] + [right]
        values[1] = values[1] + low(1, s)
        values[cells_q] = values[cells_q] + high(1, s)
        for w in range(wide):
            local[(s - 1) * wide + w] = values[w].astype(bf16)
        part, there = pl.ds((s - 1) * wide, wide), pl.ds((s + 1) * wide, wide)
        copies.append(begun(local.at[part], local_kept.at[there], sems.at[len(copies)]))
    chunk = wide * pad
    product[...] = jnp.dot(
        basis_t[:, 2 * chunk : cells_s * chunk],
        local[...].reshape(-1, columns),
        preferred_element_type=f32,
    )
    for copy in copies:
        copy.wait()


def outer_window_kernel(
    shape,
    sol,
    base,
    first_q,
    second_q,
    first_s,
    second_s,
    basis_t,
    middle,
    begun_kept,
    message,
    local_kept,
    local,
    restricted,
    sems,
):
    cells_s, cells_q, _, pad, columns = shape
    wide = cells_q + 2
    low, high = column_sides(first_q, second_q)
    row, rows = lax.axis_index("sub"), lax.axis_size("sub")
    even = row % 2 == 0

    def above(kind, w):
        return jnp.where(even, second_s[kind, w].astype(f32), first_s[kind, w].astype(f32))

    def below(kind, w):
        return jnp.where(even, first_s[kind, w].astype(f32), second_s[kind, w].astype(f32))

    copies = []
    for s in (0, cells_s - 1):
        left, right = edge_cells(low, high, sol, s, cells_q)
        values = [left] + [base[s * cells_q + q] for q in range(cells_q)] + [right]
        values[1] = values[1] + low(1, s)
        values[cells_q] = values[cells_q] + high(1, s)
        for w in range(wide):
            value = values[w]
            if s == 0:
                value = value + above(1, w)
            if s == cells_s - 1:
                value = value + below(1, w)
            local[(s + 1) * wide + w] = value.astype(bf16)
        part = pl.ds((s + 1) * wide, wide)
        copies.append(begun(local.at[part], local_kept.at[part], sems.at[len(copies)]))
    for s, side, place, there in (
        (0, above, 0, row > 0),
        (cells_s - 1, below, (cells_s + 1) * wide, row < rows - 1),
    ):
        near = [low(1, s)] + [sol[s * cells_q + q] for q in range(cells_q)] + [high(1, s)]
        for w in range(wide):
            local[place + w] = jnp.where(there, side(0, w) + near[w], 0.0).astype(bf16)
        part = pl.ds(place, wide)
        copies.append(begun(local.at[part], local_kept.at[part], sems.at[len(copies)]))
    chunk = wide * pad
    product = middle[...]
    for r in (0, cells_s):
        product = product + jnp.dot(
            basis_t[:, r * chunk : (r + 2) * chunk],
            local[r * wide : (r + 2) * wide].reshape(-1, columns),
            preferred_element_type=f32,
        )
    product = product.astype(bf16)
    half = columns // 2
    for k in range(2):
        restricted[k] = product[:, k * half : (k + 1) * half]
    for j in range(message.shape[0]):
        copies.append(begun(restricted.at[side_of(j)], message.at[j], sems.at[len(copies)]))
    for copy in copies:
        copy.wait()


def terms_kernel(spread, gathered, out, kept, sem):
    kept[...] = jnp.dot(spread[...], gathered[...], preferred_element_type=f32).astype(bf16)
    begun(kept, out, sem).wait()


def fine_kernel(shape, layers, steps, last, local_kept, inverse_kept, sol_kept, *refs):
    cells_s, cells_q, comps, pad, columns = shape
    if last:
        out, local, inverse, packed, sol, fine, sems = refs
        fields = ((sol_kept, sol),)
    else:
        base_kept, stiffness, out, base_out, local, inverse, packed, sol, fine, base, sems = refs
        fields = ((sol_kept, sol), (base_kept, base))
    per_cell = comps * layers
    wide = cells_q + 2
    span, chunk = wide * per_cell, wide * pad
    size = cells_s // steps
    loaded = begun(local_kept, local, sems.at[0])
    arriving = [
        begun(
            inverse_kept.at[0, pl.ds((k * size + 1) * span, size * span)],
            inverse.at[pl.ds(k * size * span, size * span)],
            sems.at[k + 1],
        )
        for k in range(steps)
    ]
    others = [begun(a, b, sems.at[steps + 1 + k]) for k, (a, b) in enumerate(fields)]
    pack = packing(wide, per_cell, pad)
    loaded.wait()
    for s in range(packed.shape[0] // span):
        part = local[s * wide : (s + 1) * wide].reshape(chunk, columns)
        packed[s * span : (s + 1) * span, :] = jnp.dot(
            pack, part, preferred_element_type=f32
        ).astype(bf16)
    for k in range(steps):
        arriving[k].wait()
        rows = jnp.dot(
            inverse[k * size * span : (k + 1) * size * span, :],
            packed[...],
            preferred_element_type=f32,
        )
        for s in range(size):
            for q in range(cells_q):
                i = (k * size + s) * cells_q + q
                first = s * span + (q + 1) * per_cell
                fine[i, :per_cell, :] = rows[first : first + per_cell]
                fine[i, per_cell:, :] = jnp.zeros((pad - per_cell, columns), f32)
    for copy in others:
        copy.wait()
    for i in range(fine.shape[0]):
        sol[i] = sol[i] + fine[i]
    copies = [begun(sol, out, sems.at[steps + 3])]
    if not last:
        write_base(layers, base, stiffness, fine, base, shape)
        copies.append(begun(base, base_out, sems.at[steps + 4]))
    for copy in copies:
        copy.wait()


def fine_product(shape, layers, local, sub_inverse, sol, base, stiffness, last):
    cells_s, cells_q, comps, pad, columns = shape
    width = sub_inverse.shape[2]
    rows = cells_s * (cells_q + 2) * comps * layers
    steps = 3 if cells_s % 3 == 0 else 1
    kept = pltpu.HBM((cells_s * cells_q, pad, columns), f32)
    field = pltpu.VMEM(kept.shape, f32)
    return call(
        functools.partial(fine_kernel, shape, layers, steps, last),
        (local, sub_inverse, sol) if last else (local, sub_inverse, sol, base, stiffness),
        (kept,) if last else (kept, kept),
        scratch=(
            pltpu.VMEM(local.shape, bf16),
            pltpu.VMEM((rows, width), bf16),
            pltpu.VMEM((width, columns), bf16),
        )
        + ((field, field) if last else (field, field, field))
        + (pltpu.SemaphoreType.DMA((steps + 5,)),),
        flops=2 * rows * width * columns,
        held=(0, 1, 2) if last else (0, 1, 2, 3),
    )


def coarse_values(arrived, depth):
    sums = []
    for c in range(arrived.shape[1]):
        total = arrived[0, c].astype(f32)
        for h in range(1, arrived.shape[0]):
            total = total + arrived[h, c].astype(f32)
        sums.append(total)
    rows = []
    for m in range(arrived.shape[1]):
        part = slice(side_of(m) * depth, (side_of(m) + 1) * depth)
        low = m - side_of(m) * PARTNER
        rows.append(jnp.concatenate([sums[low][part], sums[low + PARTNER][part]], axis=1))
    return jnp.concatenate(rows, axis=0).astype(bf16)


def step_sides_kernel(
    shape,
    layers,
    arrived,
    basis_kept,
    sol_kept,
    base_kept,
    stiffness,
    first,
    second,
    coarse,
    basis_p,
    stiff,
    sol,
    begin,
    base,
    sems,
):
    cells_s, cells_q, _, pad, columns = shape
    sides = (0, cells_q - 1)
    copies = [begun(basis_kept, basis_p, sems.at[0]), begun(stiffness, stiff, sems.at[1])]
    for q in sides:
        copies.append(begun(sol_kept.at[:, q], sol.at[:, q], sems.at[len(copies)]))
        copies.append(begun(base_kept.at[:, q], begin.at[:, q], sems.at[len(copies)]))
    sol, begin = (x.reshape(cells_s * cells_q, pad, columns) for x in (sol, begin))
    chosen = coarse_values(arrived, arrived.shape[2] // 2)
    copies[0].wait()
    span = cells_q * pad
    for s in range(cells_s):
        rows = jnp.dot(
            basis_p[s * span : (s + 1) * span, :], chosen, preferred_element_type=f32
        )
        coarse[s * cells_q : (s + 1) * cells_q] = rows.reshape(cells_q, pad, columns)
    for copy in copies[1:]:
        copy.wait()
    for s in range(cells_s):
        for q in sides:
            i = s * cells_q + q
            sol[i] = sol[i] + coarse[i]
    write_base(layers, begin, stiff, coarse, base, shape, sides)
    write_column_messages(sol, base, first, second, shape)


def step_kernel(shape, layers, coarse, sol_kept, base_kept, stiffness, new, base, stiff, begin, sems):
    sources, targets = (stiffness, sol_kept, base_kept), (stiff, new, begin)
    copies = [begun(a, b, sems.at[k]) for k, (a, b) in enumerate(zip(sources, targets))]
    for copy in copies:
        copy.wait()
    for i in range(new.shape[0]):
        new[i] = new[i] + coarse[i]
    write_base(layers, begin, stiff, coarse, base, shape)


def close_kernel(
    shape, layers, arrived, basis_kept, sol_kept, out_kept, basis_p, sol, out, sems
):
    cells_s, cells_q, comps, pad, columns = shape
    span = cells_q * pad
    copies = [begun(basis_kept, basis_p, sems.at[0])]
    for s in range(cells_s):
        part = pl.ds(s * cells_q, cells_q)
        copies.append(begun(sol_kept.at[part], sol.at[part], sems.at[s + 1]))
    chosen = coarse_values(arrived, arrived.shape[2] // 2)
    copies[0].wait()
    results = []
    for s in range(cells_s):
        rows = jnp.dot(
            basis_p[s * span : (s + 1) * span, :], chosen, preferred_element_type=f32
        )
        copies[s + 1].wait()
        for q in range(cells_q):
            total = sol[s * cells_q + q] + rows[q * pad : (q + 1) * pad]
            for c in range(comps):
                out[s, q, :, c, :] = total[c * layers : (c + 1) * layers]
        results.append(begun(out.at[s], out_kept.at[s], sems.at[cells_s + 1 + s]))
    for copy in results:
        copy.wait()


def places(offsets, g, j, groups, depth, kgroup):
    first = offsets[g, j]
    end = kgroup if j == groups - 1 else offsets[g, j + 1]
    shape = (1, groups * depth)
    at = lax.broadcasted_iota(jnp.int32, shape, 1)
    turn = at
    member = jnp.zeros(shape, jnp.int32)
    for m in range(1, groups):
        member = member + jnp.where(at >= m * depth, 1, 0)
        turn = turn - jnp.where(at >= m * depth, depth, 0)
    shifted = member - lax.rem(first, groups)
    shifted = jnp.where(shifted < 0, shifted + groups, shifted)
    place = shifted + turn * groups
    return first, place, place < end - first


def ordering(dims, offsets):
    groups, depth, kgroup, count = dims
    member = lax.axis_index(GROUP_AXES)
    wanted = jnp.full((1, groups * depth), -1, jnp.int32)
    for j in range(groups):
        _, place, valid = places(offsets, 0, j, groups, depth, kgroup)
        wanted = jnp.where(valid & (member == j), place, wanted)
    row = lax.broadcasted_iota(jnp.int32, (count, groups * depth), 0)
    return jnp.where(row == wanted, 1.0, 0.0).astype(bf16)


def basis_kernel(cell, dims, offsets, basis_kept, basis_t, turned_kept, own_kept, basis, own, sems):
    wide, per_cell, pad = cell
    span, chunk = wide * per_cell, wide * pad
    size = chunk - 2 * pad
    copy = begun(basis_kept.at[0], basis, sems.at[0])
    pack = packing(wide, per_cell, pad)
    pack_own = packing(wide, per_cell, pad, True)[pad : pad + size]
    order = ordering(dims, offsets)
    rows = basis.shape[0] // span
    copy.wait()
    for s in range(rows):
        ordered = jnp.dot(
            basis[s * span : (s + 1) * span, :], order, preferred_element_type=f32
        ).astype(bf16)
        basis_t[:, s * chunk : (s + 1) * chunk] = lax.dot_general(
            ordered, pack, (((0,), (0,)), ((), ())), preferred_element_type=f32
        ).astype(bf16)
        if 0 < s < rows - 1:
            own[(s - 1) * size : s * size, :] = jnp.dot(
                pack_own, ordered, preferred_element_type=f32
            ).astype(bf16)
    copies = [begun(basis_t, turned_kept, sems.at[1]), begun(own, own_kept, sems.at[2])]
    for copy in copies:
        copy.wait()


def ordered_basis(cell, dims, offsets, basis, turned, own):
    return pl.pallas_call(
        functools.partial(basis_kernel, cell, dims),
        out_shape=(jax.ShapeDtypeStruct(turned, bf16), pltpu.HBM(turned, bf16), pltpu.HBM(own, bf16)),
        in_specs=[pl.BlockSpec(memory_space=pltpu.SMEM), HBM],
        out_specs=(VMEM, HBM, HBM),
        scratch_shapes=[
            pltpu.VMEM(basis.shape[1:], bf16),
            pltpu.VMEM(own, bf16),
            pltpu.SemaphoreType.DMA((3,)),
        ],
        compiler_params=pltpu.CompilerParams(vmem_limit_bytes=12 << 20),
        cost_estimate=pl.CostEstimate(
            flops=6 * turned[0] * turned[1] * cell[0] * cell[2],
            bytes_accessed=6 * basis.size,
            transcendentals=0,
        ),
    )(offsets, pltpu.with_memory_space_constraint(basis, pltpu.HBM))


def first_index(first, member, groups):
    if groups & (groups - 1) == 0:
        return lax.shift_right_logical(first - member + groups - 1, groups.bit_length() - 1)
    return lax.div(first - member + groups - 1, groups)


def spread_kernel(dims, every, inverse_kept, partner_kept, out_kept, inverse, columns, picked, out, sems):
    groups, depth, kgroup = dims
    coarse = groups * depth
    member = lax.axis_index(GROUP_AXES)
    own = lax.axis_index("sub")
    side = side_of(member)
    copies = [
        begun(inverse_kept, inverse.at[side], sems.at[0]),
        begun(partner_kept, inverse.at[1 - side], sems.at[1]),
    ]
    slot = lax.broadcasted_iota(jnp.int32, (kgroup, coarse), 0)
    for j in range(groups):
        first, place, valid = places(every, own, j, groups, depth, kgroup)
        wanted = jnp.where(valid, place + first, -1)
        columns[:, j * coarse : (j + 1) * coarse] = jnp.where(slot == wanted, 1.0, 0.0).astype(bf16)
    _, n_sub, rows, _ = inverse.shape
    turn = lax.broadcasted_iota(jnp.int32, (depth, rows), 0)
    index = lax.broadcasted_iota(jnp.int32, (depth, rows), 1)
    for copy in copies:
        copy.wait()
    span = 2 * coarse
    steps = max(n_sub // 4, 1)
    size = n_sub // steps

    def some(k, _):
        for t in range(size):
            g = k * size + t
            for b in range(2):
                m = member + (b - side) * PARTNER
                picks = []
                for j in range(groups):
                    first = every[g, j]
                    end = kgroup if j == groups - 1 else every[g, j + 1]
                    begin = first_index(first, m, groups)
                    wanted = (index == turn + begin) & (index * groups + m < end)
                    picks.append(jnp.where(wanted, 1.0, 0.0).astype(bf16))
                part = jnp.dot(
                    jnp.concatenate(picks, axis=0), inverse[b, g], preferred_element_type=f32
                ).astype(bf16)
                for j in range(groups):
                    at = t * span + (2 * j + b) * depth
                    picked[at : at + depth, :] = part[j * depth : (j + 1) * depth]
        results = []
        for t in range(size):
            part = pl.ds(t * span, span)
            out[part, :] = jnp.dot(
                picked[part, :], columns[...], preferred_element_type=f32
            ).astype(bf16)
            there = pl.ds((k * size + t) * span, span)
            results.append(begun(out.at[part], out_kept.at[there], sems.at[2 + t]))
        for copy in results:
            copy.wait()
        return 0

    lax.fori_loop(0, steps, some, 0)


def spread_inverse(every, coarse_inverse, partner, depth):
    n_sub, share_rows, kgroup = coarse_inverse.shape
    groups = every.shape[1]
    coarse = groups * depth
    rows = n_sub * 2 * coarse
    part = rows // max(n_sub // 4, 1)
    return pl.pallas_call(
        functools.partial(spread_kernel, (groups, depth, kgroup)),
        out_shape=pltpu.HBM((rows, groups * coarse), bf16),
        in_specs=[pl.BlockSpec(memory_space=pltpu.SMEM), HBM, HBM],
        out_specs=HBM,
        scratch_shapes=[
            pltpu.VMEM((2,) + coarse_inverse.shape, bf16),
            pltpu.VMEM((kgroup, groups * coarse), bf16),
            pltpu.VMEM((part, kgroup), bf16),
            pltpu.VMEM((part, groups * coarse), bf16),
            pltpu.SemaphoreType.DMA((2 + part // (2 * coarse),)),
        ],
        compiler_params=pltpu.CompilerParams(
            vmem_limit_bytes=(16 << 20) + 4 * coarse_inverse.size + 8 * part * groups * coarse
        ),
        cost_estimate=pl.CostEstimate(
            flops=2 * rows * groups * coarse * kgroup,
            bytes_accessed=2 * rows * groups * coarse,
            transcendentals=0,
        ),
    )(
        every,
        pltpu.with_memory_space_constraint(coarse_inverse, pltpu.HBM),
        pltpu.with_memory_space_constraint(partner, pltpu.HBM),
    )


def shards(rhs, start, stiffness, sub_inverse, basis, coarse_inverse, offsets):
    cells_s, cells_q, comps, layers, columns = rhs.shape
    n_sub, _, kgroup = coarse_inverse.shape
    groups = offsets.shape[1]
    depth = -(-basis.shape[2] // groups)
    coarse = groups * depth
    cells = cells_s * cells_q
    per_cell = comps * layers
    pad = -(-per_cell // 16) * 16
    wide = cells_q + 2
    shape = (cells_s, cells_q, comps, pad, columns)

    field = jax.ShapeDtypeStruct((cells, pad, columns), f32)
    column_message = jax.ShapeDtypeStruct((2, cells_s, pad, columns), bf16)
    row_message = jax.ShapeDtypeStruct((2, wide, pad, columns), bf16)

    rows = (cells_s + 2) * wide * pad

    start_cells, rhs_cells = (x.transpose(0, 1, 3, 2, 4) for x in (start, rhs))
    tail = (layers, comps, columns)
    first, second = call(
        functools.partial(open_sides_kernel, shape, layers),
        (start_cells, rhs_cells, stiffness),
        (column_message, column_message),
        scratch=(
            pltpu.VMEM((cells_s, 4) + tail, f32),
            pltpu.VMEM((cells_s, 2) + tail, f32),
            pltpu.VMEM(stiffness.shape, f32),
            pltpu.VMEM(field.shape, f32),
            pltpu.VMEM(field.shape, f32),
            pltpu.VMEM(field.shape, f32),
            pltpu.SemaphoreType.DMA((5,)),
        ),
        held=(0, 1, 2),
    )
    solution, base, sent = call(
        functools.partial(open_kernel, shape, layers),
        (start_cells, rhs_cells, stiffness, offsets),
        (field, field, jax.ShapeDtypeStruct((n_sub, groups), jnp.int32)),
        scratch=(
            pltpu.VMEM((cells_s, cells_q) + tail, f32),
            pltpu.VMEM((cells_s, cells_q) + tail, f32),
            pltpu.VMEM(stiffness.shape, f32),
            pltpu.VMEM(offsets.shape, jnp.int32),
            pltpu.VMEM(field.shape, f32),
            pltpu.SemaphoreType.DMA((4,)),
        ),
        held=(0, 1, 2, 3),
    )
    cell = (wide, per_cell, pad)
    dims = (groups, depth, kgroup, basis.shape[2])
    basis_t = basis_kept = basis_p = every = spread = None

    for sweep in range(ITERS):
        last = sweep == ITERS - 1
        first_q, second_q = swap(first, second, GROUP_AXES)
        if sweep == 0:
            every = sent
            rounds = (n_sub - 1).bit_length()
            for power in range(rounds - 1):
                every = doubled(every, 1 << power)
            first_q, second_q, every = lax.optimization_barrier((first_q, second_q, every))
        first, second = call(
            functools.partial(row_kernel, shape),
            (solution, base, first_q, second_q),
            (row_message, row_message),
        )
        first_s, second_s = swap(first, second, "sub")
        if sweep == 0:
            later, _ = lax.optimization_barrier((basis, first))
            basis_t, basis_kept, basis_p = ordered_basis(
                cell, dims, offsets, later, (coarse, rows), (cells * pad, coarse)
            )
            shared, _ = lax.optimization_barrier((coarse_inverse, first))
            pairs = [(i, i ^ PARTNER) for i in range(groups)]
            partner = lax.ppermute(shared, GROUP_AXES, pairs)
            every = doubled(every, 1 << (rounds - 1))
            first_s, second_s, every = lax.optimization_barrier((first_s, second_s, every))
        turned = basis_t if sweep == 0 else basis_kept
        begun_kept, middle = call(
            functools.partial(middle_window_kernel, shape),
            (solution, base, first_q, second_q, turned),
            (
                pltpu.HBM(((cells_s + 2) * wide, pad, columns), bf16),
                jax.ShapeDtypeStruct((coarse, columns), f32),
            ),
            scratch=(
                pltpu.VMEM(((cells_s - 2) * wide, pad, columns), bf16),
                pltpu.SemaphoreType.DMA((cells_s - 2,)),
            ),
            flops=rows * coarse * columns,
        )
        message, local = call(
            functools.partial(outer_window_kernel, shape),
            (solution, base, first_q, second_q, first_s, second_s, turned, middle, begun_kept),
            (
                pltpu.HBM((groups, coarse, columns // 2), bf16),
                pltpu.HBM(((cells_s + 2) * wide, pad, columns), bf16),
            ),
            scratch=(
                pltpu.VMEM(((cells_s + 2) * wide, pad, columns), bf16),
                pltpu.VMEM((2, coarse, columns // 2), bf16),
                pltpu.SemaphoreType.DMA((groups + cells_s + 2,)),
            ),
            flops=rows * coarse * columns,
            held=(8,),
            aliases={8: 1},
        )
        if sweep == 0:
            waited, _ = lax.optimization_barrier((every, message))
            spread = spread_inverse(waited, coarse_inverse, partner, depth)
        gathered = lax.all_to_all(message, GROUP_AXES, 0, 0, tiled=True)
        held = pltpu.VMEM((spread.shape[0], columns // 2), bf16)
        (terms,) = call(
            terms_kernel,
            (spread, gathered.reshape(-1, columns // 2)),
            (pltpu.HBM(held.shape, bf16),),
            scratch=(held, pltpu.SemaphoreType.DMA),
            flops=2 * spread.size * columns // 2,
        )
        arrived = lax.all_to_all(
            terms.reshape(n_sub * groups, 2 * depth, columns // 2), ALL_AXES, 0, 0, tiled=True
        ).reshape(n_sub, groups, 2 * depth, columns // 2)
        kept = fine_product(
            shape, layers, local, sub_inverse, solution, base, stiffness, last
        )
        if last:
            (out,) = call(
                functools.partial(close_kernel, shape, layers),
                (arrived, basis_p, *kept),
                (pltpu.HBM((cells_s, cells_q) + tail, f32),),
                scratch=(
                    pltpu.VMEM(basis_p.shape, bf16),
                    pltpu.VMEM(field.shape, f32),
                    pltpu.VMEM((cells_s, cells_q) + tail, f32),
                    pltpu.SemaphoreType.DMA((2 * cells_s + 1,)),
                ),
                held=(1, 2),
            )
        else:
            first, second, change = call(
                functools.partial(step_sides_kernel, shape, layers),
                (
                    arrived,
                    basis_p,
                    *(x.reshape(cells_s, cells_q, pad, columns) for x in kept),
                    stiffness,
                ),
                (column_message, column_message, field),
                scratch=(
                    pltpu.VMEM(basis_p.shape, bf16),
                    pltpu.VMEM(stiffness.shape, f32),
                    pltpu.VMEM((cells_s, cells_q, pad, columns), f32),
                    pltpu.VMEM((cells_s, cells_q, pad, columns), f32),
                    pltpu.VMEM(field.shape, f32),
                    pltpu.SemaphoreType.DMA((6,)),
                ),
                held=(1, 2, 3, 4),
            )
            solution, base = call(
                functools.partial(step_kernel, shape, layers),
                (change, *kept, stiffness),
                (field, field),
                scratch=(
                    pltpu.VMEM(stiffness.shape, f32),
                    pltpu.VMEM(field.shape, f32),
                    pltpu.SemaphoreType.DMA((3,)),
                ),
                held=(1, 2, 3),
            )
    return out.transpose(0, 1, 3, 2, 4)


def solution(mesh):
    return jax.shard_map(
        shards,
        mesh=mesh,
        in_specs=(
            P("sub", ("crow", "ccol"), None, None, None),
            P("sub", ("crow", "ccol"), None, None, None),
            P("sub", ("crow", "ccol"), None, None),
            P(("sub", "crow", "ccol"), None, None),
            P(("sub", "crow", "ccol"), None, None),
            P(None, ("crow", "ccol"), "sub"),
            P("sub", None),
        ),
        out_specs=P("sub", ("crow", "ccol"), None, None, None),
        check_vma=False,
    )
```
